32 devices in a mesh: dp: 8 (over y, x, core), mp: 4 (over z).
Axes of the slice: x: 2, y: 2, z: 4, core: 2. Of those that a mesh axis runs over, the one named last changes fastest.
Arguments:
- tokens: bfloat16 [8, 2048, 2048], P('dp', 'mp'), may hold values from -6 to 6
- seq_lengths: int32 [8, 16], P('dp'), may hold values from 1 to 1537, 2048 in all within a row
- attn_gain: float32 [2048], replicated, may hold values from 0.5 to 1.5
- attn_shift: float32 [2048], replicated, may hold values from -3 to 3
- mlp_gain: float32 [2048], replicated, may hold values from 0.5 to 1.5
- mlp_shift: float32 [2048], replicated, may hold values from -3 to 3
- in_weight: bfloat16 [2048, 8, 768], P(None, 'mp'), may hold values from -0.125 to 0.125
- in_bias: float32 [8, 768], P('mp'), may hold values from -3 to 3
- out_weight: bfloat16 [2048, 2048], P('mp'), may hold values from -0.5 to 0.5
- out_bias: float32 [2048], replicated, may hold values from -3 to 3
- up_weight: bfloat16 [2048, 8192], P(None, 'mp'), may hold values from -0.125 to 0.125
- up_bias: float32 [8192], P('mp'), may hold values from -3 to 3
- down_weight: bfloat16 [8192, 2048], P('mp'), may hold values from -0.0625 to 0.0625
- down_bias: float32 [2048], replicated, may hold values from -3 to 3
- cotangent: bfloat16 [8, 2048, 2048], P('dp', 'mp'), may hold values from -6 to 6
Outputs:
- block_out: bfloat16 [8, 2048, 2048], P('dp', 'mp')
- tokens_grad: bfloat16 [8, 2048, 2048], P('dp', 'mp')
- grad_attn_gain: float32 [2048], replicated
- grad_attn_shift: float32 [2048], replicated
- grad_mlp_gain: float32 [2048], replicated
- grad_mlp_shift: float32 [2048], replicated
- grad_in_weight: float32 [2048, 8, 768], P(None, 'mp')
- grad_in_bias: float32 [8, 768], P('mp')
- grad_out_weight: float32 [2048, 2048], P('mp')
- grad_out_bias: float32 [2048], replicated
- grad_up_weight: float32 [2048, 8192], P(None, 'mp')
- grad_up_bias: float32 [8192], P('mp')
- grad_down_weight: float32 [8192, 2048], P('mp')
- grad_down_bias: float32 [2048], replicated
- branch_rms: float32 [2], replicated
The draws below stay inside these ranges and needn't reach their ends.
Inputs may be any that keep to these rules, and one draw needn't show every extreme that they name: `seq_lengths`: each row's 16 lengths sum to 2048, and one of them is 1537.
All inputs are finite; a program needn't handle non-finite values.
Results may differ from the reference program's by a relative error of at most 0.012.
Values may be sent and summed in bfloat16 or wider, within the bound.
A program may use at most 384 MiB of HBM per device.

```python
import math
import jax
import jax.numpy as jnp
import numpy as np
from jax import lax

D = 2048
HEADS = 8
HD = 256
ROT = 64
FF = 8192
LEN = 2048
QBLOCK = 512
NSEG = 16
ROWS = 8
TOKENS = 16384
LONGEST = 1537


def level_of(stream_key, dims, shards, least, top_value):
    gain, own = 1.0, jax.random.fold_in(stream_key, 6)
    for axis_at, shards_of in shards:
        draws = jnp.exp(jax.random.uniform(jax.random.fold_in(own, axis_at), (shards_of,), jnp.float32, least / len(shards), top_value / len(shards)))
        gain = gain * jnp.repeat(draws, dims[axis_at] // shards_of).reshape([-1 if axis == axis_at else 1 for axis in range(len(dims))])
    return gain


def length_profile(number_of, total, limit, skew):
    loads = [(1 << 20) // math.isqrt(grade ** skew) + 1 for grade in range(2, number_of + 1)]
    rest, given = total - limit - (number_of - 1), [1] * (number_of - 1)
    while rest > 0:
        free = [i for i in range(number_of - 1) if given[i] < limit]
        whole, remaining = sum([loads[i] for i in free]), rest
        for i in free:
            extra = min(limit - given[i], max(1, remaining * loads[i] // whole), rest)
            given[i] = given[i] + extra
            rest = rest - extra
    return np.array([limit] + given)


def ragged(own_key, amount, total, reach, slope):
    if amount == 2:
        one = jax.random.randint(own_key, (), max(1, total - reach), min(reach, total - 1) + 1)
        return jnp.stack([one, total - one])
    tallies = jnp.asarray(length_profile(amount, total, reach, slope), jnp.int32)
    twos = (amount - 1) // 2
    donor, sink = tallies[1:1 + 2 * twos:2], tallies[2:2 + 2 * twos:2]
    slack = jnp.minimum(donor - 1, reach - sink)
    passed = jax.random.randint(jax.random.fold_in(own_key, 1), (twos,), 0, 1 << 20) % (slack + 1)
    tallies = tallies.at[1:1 + 2 * twos:2].set(donor - passed).at[2:2 + 2 * twos:2].set(sink + passed)
    return tallies[jax.random.permutation(jax.random.fold_in(own_key, 2), amount)]


def normal_values(key, extent, deviation, reach, cuts=(), kind=jnp.bfloat16):
    entries = jax.random.normal(key, extent, jnp.float32) * deviation
    if len(cuts) > 0:
        entries = level_of(key, extent, cuts, -0.22, 0.18) * entries
    return jnp.clip(entries, min=-reach, max=reach).astype(kind)


def setup_inputs(seed: int = 0) -> dict:
    streams_of = jax.random.split(jax.random.key(seed), 16)
    return {
        "tokens": normal_values(streams_of[0], (ROWS, LEN, D), 1.0, 6.0, ((0, 8), (1, 4))),
        "seq_lengths": jax.vmap(lambda own: ragged(own, NSEG, LEN, LONGEST, 2))(jax.random.split(streams_of[1], ROWS)).reshape((ROWS, NSEG)).astype(jnp.int32),
        "attn_gain": jnp.clip(1.0 + 0.1 * jax.random.normal(streams_of[2], (D,), jnp.float32), 0.5, 1.5),
        "attn_shift": normal_values(streams_of[3], (D,), 0.3, 3.0, (), jnp.float32),
        "mlp_gain": jnp.clip(1.0 + 0.1 * jax.random.normal(streams_of[4], (D,), jnp.float32), 0.5, 1.5),
        "mlp_shift": normal_values(streams_of[5], (D,), 0.3, 3.0, (), jnp.float32),
        "in_weight": normal_values(streams_of[6], (D, HEADS, 3 * HD), D ** -0.5, 0.125, ((1, 4),)),
        "in_bias": normal_values(streams_of[7], (HEADS, 3 * HD), 0.3, 3.0, ((0, 4),), jnp.float32),
        "out_weight": normal_values(streams_of[8], (HEADS * HD, D), (HEADS * HD // 16) ** -0.5, 0.5, ((0, 4),)),
        "out_bias": normal_values(streams_of[9], (D,), 0.3, 3.0, (), jnp.float32),
        "up_weight": normal_values(streams_of[10], (D, FF), D ** -0.5, 0.125, ((1, 4),)),
        "up_bias": normal_values(streams_of[11], (FF,), 0.3, 3.0, ((0, 4),), jnp.float32),
        "down_weight": normal_values(streams_of[12], (FF, D), FF ** -0.5, 0.0625, ((0, 4),)),
        "down_bias": normal_values(streams_of[13], (D,), 0.3, 3.0, (), jnp.float32),
        "cotangent": normal_values(streams_of[14], (ROWS, LEN, D), 1.0, 6.0, ((0, 8), (1, 4))),
    }


NORM_EPS = 1e-05
NEG_FILL = -1000000000.0
PRECISE = lax.Precision.HIGHEST

@jax.custom_vjp
def low(v):
    return lax.optimization_barrier(v.astype(jnp.bfloat16)).astype(jnp.float32)

@jax.custom_vjp
def low_back(v):
    return v

def low_keep(v):
    return (low(v), None)

def low_pass(kept, grad):
    return (grad,)

def back_keep(v):
    return (v, None)

def back_low(kept, grad):
    return (low(grad),)
low.defvjp(low_keep, low_pass)
low_back.defvjp(back_keep, back_low)

def layer_norm(values, norm_gain, norm_shift):
    average = lax.optimization_barrier(jnp.mean(values, axis=-1, keepdims=True))
    centred = values - average
    variance = lax.optimization_barrier(jnp.mean(centred * centred, axis=-1, keepdims=True))
    return centred * lax.rsqrt(variance + NORM_EPS) * norm_gain + norm_shift

def segment_layout(row_lengths):
    seg_ends = jnp.cumsum(row_lengths).astype(jnp.int32)
    seg_starts = (seg_ends - row_lengths).astype(jnp.int32)
    places = jnp.arange(LEN, dtype=jnp.int32)
    segment = lax.optimization_barrier(jnp.sum((places[:, None] >= seg_ends[None, :]).astype(jnp.int32), axis=1)).astype(jnp.int32)
    matches = segment[:, None] == jnp.arange(NSEG, dtype=jnp.int32)[None, :]
    offset = lax.optimization_barrier(jnp.sum(jnp.where(matches, seg_starts[None, :], 0), axis=1)).astype(jnp.int32)
    return (segment, (places - offset).astype(jnp.int32))

def rotary_tables(positions):
    inverse = 10000.0 ** (-jnp.arange(0, ROT, 2).astype(jnp.float32) / ROT)
    angles = positions.astype(jnp.float32)[:, None] * inverse[None, :]
    angles = jnp.concatenate([angles, angles], axis=-1)[:, None, :]
    return (jnp.cos(angles), jnp.sin(angles))

def rotate(values, cosine_table, sine_table):
    turned = values[..., :ROT]
    first_half = turned[..., :ROT // 2]
    second_half = turned[..., ROT // 2:]
    swapped = jnp.concatenate([-second_half, first_half], axis=-1)
    return jnp.concatenate([turned * cosine_table + swapped * sine_table, values[..., ROT:]], axis=-1)

def attention(queries, all_keys, all_values, segment):
    scaling = HD ** (-0.5)
    block_count = LEN // QBLOCK
    head_count = queries.shape[1]
    places = jnp.arange(LEN, dtype=jnp.int32)
    query_blocks = queries.reshape(block_count, QBLOCK, head_count, HD)
    segment_blocks = segment.reshape(block_count, QBLOCK)
    place_blocks = places.reshape(block_count, QBLOCK)

    def one_block(inputs):
        query_block, block_segment, block_places = inputs
        scores = low_back(jnp.einsum('qhc,khc->hqk', query_block, all_keys, precision=PRECISE) * scaling)
        allowed = (segment[None, :] == block_segment[:, None]) & (places[None, :] <= block_places[:, None])
        scores = jnp.where(allowed[None], scores, NEG_FILL)
        row_max = lax.optimization_barrier(jnp.max(scores, axis=-1, keepdims=True))
        weights = jnp.exp(scores - row_max)
        shares = low(weights / lax.optimization_barrier(jnp.sum(weights, axis=-1, keepdims=True)))
        return jnp.einsum('hqk,khc->qhc', shares, all_values, precision=PRECISE)
    outputs = lax.map(jax.checkpoint(one_block), (query_blocks, segment_blocks, place_blocks))
    return outputs.reshape(LEN, head_count, HD)

def forward_row(params, row_tokens, segment, positions):
    attn_gain, attn_shift, mlp_gain, mlp_shift, in_weight, in_bias, out_weight, out_bias, up_weight, up_bias, down_weight, down_bias = params
    attn_in = low(layer_norm(row_tokens, attn_gain, attn_shift))
    mlp_in = low(layer_norm(row_tokens, mlp_gain, mlp_shift))
    projected = low_back(jnp.einsum('td,dhc->thc', attn_in, in_weight, precision=PRECISE) + in_bias)
    cosine_table, sine_table = rotary_tables(positions)
    queries = low(rotate(projected[..., :HD], cosine_table, sine_table))
    all_keys = low(rotate(projected[..., HD:2 * HD], cosine_table, sine_table))
    all_values = low(projected[..., 2 * HD:])
    heads_out = low(low_back(attention(queries, all_keys, all_values, segment)))
    attn_branch = jnp.dot(heads_out.reshape(LEN, HEADS * HD), out_weight, precision=PRECISE) + out_bias
    up_values = low_back(jnp.dot(mlp_in, up_weight, precision=PRECISE) + up_bias)
    activated = low(jax.nn.gelu(up_values, approximate=False))
    mlp_branch = jnp.dot(activated, down_weight, precision=PRECISE) + down_bias
    block_out = row_tokens + attn_branch + mlp_branch
    squares = jnp.stack([jnp.sum(attn_branch * attn_branch), jnp.sum(mlp_branch * mlp_branch)])
    return (block_out, squares)

def add_trees(left, right):
    return left + right

def reference(tokens, seq_lengths, attn_gain, attn_shift, mlp_gain, mlp_shift, in_weight, in_bias, out_weight, out_bias, up_weight, up_bias, down_weight, down_bias, cotangent):
    params = (attn_gain.astype(jnp.float32), attn_shift.astype(jnp.float32), mlp_gain.astype(jnp.float32), mlp_shift.astype(jnp.float32), in_weight.astype(jnp.float32), in_bias.astype(jnp.float32), out_weight.astype(jnp.float32), out_bias.astype(jnp.float32), up_weight.astype(jnp.float32), up_bias.astype(jnp.float32), down_weight.astype(jnp.float32), down_bias.astype(jnp.float32))

    def row_step(carried, inputs):
        grad_sums, square_sums = carried
        row_tokens, row_lengths, row_cotangent = inputs
        segment, positions = segment_layout(row_lengths)

        def wrapped(param_list, values):
            return forward_row(param_list, values, segment, positions)
        out_row, pullback, row_squares = jax.vjp(wrapped, params, row_tokens.astype(jnp.float32), has_aux=True)
        param_grads, token_grad = pullback(row_cotangent.astype(jnp.float32))
        grad_sums = jax.tree.map(add_trees, grad_sums, param_grads)
        return ((grad_sums, square_sums + row_squares), (out_row.astype(jnp.bfloat16), token_grad.astype(jnp.bfloat16)))
    zero_grads = jax.tree.map(jnp.zeros_like, params)
    start = (zero_grads, jnp.zeros((2,), jnp.float32))
    (grad_sums, square_sums), (block_out, tokens_grad) = lax.scan(row_step, start, (tokens, seq_lengths, cotangent))
    branch_rms = jnp.sqrt(square_sums / (TOKENS * D))
    return (block_out, tokens_grad, grad_sums[0], grad_sums[1], grad_sums[2], grad_sums[3], grad_sums[4], grad_sums[5], grad_sums[6], grad_sums[7], grad_sums[8], grad_sums[9], grad_sums[10], grad_sums[11], branch_rms)
```

```python
import functools

import jax
import jax.numpy as jnp
import numpy as np
from jax import lax
from jax.experimental import pallas as pl
from jax.experimental.pallas import tpu as pltpu
from jax.sharding import PartitionSpec as P

HD = 256
ROT = 64
KBLOCK = 256
NORM_EPS = 1e-05
NEG_FILL = -1000000000.0
VMEM_LIMIT = 56 * 1024 * 1024
BF16 = jnp.bfloat16
F32 = jnp.float32

NT = (((1,), (1,)), ((), ()))
NN = (((1,), (0,)), ((), ()))
TN = (((0,), (0,)), ((), ()))


def dot(a, b, dims=NN):
    return lax.dot_general(a, b, dims, preferred_element_type=F32)


def params():
    return pltpu.CompilerParams(vmem_limit_bytes=VMEM_LIMIT)


def turn(part, cosine, sine):
    lane = lax.broadcasted_iota(jnp.int32, part.shape, 1)
    swapped = jnp.where(
        lane < ROT // 2,
        pltpu.roll(part, 128 - ROT // 2, 1),
        pltpu.roll(part, ROT // 2, 1),
    )
    return part * cosine + swapped * sine


def qkv_kernel(x_ref, w_ref, b_ref, cos_ref, sin_ref, *refs):
    out_ref = refs[-1]
    kind = lax.rem(pl.program_id(0), 3)
    acc = dot(x_ref[...], w_ref[...]) + b_ref[...]

    @pl.when(kind < 2)
    def _():
        scale = jnp.where(kind == 0, HD**-0.5, 1.0)
        out_ref[:, :128] = (turn(acc[:, :128], cos_ref[...], sin_ref[...]) * scale).astype(BF16)
        out_ref[:, 128:] = (acc[:, 128:] * scale).astype(BF16)

    @pl.when(kind == 2)
    def _():
        out_ref[...] = acc.astype(BF16)


def qkv_slot(slot, rows, x, weight, bias, cosine, sine, buffer):
    t, d = x.shape
    width = weight.shape[1]
    in_specs = [
        pl.BlockSpec((t, d), lambda j: (0, 0)),
        pl.BlockSpec((d, HD), lambda j: (0, j)),
        pl.BlockSpec((1, HD), lambda j: (0, j)),
        pl.BlockSpec((t, 128), lambda j: (slot, 0)),
        pl.BlockSpec((t, 128), lambda j: (slot, 0)),
    ]
    args = [x, weight, bias, cosine, sine]
    aliases = {}
    if buffer is not None:
        in_specs.append(pl.BlockSpec(memory_space=pl.ANY))
        args.append(buffer)
        aliases = {5: 0}
    return pl.pallas_call(
        qkv_kernel,
        grid=(width // HD,),
        in_specs=in_specs,
        out_specs=pl.BlockSpec((t, HD), lambda j: (slot, j)),
        out_shape=jax.ShapeDtypeStruct((rows, width), BF16),
        input_output_aliases=aliases,
        compiler_params=params(),
        cost_estimate=pl.CostEstimate(
            flops=2 * t * d * width, bytes_accessed=2 * (t * d + d * width + t * width), transcendentals=0
        ),
        name="qkv",
    )(*args)


def up_kernel(x_ref, w_ref, b_ref, *refs):
    act_ref, slope_ref = refs[-2:]
    u = dot(x_ref[...], w_ref[...]) + b_ref[...]
    below = 0.5 + 0.5 * lax.erf(u * (0.5**0.5))
    act_ref[...] = (u * below).astype(BF16)
    density = jnp.exp(u * u * -0.5) * ((2.0 * np.pi) ** -0.5)
    slope_ref[...] = (below + u * density).astype(BF16)


def up_slot(slot, rows, x, weight, bias, buffers):
    t, d = x.shape
    width = weight.shape[1]
    tile = 512
    in_specs = [
        pl.BlockSpec((t, d), lambda j: (0, 0)),
        pl.BlockSpec((d, tile), lambda j: (0, j)),
        pl.BlockSpec((1, tile), lambda j: (0, j)),
    ]
    args = [x, weight, bias]
    aliases = {}
    if buffers is not None:
        in_specs += [pl.BlockSpec(memory_space=pl.ANY)] * 2
        args += list(buffers)
        aliases = {3: 0, 4: 1}
    return pl.pallas_call(
        up_kernel,
        grid=(width // tile,),
        in_specs=in_specs,
        out_specs=[pl.BlockSpec((t, tile), lambda j: (slot, j))] * 2,
        out_shape=[jax.ShapeDtypeStruct((rows, width), BF16)] * 2,
        input_output_aliases=aliases,
        compiler_params=params(),
        cost_estimate=pl.CostEstimate(
            flops=2 * t * d * width,
            bytes_accessed=2 * (t * d + d * width + 2 * t * width),
            transcendentals=2 * t * width,
        ),
        name="up",
    )(*args)


def key_row(slot_ref, j, t):
    per = t // KBLOCK
    return pl.multiple_of(slot_ref[j // per] * t + lax.rem(j, per) * KBLOCK, KBLOCK)


def allowed(j, i, t, start):
    key = j * KBLOCK + lax.broadcasted_iota(jnp.int32, (KBLOCK, t), 0)
    query = i * t + lax.broadcasted_iota(jnp.int32, (1, t), 1)
    return (key >= start) & (key <= query)


def attend_kernel(t, heads, slot_ref, low_ref, qkv_ref, start_ref, out_ref, log_ref, vt_ref, acc_ref):
    blocks = qkv_ref.shape[0] // t
    per = t // KBLOCK

    for h in range(heads):
        for c in range(blocks):
            rows = pl.ds(c * t, t)
            vt_ref[h, :, rows] = qkv_ref[rows, (3 * h + 2) * HD : (3 * h + 3) * HD].T

    def query_block(i, unused):
        row = pl.multiple_of(slot_ref[i] * t, t)
        where = pl.ds(pl.multiple_of(i * t, t), t)
        start = start_ref[:, where]
        acc_ref[...] = jnp.zeros_like(acc_ref)

        def key_block(j, carried):
            place = key_row(slot_ref, j, t)
            mask = allowed(j, i, t, start)
            new = []
            for h in range(heads):
                top, total = carried[h]
                query = qkv_ref[pl.ds(row, t), 3 * h * HD : (3 * h + 1) * HD]
                key = qkv_ref[pl.ds(place, KBLOCK), (3 * h + 1) * HD : (3 * h + 2) * HD]
                s = jnp.where(mask, dot(key, query, NT), NEG_FILL)
                higher = jnp.maximum(top, jnp.max(s, axis=0, keepdims=True))
                p = jnp.exp(s - higher)
                shrink = jnp.exp(top - higher)
                total = total * shrink + jnp.sum(p, axis=0, keepdims=True)
                vt = vt_ref[h, :, pl.ds(place, KBLOCK)]
                acc_ref[h] = acc_ref[h] * shrink + dot(vt, p.astype(BF16))
                new.append((higher, total))
            return tuple(new)

        first = (jnp.full((1, t), 2 * NEG_FILL, F32), jnp.zeros((1, t), F32))
        carried = lax.fori_loop(low_ref[i], (i + 1) * per, key_block, (first,) * heads)
        for h in range(heads):
            top, total = carried[h]
            log_ref[h : h + 1, where] = top + jnp.log(total)
            out_ref[pl.ds(row, t), h * HD : (h + 1) * HD] = (acc_ref[h] / total).T.astype(BF16)
        return unused

    lax.fori_loop(0, blocks, query_block, 0)


def attend(t, slot_of, low, qkv, start):
    rows, width = qkv.shape
    heads = width // (3 * HD)
    return pl.pallas_call(
        functools.partial(attend_kernel, t, heads),
        in_specs=[pl.BlockSpec(memory_space=pltpu.SMEM)] * 2 + [pl.BlockSpec(memory_space=pltpu.VMEM)] * 2,
        out_specs=[pl.BlockSpec(memory_space=pltpu.VMEM)] * 2,
        out_shape=[
            jax.ShapeDtypeStruct((rows, heads * HD), BF16),
            jax.ShapeDtypeStruct((heads, rows), F32),
        ],
        scratch_shapes=[pltpu.VMEM((heads, HD, rows), BF16), pltpu.VMEM((heads, HD, t), F32)],
        compiler_params=params(),
        cost_estimate=pl.CostEstimate(
            flops=2 * rows * rows * HD * heads,
            bytes_accessed=2 * rows * width,
            transcendentals=rows * rows * heads // 2,
        ),
        name="attend",
    )(slot_of, low, qkv, start)


def attend_back_kernel(
    t, heads, slot_ref, high_ref, qkv_ref, grad_ref, out_ref, log_ref, start_ref, cos_ref, sin_ref,
    proj_ref, query_grad, delta, key_grad, value_grad,
):
    rows = qkv_ref.shape[0]
    blocks = rows // t
    per = t // KBLOCK
    query_grad[...] = jnp.zeros_like(query_grad)

    def prepare(i, unused):
        row = pl.multiple_of(slot_ref[i] * t, t)
        for h in range(heads):
            cols = slice(h * HD, (h + 1) * HD)
            both = grad_ref[pl.ds(row, t), cols].astype(F32) * out_ref[pl.ds(row, t), cols].astype(F32)
            delta[h : h + 1, pl.ds(pl.multiple_of(i * t, t), t)] = jnp.sum(both.T, axis=0, keepdims=True)
        return unused

    lax.fori_loop(0, blocks, prepare, 0)

    def turned_back(grad, place, count):
        cosine, sine = cos_ref[pl.ds(place, count), :], sin_ref[pl.ds(place, count), :]
        return turn(grad[:, :128], cosine, -sine)

    def key_block(j, unused):
        place = key_row(slot_ref, j, t)
        key_grad[...] = jnp.zeros_like(key_grad)
        value_grad[...] = jnp.zeros_like(value_grad)

        def query_block(i, unused):
            row = pl.multiple_of(slot_ref[i] * t, t)
            where = pl.ds(pl.multiple_of(i * t, t), t)
            mask = allowed(j, i, t, start_ref[:, where])
            for h in range(heads):
                query = qkv_ref[pl.ds(row, t), 3 * h * HD : (3 * h + 1) * HD]
                key = qkv_ref[pl.ds(place, KBLOCK), (3 * h + 1) * HD : (3 * h + 2) * HD]
                value = qkv_ref[pl.ds(place, KBLOCK), (3 * h + 2) * HD : (3 * h + 3) * HD]
                grad = grad_ref[pl.ds(row, t), h * HD : (h + 1) * HD]
                s = dot(key, query, NT) - log_ref[h : h + 1, where]
                p = jnp.exp(jnp.where(mask, s, NEG_FILL))
                p_grad = dot(value, grad, NT)
                value_grad[h] += dot(p.astype(BF16), grad)
                s_grad = (p * (p_grad - delta[h : h + 1, where])).astype(BF16)
                key_grad[h] += dot(s_grad, query)
                query_grad[pl.ds(row, t), h * HD : (h + 1) * HD] += dot(s_grad, key, TN)
            return unused

        lax.fori_loop(j // per, high_ref[j], query_block, 0)
        for h in range(heads):
            base = 3 * h * HD
            grad = key_grad[h]
            proj_ref[pl.ds(place, KBLOCK), base + HD : base + HD + 128] = turned_back(grad, place, KBLOCK).astype(BF16)
            proj_ref[pl.ds(place, KBLOCK), base + HD + 128 : base + 2 * HD] = grad[:, 128:].astype(BF16)
            proj_ref[pl.ds(place, KBLOCK), base + 2 * HD : base + 3 * HD] = value_grad[h].astype(BF16)
        return unused

    lax.fori_loop(0, rows // KBLOCK, key_block, 0)

    def finish(c, unused):
        place = pl.multiple_of(c * t, t)
        for h in range(heads):
            base = 3 * h * HD
            grad = query_grad[pl.ds(place, t), h * HD : (h + 1) * HD] * HD**-0.5
            proj_ref[pl.ds(place, t), base : base + 128] = turned_back(grad, place, t).astype(BF16)
            proj_ref[pl.ds(place, t), base + 128 : base + HD] = grad[:, 128:].astype(BF16)
        return unused

    lax.fori_loop(0, blocks, finish, 0)


def attend_back(t, slot_of, high, qkv, heads_grad, heads_out, logs, start, cosine, sine):
    rows, width = qkv.shape
    heads = width // (3 * HD)
    return pl.pallas_call(
        functools.partial(attend_back_kernel, t, heads),
        in_specs=[pl.BlockSpec(memory_space=pltpu.SMEM)] * 2 + [pl.BlockSpec(memory_space=pltpu.VMEM)] * 7,
        out_specs=pl.BlockSpec(memory_space=pltpu.VMEM),
        out_shape=jax.ShapeDtypeStruct((rows, width), BF16),
        scratch_shapes=[
            pltpu.VMEM((rows, heads * HD), F32),
            pltpu.VMEM((heads, rows), F32),
            pltpu.VMEM((heads, KBLOCK, HD), F32),
            pltpu.VMEM((heads, KBLOCK, HD), F32),
        ],
        compiler_params=params(),
        cost_estimate=pl.CostEstimate(
            flops=5 * rows * rows * HD * heads,
            bytes_accessed=4 * rows * width,
            transcendentals=rows * rows * heads // 2,
        ),
        name="attend_back",
    )(slot_of, high, qkv, heads_grad, heads_out, logs, start, cosine, sine)


def arrival_order(n):
    return [sorted(range(n), key=lambda p, z=z: (abs(p - z), p)) for z in range(n)]


def gather_slots(own, z, n):
    right = left = own
    came = {}
    for k in range(1, n):
        right = lax.ppermute(right, "mp", [(i, i + 1) for i in range(k - 1, n - 1)])
        left = lax.ppermute(left, "mp", [(i, i - 1) for i in range(1, n - k + 1)])
        came[k], came[-k] = right, left
    order = arrival_order(n)
    slots = [own]
    for s in range(1, n):
        chosen = came[n - 1 - order[n - 1][s]]
        for at in range(n - 1):
            source = came[at - order[at][s]]
            if at == 0 or source is not chosen:
                chosen = jnp.where(z == at, source, chosen)
        slots.append(chosen)
    return slots


def scatter_sum(part, own, z, n):
    right = left = None
    for k in range(n - 1, 0, -1):
        for_right, for_left = part(z + k), part(z - k)
        if right is not None:
            for_right = (for_right.astype(F32) + right.astype(F32)).astype(BF16)
            for_left = (for_left.astype(F32) + left.astype(F32)).astype(BF16)
        right = lax.ppermute(for_right, "mp", [(i, i + 1) for i in range(n - k)])
        left = lax.ppermute(for_left, "mp", [(i, i - 1) for i in range(k, n)])
    return own + right.astype(F32) + left.astype(F32)


def exchange(part, own, z, n):
    came = [None] * (2 * n - 1)
    came[n - 1] = own
    for k in range(1, n):
        came[n - 1 - k] = lax.ppermute(part(z + k), "mp", [(i, i + k) for i in range(n - k)])
        came[n - 1 + k] = lax.ppermute(part(z - k), "mp", [(i, i - k) for i in range(k, n)])
    return lax.dynamic_slice_in_dim(jnp.stack(came), n - 1 - z, n, axis=0)


def sum_over_dp(part):
    return lax.psum(part, "dp")


def document_starts(row_lengths, length):
    count = row_lengths.shape[0]
    before = np.tri(count, k=-1, dtype=np.int32)
    starts = jnp.sum(before * row_lengths[None, :], axis=1)
    places = jnp.arange(length, dtype=jnp.int32)
    return jnp.max(jnp.where(starts[None, :] <= places[:, None], starts[None, :], 0), axis=1)


def per_device(
    tokens, seq_lengths, attn_gain, attn_shift, mlp_gain, mlp_shift, in_weight, in_bias, out_weight, out_bias,
    up_weight, up_bias, down_weight, down_bias, cotangent,
):
    n, groups = lax.axis_size("mp"), lax.axis_size("dp")
    z, group = lax.axis_index("mp"), lax.axis_index("dp")
    t, d = tokens.shape[1:]
    length = n * t
    local_heads = in_weight.shape[1]
    in_width, hidden = local_heads * 3 * HD, up_weight.shape[1]
    order = np.array(arrival_order(n), np.int32)
    slot_table = np.argsort(order, axis=1).astype(np.int32)
    slot_of = jnp.asarray(slot_table)[z]
    position_of = jnp.asarray(order)[z]

    own_tokens = tokens[0].astype(F32)
    centred = own_tokens - jnp.mean(own_tokens, axis=-1, keepdims=True)
    spread = lax.rsqrt(jnp.mean(centred * centred, axis=-1, keepdims=True) + NORM_EPS)
    normed = centred * spread
    own_grad = cotangent[0]
    x_slots = gather_slots(normed.astype(BF16), z, n)

    flat_in = in_weight.reshape(d, in_width)
    in_scaled = (flat_in.astype(F32) * attn_gain[:, None]).astype(BF16)
    up_scaled = (up_weight.astype(F32) * mlp_gain[:, None]).astype(BF16)
    in_offset = jnp.sum(flat_in.astype(F32) * attn_shift[:, None], axis=0) + in_bias.reshape(in_width)
    up_offset = jnp.sum(up_weight.astype(F32) * mlp_shift[:, None], axis=0) + up_bias
    share = out_weight.shape[0] // groups
    out_full = lax.all_gather(
        lax.dynamic_slice_in_dim(out_weight, group * share, share, axis=0), ("mp", "dp"), axis=0, tiled=True
    )

    starts = document_starts(seq_lengths[0], length)
    first_of_block = starts[:: t]
    low = first_of_block // KBLOCK
    last_key = (jnp.arange(length // KBLOCK, dtype=jnp.int32) + 1) * KBLOCK - 1
    high = jnp.sum((first_of_block[None, :] <= last_key[:, None]).astype(jnp.int32), axis=1)
    places = jnp.arange(length, dtype=jnp.int32).reshape(n, t)
    offsets = (places - starts.reshape(n, t))[position_of].reshape(length)
    inverse = 10000.0 ** (-jnp.arange(0, ROT, 2).astype(F32) / ROT)
    angles = offsets.astype(F32)[:, None] * inverse[None, :]
    cosine, sine = jnp.cos(angles), jnp.sin(angles)
    cosine = jnp.concatenate([cosine, cosine, jnp.ones((length, 128 - ROT), F32)], axis=1)
    sine = jnp.concatenate([-sine, sine, jnp.zeros((length, 128 - ROT), F32)], axis=1)
    start_row = starts[None, :]

    qkv = hidden_pair = None
    for s, x in enumerate(x_slots):
        qkv = qkv_slot(s, length, x, in_scaled, in_offset[None, :], cosine, sine, qkv)
        hidden_pair = up_slot(s, length, x, up_scaled, up_offset[None, :], hidden_pair)
    activated, slope = hidden_pair
    x_rows = jnp.concatenate(x_slots, axis=0)
    own_grad, unused = lax.optimization_barrier((own_grad, x_slots[-1]))
    g_slots = gather_slots(own_grad, z, n)
    heads_out, logs = attend(t, slot_of, low, qkv, start_row)

    def rows_for(array):
        def part(position):
            slot = slot_of[jnp.clip(position, 0, n - 1)]
            return lax.dynamic_slice_in_dim(array, slot * t, t, axis=0)

        return part

    heads_mine = exchange(rows_for(heads_out), heads_out[:t], z, n)
    heads_mine = heads_mine.transpose(1, 0, 2).reshape(t, n * local_heads * HD)
    attn_branch = dot(heads_mine, out_full) + out_bias
    down_part = dot(activated, down_weight).astype(BF16)
    mlp_branch = scatter_sum(rows_for(down_part), dot(activated[:t], down_weight), z, n) + down_bias
    block_out = (own_tokens + attn_branch + mlp_branch).astype(BF16)
    squares = jnp.stack([jnp.sum(attn_branch * attn_branch), jnp.sum(mlp_branch * mlp_branch)])

    g_rows = jnp.concatenate(g_slots, axis=0)
    heads_grad = dot(g_rows, out_weight, NT).astype(BF16)
    up_grad = (dot(g_rows, down_weight, NT) * slope.astype(F32)).astype(BF16)
    proj_grad = attend_back(t, slot_of, high, qkv, heads_grad, heads_out, logs, start_row, cosine, sine)
    norm_part = dot(up_grad, up_scaled, NT) + dot(proj_grad, in_scaled, NT)
    norm_grad = scatter_sum(rows_for(norm_part.astype(BF16)), norm_part[:t], z, n)
    mean_grad = jnp.mean(norm_grad, axis=-1, keepdims=True)
    mean_normed = jnp.mean(norm_grad * normed, axis=-1, keepdims=True)
    tokens_grad = (own_grad.astype(F32) + spread * (norm_grad - mean_grad - normed * mean_normed)).astype(BF16)

    down_grad = dot(activated, g_rows, TN).astype(BF16)
    out_grad = dot(heads_out, g_rows, TN).astype(BF16)
    up_cross = dot(x_rows, up_grad, TN).astype(BF16)
    in_cross = dot(x_rows, proj_grad, TN).astype(BF16)
    up_total = jnp.sum(up_grad.astype(F32), axis=0)
    in_total = jnp.sum(proj_grad.astype(F32), axis=0)
    wide_in, wide_up = flat_in.astype(F32), up_weight.astype(F32)
    small = (
        jnp.sum(in_cross.astype(F32) * wide_in, axis=1),
        jnp.sum(wide_in * in_total[None, :], axis=1),
        jnp.sum(up_cross.astype(F32) * wide_up, axis=1),
        jnp.sum(wide_up * up_total[None, :], axis=1),
        jnp.sum(own_grad.astype(F32), axis=0),
        squares,
    )
    grad_attn_gain, grad_attn_shift, grad_mlp_gain, grad_mlp_shift, bias_total, square_sums = lax.psum(
        small, ("dp", "mp")
    )
    in_total, up_total = lax.psum((in_total, up_total), "dp")
    down_grad, out_grad, up_cross, in_cross = (sum_over_dp(a) for a in (down_grad, out_grad, up_cross, in_cross))
    grad_in_weight = in_cross.astype(F32) * attn_gain[:, None] + attn_shift[:, None] * in_total[None, :]
    grad_up_weight = up_cross.astype(F32) * mlp_gain[:, None] + mlp_shift[:, None] * up_total[None, :]
    element_count = float(groups * n * t * d)
    return (
        block_out[None],
        tokens_grad[None],
        grad_attn_gain,
        grad_attn_shift,
        grad_mlp_gain,
        grad_mlp_shift,
        grad_in_weight.reshape(d, local_heads, 3 * HD),
        in_total.reshape(local_heads, 3 * HD),
        out_grad.astype(F32),
        bias_total,
        grad_up_weight,
        up_total,
        down_grad.astype(F32),
        bias_total,
        jnp.sqrt(square_sums / element_count),
    )


def solution(mesh):
    rows, weights = P("dp", "mp", None), P(None, "mp", None)
    in_specs = (
        rows, P("dp", None), P(), P(), P(), P(), weights, P("mp", None), P("mp", None), P(),
        P(None, "mp"), P("mp"), P("mp", None), P(), rows,
    )
    out_specs = (
        rows, rows, P(), P(), P(), P(), weights, P("mp", None), P("mp", None), P(),
        P(None, "mp"), P("mp"), P("mp", None), P(), P(),
    )
    return jax.shard_map(per_device, mesh=mesh, in_specs=in_specs, out_specs=out_specs, check_vma=False)
```

```python
import functools

import jax
import jax.numpy as jnp
import numpy as np
from jax import lax
from jax.experimental import pallas as pl
from jax.experimental.pallas import tpu as pltpu
from jax.sharding import PartitionSpec as P

HD = 256
ROT = 64
KBLOCK = 256
NORM_EPS = 1e-05
NEG_FILL = -1000000000.0
VMEM_LIMIT = 56 * 1024 * 1024
BF16 = jnp.bfloat16
F32 = jnp.float32

NT = (((1,), (1,)), ((), ()))
NN = (((1,), (0,)), ((), ()))
TN = (((0,), (0,)), ((), ()))


def dot(a, b, dims=NN):
    return lax.dot_general(a, b, dims, preferred_element_type=F32)


def arrival_order(n):
    return [sorted(range(n), key=lambda p, z=z: (abs(p - z), p)) for z in range(n)]


def params():
    return pltpu.CompilerParams(vmem_limit_bytes=VMEM_LIMIT)


def turn(part, cosine, sine):
    lane = lax.broadcasted_iota(jnp.int32, part.shape, 1)
    swapped = jnp.where(
        lane < ROT // 2,
        pltpu.roll(part, 128 - ROT // 2, 1),
        pltpu.roll(part, ROT // 2, 1),
    )
    return part * cosine + swapped * sine


def after(array, *others):
    anywhere = pl.BlockSpec(memory_space=pl.ANY)
    return pl.pallas_call(
        lambda *refs: None,
        in_specs=[anywhere] * (1 + len(others)),
        out_specs=anywhere,
        out_shape=jax.ShapeDtypeStruct(array.shape, array.dtype),
        input_output_aliases={0: 0},
        name="after",
    )(array, *others)


def across(z, n, values):
    picked = jnp.int32(0)
    for at in range(n):
        picked = picked + jnp.where(z == at, values[at], 0)
    return picked


def opening_kernel(n, heads, *refs):
    x_ref, in_ref, up_ref, down_ref, vec_ref, in_bias_ref, up_bias_ref, cos_ref, sin_ref = refs[:9]
    x_rows, qkv_ref, joint_ref, slope_ref, part_ref = refs[9:14]
    w_in, w_up, w_down, chunk, attn_in, mlp_in, qkv_out, act_out, slope_out, part_out = refs[14:24]
    send, recv, load, store = refs[24:]
    z = lax.axis_index("mp")
    t, d = x_ref.shape
    in_width, hidden = in_ref.shape[1], up_ref.shape[1]
    ids = pl.DeviceIdType.MESH

    barrier = pltpu.get_barrier_semaphore()
    for way in (1, -1):

        @pl.when((z + way >= 0) & (z + way < n))
        def _():
            pl.semaphore_signal(barrier, inc=1, device_id={"mp": z + way}, device_id_type=ids)

    pl.semaphore_wait(barrier, 2 - jnp.where(z == 0, 1, 0) - jnp.where(z == n - 1, 1, 0))

    def rows_of(position):
        return pl.ds(pl.multiple_of(position * t, t), t)

    own = pltpu.make_async_copy(x_ref, x_rows.at[rows_of(z)], load.at[0])
    own.start()
    hops = {}
    for k in range(1, n):
        for way in (1, -1):
            origin = z - way * (k - 1)
            there = z + way
            goes = (origin >= 0) & (origin < n) & (there >= 0) & (there < n)
            rows = rows_of(jnp.clip(origin, 0, n - 1))
            at = 2 * (k - 1) + (way < 0)
            copy = pltpu.make_async_remote_copy(
                x_ref if k == 1 else x_rows.at[rows], x_rows.at[rows], send.at[at], recv.at[at], {"mp": there}, ids
            )
            arrives = (z - way * k >= 0) & (z - way * k < n)
            hops[k, way] = (copy, goes, arrives)

    def start_step(k):
        for way in (1, -1):
            copy, goes, _ = hops[k, way]
            pl.when(goes)(copy.start)

    start_step(1)
    weights = [
        pltpu.make_async_copy(source, target, load.at[1 + i])
        for i, (source, target) in enumerate(((in_ref, w_in), (up_ref, w_up), (down_ref, w_down)))
    ]
    for copy in weights:
        copy.start()
    order = arrival_order(n)
    positions = [across(z, n, [order[zz][s] for zz in range(n)]) for s in range(n)]

    def slot(s, unused):
        position = jnp.int32(0)
        for at in range(n):
            position = position + jnp.where(s == at, positions[at], 0)
        rows = rows_of(position)
        for k in range(1, n):

            @pl.when(s == k)
            def _():
                for way in (1, -1):
                    copy, _, arrives = hops[k, way]
                    pl.when(arrives)(copy.wait_recv)
                if k < n - 1:
                    start_step(k + 1)

        @pl.when(s == 0)
        def _():
            pltpu.make_async_copy(x_ref, chunk, load.at[4]).start()

        @pl.when(s > 0)
        def _():
            pltpu.make_async_copy(x_rows.at[rows], chunk, load.at[4]).start()

        pltpu.make_async_copy(x_ref, chunk, load.at[4]).wait()

        def norm_rows(i, unused):
            block = pl.ds(pl.multiple_of(i * 32, 32), 32)
            x = chunk[block, :].astype(F32)
            attn_in[block, :] = (x * vec_ref[0:1, :] + vec_ref[1:2, :]).astype(BF16)
            mlp_in[block, :] = (x * vec_ref[2:3, :] + vec_ref[3:4, :]).astype(BF16)
            return unused

        lax.fori_loop(0, t // 32, norm_rows, 0)
        outs = [
            pltpu.make_async_copy(qkv_out, qkv_ref.at[rows], store.at[0]),
            pltpu.make_async_copy(act_out, joint_ref.at[rows, pl.ds(heads * HD, hidden)], store.at[1]),
            pltpu.make_async_copy(slope_out, slope_ref.at[rows], store.at[2]),
            pltpu.make_async_copy(part_out, part_ref.at[rows], store.at[3]),
        ]

        @pl.when(s == 0)
        def _():
            weights[0].wait()

        @pl.when(s > 0)
        def _():
            outs[0].wait()

        cosine, sine = cos_ref[rows, :], sin_ref[rows, :]
        for j in range(3 * heads):
            cols = slice(j * HD, (j + 1) * HD)
            acc = dot(attn_in[...], w_in[:, cols]) + in_bias_ref[:, cols]
            if j % 3 < 2:
                scale = HD**-0.5 if j % 3 == 0 else 1.0
                qkv_out[:, cols] = jnp.concatenate(
                    [turn(acc[:, :128], cosine, sine) * scale, acc[:, 128:] * scale], axis=1
                ).astype(BF16)
            else:
                qkv_out[:, cols] = acc.astype(BF16)
        outs[0].start()

        @pl.when(s == 0)
        def _():
            weights[1].wait()
            weights[2].wait()

        @pl.when(s > 0)
        def _():
            for copy in outs[1:]:
                copy.wait()

        tile = min(512, hidden)
        for first in range(0, hidden, tile):
            cols = slice(first, first + tile)
            u = dot(mlp_in[...], w_up[:, cols]) + up_bias_ref[:, cols]
            below = 0.5 + 0.5 * lax.erf(u * (0.5**0.5))
            act_out[:, cols] = (u * below).astype(BF16)
            density = jnp.exp(u * u * -0.5) * ((2.0 * np.pi) ** -0.5)
            slope_out[:, cols] = (below + u * density).astype(BF16)
        outs[1].start()
        outs[2].start()
        for first in range(0, d, 512):
            cols = slice(first, first + 512)
            part_out[:, cols] = dot(act_out[...], w_down[:, cols]).astype(BF16)
        outs[3].start()

        @pl.when(s == n - 1)
        def _():
            for copy in outs:
                copy.wait()

        return unused

    lax.fori_loop(0, n, slot, 0)
    own.wait()
    for copy, goes, _ in hops.values():
        pl.when(goes)(copy.wait_send)


def opening(n, x, flat_in, up_weight, down_weight, vectors, in_bias, up_bias, cosine, sine):
    t, d = x.shape
    in_width, hidden = flat_in.shape[1], up_weight.shape[1]
    heads, rows = in_width // (3 * HD), n * t
    anywhere, whole = pl.BlockSpec(memory_space=pl.ANY), pl.BlockSpec(memory_space=pltpu.VMEM)
    return pl.pallas_call(
        functools.partial(opening_kernel, n, heads),
        in_specs=[anywhere] * 4 + [whole] * 5,
        out_specs=[anywhere] * 5,
        out_shape=[
            jax.ShapeDtypeStruct(shape, BF16)
            for shape in (
                (rows, d), (rows, in_width), (rows, heads * HD + hidden), (rows, hidden), (rows, d),
            )
        ],
        scratch_shapes=[
            pltpu.VMEM(shape, BF16)
            for shape in (
                (d, in_width), (d, hidden), (hidden, d), (t, d), (t, d), (t, d),
                (t, in_width), (t, hidden), (t, hidden), (t, d),
            )
        ]
        + [pltpu.SemaphoreType.DMA((2 * (n - 1),))] * 2
        + [pltpu.SemaphoreType.DMA((5,)), pltpu.SemaphoreType.DMA((4,))],
        compiler_params=pltpu.CompilerParams(
            vmem_limit_bytes=VMEM_LIMIT, collective_id=1, has_side_effects=True
        ),
        cost_estimate=pl.CostEstimate(
            flops=16 * 2 * rows * d * (in_width + 2 * hidden), bytes_accessed=200 * 2**20, transcendentals=0
        ),
        name="opening",
    )(x, flat_in, up_weight, down_weight, vectors, in_bias, up_bias, cosine, sine)


def up_back_kernel(g_ref, w_ref, slope_ref, out_ref):
    out_ref[...] = (dot(g_ref[...], w_ref[...], NT) * slope_ref[...].astype(F32)).astype(BF16)


def up_back(in_width, tile, g, down_weight, slope):
    rows, d = g.shape
    width = down_weight.shape[0]
    first = in_width // tile
    block = min(rows, 1024)
    return pl.pallas_call(
        up_back_kernel,
        grid=(rows // block, width // tile),
        in_specs=[
            pl.BlockSpec((block, d), lambda i, j: (i, 0)),
            pl.BlockSpec((tile, d), lambda i, j: (j, 0)),
            pl.BlockSpec((block, tile), lambda i, j: (i, j)),
        ],
        out_specs=pl.BlockSpec((block, tile), lambda i, j: (i, first + j)),
        out_shape=jax.ShapeDtypeStruct((rows, in_width + width), BF16),
        compiler_params=params(),
        cost_estimate=pl.CostEstimate(
            flops=2 * rows * d * width, bytes_accessed=2 * (rows * d + d * width + 2 * rows * width), transcendentals=0
        ),
        name="up_back",
    )(g, down_weight, slope)


def cross_kernel(heads_tile, x_ref, back_ref, in_ref, up_ref, cross_ref, sums_ref, total_ref, xt_ref):
    width, in_width = back_ref.shape[1], in_ref.shape[1]
    tile = heads_tile

    @pl.when(pl.program_id(0) == 0)
    def _():
        total_ref[...] = jnp.zeros_like(total_ref)
        step = 64

        def body(i, unused):
            rows = back_ref[pl.ds(pl.multiple_of(i * step, step), step), :].astype(F32)
            for r in range(0, step, 8):
                total_ref[...] += rows[r : r + 8]
            return unused

        lax.fori_loop(0, back_ref.shape[0] // step, body, 0)
        total_ref[...] = jnp.broadcast_to(jnp.sum(total_ref[...], axis=0, keepdims=True), total_ref.shape)

    xt_ref[...] = x_ref[...].T
    sums = [jnp.zeros((xt_ref.shape[0], 128), F32) for _ in range(4)]
    for first in range(0, width, tile):
        cols = slice(first, first + tile)
        product = dot(xt_ref[...], back_ref[:, cols])
        cross_ref[:, cols] = product.astype(BF16)
        inside = first < in_width
        wide = (in_ref[:, cols] if inside else up_ref[:, first - in_width : first - in_width + tile]).astype(F32)
        kind = 0 if inside else 2
        for at, term in ((kind, product * wide), (kind + 1, total_ref[0:1, cols] * wide)):
            for lane in range(0, tile, 128):
                sums[at] = sums[at] + term[:, lane : lane + 128]
    lane = lax.broadcasted_iota(jnp.int32, sums[0].shape, 1)
    out = jnp.zeros_like(sums[0])
    for at in range(4):
        out = out + jnp.where(lane == at, jnp.sum(sums[at], axis=1, keepdims=True), 0.0)
    sums_ref[...] = out


def cross_products(heads_tile, x_rows, back, flat_in, up_weight):
    rows, d = x_rows.shape
    width = back.shape[1]
    tile = 512
    once = pl.Buffered(1)
    return pl.pallas_call(
        functools.partial(cross_kernel, heads_tile),
        grid=(d // tile,),
        in_specs=[
            pl.BlockSpec((rows, tile), lambda i: (0, i)),
            pl.BlockSpec((rows, width), lambda i: (0, 0), pipeline_mode=once),
            pl.BlockSpec((tile, flat_in.shape[1]), lambda i: (i, 0)),
            pl.BlockSpec((tile, up_weight.shape[1]), lambda i: (i, 0)),
        ],
        out_specs=[
            pl.BlockSpec((tile, width), lambda i: (i, 0)),
            pl.BlockSpec((tile, 128), lambda i: (i, 0)),
            pl.BlockSpec((8, width), lambda i: (0, 0)),
        ],
        out_shape=[
            jax.ShapeDtypeStruct((d, width), BF16),
            jax.ShapeDtypeStruct((d, 128), F32),
            jax.ShapeDtypeStruct((8, width), F32),
        ],
        scratch_shapes=[pltpu.VMEM((tile, rows), BF16)],
        compiler_params=params(),
        cost_estimate=pl.CostEstimate(
            flops=2 * rows * d * width, bytes_accessed=2 * (rows * d + rows * width + 2 * d * width), transcendentals=0
        ),
        name="cross",
    )(x_rows, back, flat_in, up_weight)


def allowed(j, i, t, start):
    key = j * KBLOCK + lax.broadcasted_iota(jnp.int32, (KBLOCK, t), 0)
    query = i * t + lax.broadcasted_iota(jnp.int32, (1, t), 1)
    return (key >= start) & (key <= query)


def attend_kernel(t, heads, low_ref, qkv_ref, start_ref, held_ref, out_ref, log_ref, vt_ref, acc_ref):
    blocks = qkv_ref.shape[0] // t
    per = t // KBLOCK

    for h in range(heads):
        for c in range(blocks):
            rows = pl.ds(c * t, t)
            vt_ref[h, :, rows] = qkv_ref[rows, (3 * h + 2) * HD : (3 * h + 3) * HD].T

    def query_block(i, unused):
        row = pl.multiple_of(i * t, t)
        where = pl.ds(pl.multiple_of(i * t, t), t)
        start = start_ref[:, where]
        acc_ref[...] = jnp.zeros_like(acc_ref)

        def key_block(j, carried):
            place = pl.multiple_of(j * KBLOCK, KBLOCK)
            mask = allowed(j, i, t, start)
            new = []
            for h in range(heads):
                top, total = carried[h]
                query = qkv_ref[pl.ds(row, t), 3 * h * HD : (3 * h + 1) * HD]
                key = qkv_ref[pl.ds(place, KBLOCK), (3 * h + 1) * HD : (3 * h + 2) * HD]
                s = jnp.where(mask, dot(key, query, NT), NEG_FILL)
                higher = jnp.maximum(top, jnp.max(s, axis=0, keepdims=True))
                p = jnp.exp(s - higher)
                shrink = jnp.exp(top - higher)
                total = total * shrink + jnp.sum(p, axis=0, keepdims=True)
                vt = vt_ref[h, :, pl.ds(place, KBLOCK)]
                acc_ref[h] = acc_ref[h] * shrink + dot(vt, p.astype(BF16))
                new.append((higher, total))
            return tuple(new)

        first = (jnp.full((1, t), 2 * NEG_FILL, F32), jnp.zeros((1, t), F32))
        carried = lax.fori_loop(low_ref[i], (i + 1) * per, key_block, (first,) * heads)
        for h in range(heads):
            top, total = carried[h]
            log_ref[h : h + 1, where] = top + jnp.log(total)
            out_ref[pl.ds(row, t), h * HD : (h + 1) * HD] = (acc_ref[h] / total).T.astype(BF16)
        return unused

    lax.fori_loop(0, blocks, query_block, 0)


def attend(t, low, qkv, start, hidden):
    rows, width = qkv.shape
    heads = width // (3 * HD)
    whole = pl.BlockSpec(memory_space=pltpu.VMEM)
    return pl.pallas_call(
        functools.partial(attend_kernel, t, heads),
        grid=(1,),
        in_specs=[pl.BlockSpec(memory_space=pltpu.SMEM)] + [whole] * 2 + [pl.BlockSpec(memory_space=pl.ANY)],
        out_specs=[pl.BlockSpec((rows, heads * HD), lambda i: (0, 0)), whole],
        out_shape=[
            jax.ShapeDtypeStruct(hidden.shape, BF16),
            jax.ShapeDtypeStruct((heads, rows), F32),
        ],
        scratch_shapes=[pltpu.VMEM((heads, HD, rows), BF16), pltpu.VMEM((heads, HD, t), F32)],
        input_output_aliases={3: 0},
        compiler_params=params(),
        cost_estimate=pl.CostEstimate(
            flops=2 * rows * rows * HD * heads,
            bytes_accessed=2 * rows * width,
            transcendentals=rows * rows * heads // 2,
        ),
        name="attend",
    )(low, qkv, start, hidden)


def attend_back_kernel(
    t, heads, high_ref, qkv_ref, grad_ref, out_ref, log_ref, start_ref, cos_ref, sin_ref, held_ref, after_ref,
    proj_ref, query_grad, delta, key_grad, value_grad,
):
    rows = qkv_ref.shape[0]
    blocks = rows // t
    per = t // KBLOCK
    query_grad[...] = jnp.zeros_like(query_grad)

    def prepare(i, unused):
        row = pl.multiple_of(i * t, t)
        for h in range(heads):
            cols = slice(h * HD, (h + 1) * HD)
            both = grad_ref[pl.ds(row, t), cols].astype(F32) * out_ref[pl.ds(row, t), cols].astype(F32)
            delta[h : h + 1, pl.ds(pl.multiple_of(i * t, t), t)] = jnp.sum(both.T, axis=0, keepdims=True)
        return unused

    lax.fori_loop(0, blocks, prepare, 0)

    def turned_back(grad, place, count):
        cosine, sine = cos_ref[pl.ds(place, count), :], sin_ref[pl.ds(place, count), :]
        return turn(grad[:, :128], cosine, -sine)

    def key_block(j, unused):
        place = pl.multiple_of(j * KBLOCK, KBLOCK)
        key_grad[...] = jnp.zeros_like(key_grad)
        value_grad[...] = jnp.zeros_like(value_grad)

        def query_block(i, unused):
            row = pl.multiple_of(i * t, t)
            where = pl.ds(pl.multiple_of(i * t, t), t)
            mask = allowed(j, i, t, start_ref[:, where])
            for h in range(heads):
                query = qkv_ref[pl.ds(row, t), 3 * h * HD : (3 * h + 1) * HD]
                key = qkv_ref[pl.ds(place, KBLOCK), (3 * h + 1) * HD : (3 * h + 2) * HD]
                value = qkv_ref[pl.ds(place, KBLOCK), (3 * h + 2) * HD : (3 * h + 3) * HD]
                grad = grad_ref[pl.ds(row, t), h * HD : (h + 1) * HD]
                s = dot(key, query, NT) - log_ref[h : h + 1, where]
                p = jnp.exp(jnp.where(mask, s, NEG_FILL))
                p_grad = dot(value, grad, NT)
                value_grad[h] += dot(p.astype(BF16), grad)
                s_grad = (p * (p_grad - delta[h : h + 1, where])).astype(BF16)
                key_grad[h] += dot(s_grad, query)
                query_grad[pl.ds(row, t), h * HD : (h + 1) * HD] += dot(s_grad, key, TN)
            return unused

        lax.fori_loop(j // per, high_ref[j], query_block, 0)
        for h in range(heads):
            base = 3 * h * HD
            grad = key_grad[h]
            proj_ref[pl.ds(place, KBLOCK), base + HD : base + HD + 128] = turned_back(grad, place, KBLOCK).astype(BF16)
            proj_ref[pl.ds(place, KBLOCK), base + HD + 128 : base + 2 * HD] = grad[:, 128:].astype(BF16)
            proj_ref[pl.ds(place, KBLOCK), base + 2 * HD : base + 3 * HD] = value_grad[h].astype(BF16)
        return unused

    lax.fori_loop(0, rows // KBLOCK, key_block, 0)

    def finish(c, unused):
        place = pl.multiple_of(c * t, t)
        for h in range(heads):
            base = 3 * h * HD
            grad = query_grad[pl.ds(place, t), h * HD : (h + 1) * HD] * HD**-0.5
            proj_ref[pl.ds(place, t), base : base + 128] = turned_back(grad, place, t).astype(BF16)
            proj_ref[pl.ds(place, t), base + 128 : base + HD] = grad[:, 128:].astype(BF16)
        return unused

    lax.fori_loop(0, blocks, finish, 0)


def attend_back(t, high, qkv, heads_grad, hidden, logs, start, cosine, sine, buffer, after):
    rows, width = qkv.shape
    heads = width // (3 * HD)
    whole = pl.BlockSpec(memory_space=pltpu.VMEM)
    left = pl.BlockSpec((rows, heads * HD), lambda i: (0, 0))
    return pl.pallas_call(
        functools.partial(attend_back_kernel, t, heads),
        grid=(1,),
        in_specs=[pl.BlockSpec(memory_space=pltpu.SMEM)]
        + [whole, whole, left, whole, whole, whole, whole]
        + [pl.BlockSpec(memory_space=pl.ANY)] * 2,
        out_specs=pl.BlockSpec((rows, width), lambda i: (0, 0)),
        out_shape=jax.ShapeDtypeStruct(buffer.shape, BF16),
        scratch_shapes=[
            pltpu.VMEM((rows, heads * HD), F32),
            pltpu.VMEM((heads, rows), F32),
            pltpu.VMEM((heads, KBLOCK, HD), F32),
            pltpu.VMEM((heads, KBLOCK, HD), F32),
        ],
        input_output_aliases={8: 0},
        compiler_params=params(),
        cost_estimate=pl.CostEstimate(
            flops=5 * rows * rows * HD * heads,
            bytes_accessed=4 * rows * width,
            transcendentals=rows * rows * heads // 2,
        ),
        name="attend_back",
    )(high, qkv, heads_grad, hidden, logs, start, cosine, sine, buffer, after)


def add_rows(into, at, terms, terms_at, count):
    step = 32

    def body(i, unused):
        rows = pl.ds(pl.multiple_of(at + i * step, step), step)
        more = pl.ds(pl.multiple_of(terms_at + i * step, step), step)
        into[rows, :] = (into[rows, :].astype(F32) + terms[more, :].astype(F32)).astype(BF16)
        return unused

    lax.fori_loop(0, count // step, body, 0)


def closing_kernel(n, groups, *refs):
    bits, mp_bits = groups.bit_length() - 1, n.bit_length() - 1
    part_ref, cross_ref, small_ref, norm_ref, summed_ref, small_out = refs[:6]
    come = {1: refs[6], -1: refs[7]}
    keep, core_in = refs[8:10]
    stage_in = [refs[10 : 9 + bits], refs[9 + bits : 8 + 2 * bits]]
    small_in, small_sum, send, recv, load = refs[8 + 2 * bits :]
    z, group = lax.axis_index("mp"), lax.axis_index("dp")
    t = norm_ref.shape[0]
    half = keep.shape[0]
    quarter = half // 2
    ids = pl.DeviceIdType.MESH
    sems = iter(range(send.shape[0]))

    def bit_of(b):
        return lax.rem(group // 2**b, 2)

    def dp_peer(b):
        return {"dp": group + (1 - 2 * bit_of(b)) * 2**b}

    def mp_peer(b):
        return {"mp": z + (1 - 2 * lax.rem(z // 2**b, 2)) * 2**b}

    def remote(source, target, device):
        k = next(sems)
        return pltpu.make_async_remote_copy(source, target, send.at[k], recv.at[k], device, ids)

    barrier = pltpu.get_barrier_semaphore()
    for peer in [dp_peer(b) for b in range(bits)] + [mp_peer(b) for b in range(mp_bits)]:
        pl.semaphore_signal(barrier, inc=1, device_id=peer, device_id_type=ids)

    @pl.when(z + 1 < n)
    def _():
        pl.semaphore_signal(barrier, inc=1, device_id={"mp": z + 1}, device_id_type=ids)

    @pl.when(z >= 1)
    def _():
        pl.semaphore_signal(barrier, inc=1, device_id={"mp": z - 1}, device_id_type=ids)

    ends = jnp.where(z == 0, 1, 0) + jnp.where(z == n - 1, 1, 0)
    pl.semaphore_wait(barrier, bits + mp_bits + 2 - ends)

    small_peers = [dp_peer(b) for b in range(bits)] + [mp_peer(b) for b in range(mp_bits)]
    small_copies = []

    def small_step(i):
        if i == 0:
            small_sum[0] = small_ref[...]
        else:
            small_copies[i - 1].wait_recv()
            if i - 1 < bits:
                total = small_sum[i - 1] + small_in[i - 1]
            else:
                total = small_sum[i - 1]
                small_sum[i, 8:, :] = total[8:]
                total = total[:8] + small_in[i - 1, :8, :]
            small_sum[i, : total.shape[0], :] = total
        if i < len(small_peers):
            small_copies.append(remote(small_sum.at[i], small_in.at[i], small_peers[i]))
            small_copies[i].start()
        else:
            small_out[...] = small_sum[i]

    hops = {}

    def rows_at(distance):
        return pl.multiple_of(jnp.clip(z + distance, 0, n - 1) * t, t)

    def line_step(k):
        for way in (1, -1):
            buffer = come[way].at[k]
            here = (z + k < n) if way == 1 else (z >= k)
            first = (z == 0) if way == 1 else (z == n - 1)
            if k < n - 1:

                @pl.when(here & jnp.logical_not(first))
                def _():
                    hops[k + 1, way][0].wait_recv()
                    add_rows(buffer, 0, part_ref, rows_at(way * k), t) if k > 0 else None

            if k > 0:

                @pl.when(here & first)
                def _():
                    buffer[...] = part_ref[pl.ds(rows_at(way * k), t), :]

                hops[k, way] = (remote(buffer, come[way].at[k - 1], {"mp": z + way}), here)

                @pl.when(here)
                def _():
                    hops[k, way][0].start()

        if k == 0:
            step = 32

            def body(i, unused):
                rows = pl.ds(pl.multiple_of(i * step, step), step)
                total = part_ref[pl.ds(pl.multiple_of(z * t + i * step, step), step), :].astype(F32)
                for way in (1, -1):
                    first = (z == 0) if way == 1 else (z == n - 1)
                    total = total + jnp.where(first, 0.0, come[way][0, rows, :].astype(F32))
                norm_ref[rows, :] = total
                return unused

            lax.fori_loop(0, t // step, body, 0)

    mine, other = bit_of(0) * half, (1 - bit_of(0)) * half
    path = [list(range(1, bits)), list(range(bits - 1, 0, -1))]
    base = [0, quarter]
    size = quarter
    regions = [[], []]
    current = [None, None]

    def first_halving():
        own.wait()
        for p in (0, 1):
            core[p].wait_recv()
            add_rows(keep, p * quarter, core_in, p * quarter, quarter)
            halve(p, 0)

    def halve(p, s):
        b = path[p][s]
        part = quarter // 2 ** (s + 1)
        regions[p].append((base[p], 2 * part))
        away = pl.multiple_of(base[p] + (1 - bit_of(b)) * part, 32)
        current[p] = remote(keep.at[pl.ds(away, part)], stage_in[p][s], dp_peer(b))
        current[p].start()
        started.append(current[p])
        base[p] = base[p] + bit_of(b) * part

    def next_halving(s):
        for p in (0, 1):
            current[p].wait_recv()
            add_rows(keep, base[p], stage_in[p][s - 1], 0, quarter // 2**s)
            if s < bits - 1:
                halve(p, s)
            else:
                count = quarter // 2**s
                place = pl.ds(pl.multiple_of(base[p], 32), count)
                target = summed_ref.at[pl.ds(pl.multiple_of(mine + base[p], 32), count)]
                local = pltpu.make_async_copy(keep.at[place], target, load.at[1 + p])
                local.start()
                current[p] = remote(keep.at[place], target, dp_peer(path[p][s - 1]))
                current[p].start()
                started.append(current[p])
                locals_.append(local)

    def doubling(s):
        for p in (0, 1):
            current[p].wait_recv()
            if s == bits - 2:
                locals_[p].wait()
            at, count = regions[p][s]
            rows = summed_ref.at[pl.ds(pl.multiple_of(mine + at, 32), count)]
            current[p] = remote(rows, rows, dp_peer(path[p][s - 1] if s > 0 else 0))
            current[p].start()
            started.append(current[p])

    started, locals_ = [], []
    core = [
        remote(
            cross_ref.at[pl.ds(pl.multiple_of(other + p * quarter, 32), quarter)],
            core_in.at[pl.ds(p * quarter, quarter)],
            dp_peer(0),
        )
        for p in (0, 1)
    ]
    own = pltpu.make_async_copy(cross_ref.at[pl.ds(pl.multiple_of(mine, 32), half)], keep, load.at[0])
    for copy in core:
        copy.start()
    own.start()
    line_step(n - 1)
    small_step(0)

    sums = [first_halving]
    sums += [functools.partial(next_halving, s) for s in range(1, bits)]
    sums += [functools.partial(doubling, s) for s in range(bits - 2, -1, -1)]
    lines = list(range(n - 2, -1, -1))
    smalls = list(range(1, bits + mp_bits + 1))
    for at, step in enumerate(sums):
        step()
        if at in (0, bits - 1) or at >= bits:
            if lines:
                line_step(lines.pop(0))
        if smalls:
            small_step(smalls.pop(0))
    for k in lines:
        line_step(k)
    for i in smalls:
        small_step(i)
    for p in (0, 1):
        current[p].wait_recv()
    for copy in core + started + small_copies:
        copy.wait_send()
    for copy, here in hops.values():

        @pl.when(here)
        def _():
            copy.wait_send()


def closing_sums(n, groups, part, cross, small):
    rows, d = part.shape
    width = cross.shape[1]
    t, half = rows // n, d // 2
    bits, mp_bits = groups.bit_length() - 1, n.bit_length() - 1
    stages = [pltpu.VMEM((half // 2 // 2**s, width), BF16) for s in range(1, bits)]
    copies = 2 + 2 * (bits - 1) + 2 + 2 * (bits - 1) + 2 * (n - 1) + bits + mp_bits
    whole = pl.BlockSpec(memory_space=pltpu.VMEM)
    return pl.pallas_call(
        functools.partial(closing_kernel, n, groups),
        in_specs=[whole, pl.BlockSpec(memory_space=pl.ANY), whole],
        out_specs=[whole, pl.BlockSpec(memory_space=pl.ANY), whole],
        out_shape=[
            jax.ShapeDtypeStruct((t, d), F32),
            jax.ShapeDtypeStruct((d, width), BF16),
            jax.ShapeDtypeStruct(small.shape, F32),
        ],
        scratch_shapes=[pltpu.VMEM((n, t, d), BF16)] * 2
        + [pltpu.VMEM((half, width), BF16)] * 2
        + stages * 2
        + [pltpu.VMEM((bits + mp_bits,) + small.shape, F32), pltpu.VMEM((bits + mp_bits + 1,) + small.shape, F32)]
        + [pltpu.SemaphoreType.DMA((copies,))] * 2
        + [pltpu.SemaphoreType.DMA((3,))],
        compiler_params=pltpu.CompilerParams(
            vmem_limit_bytes=VMEM_LIMIT, collective_id=0, has_side_effects=True
        ),
        name="closing_sums",
    )(part, cross, small)


def scatter_sum(part, own, z, n):
    right = left = None
    for k in range(n - 1, 0, -1):
        for_right, for_left = part(z + k), part(z - k)
        if right is not None:
            for_right = (for_right.astype(F32) + right.astype(F32)).astype(BF16)
            for_left = (for_left.astype(F32) + left.astype(F32)).astype(BF16)
        right = lax.ppermute(for_right, "mp", [(i, i + 1) for i in range(n - k)])
        left = lax.ppermute(for_left, "mp", [(i, i - 1) for i in range(k, n)])
    return own + right.astype(F32) + left.astype(F32)


def exchange(part, own, z, n):
    came = [None] * (2 * n - 1)
    came[n - 1] = own
    for k in range(1, n):
        came[n - 1 - k] = lax.ppermute(part(z + k), "mp", [(i, i + k) for i in range(n - k)])
        came[n - 1 + k] = lax.ppermute(part(z - k), "mp", [(i, i - k) for i in range(k, n)])
    return lax.dynamic_slice_in_dim(jnp.stack(came), n - 1 - z, n, axis=0)


def document_starts(row_lengths, length):
    count = row_lengths.shape[0]
    before = np.tri(count, k=-1, dtype=np.int32)
    starts = jnp.sum(before * row_lengths[None, :], axis=1)
    places = jnp.arange(length, dtype=jnp.int32)
    return jnp.max(jnp.where(starts[None, :] <= places[:, None], starts[None, :], 0), axis=1)


def per_device(
    tokens, seq_lengths, attn_gain, attn_shift, mlp_gain, mlp_shift, in_weight, in_bias, out_weight, out_bias,
    up_weight, up_bias, down_weight, down_bias, cotangent,
):
    n, groups = lax.axis_size("mp"), lax.axis_size("dp")
    z, group = lax.axis_index("mp"), lax.axis_index("dp")
    t, d = tokens.shape[1:]
    length = n * t
    local_heads = in_weight.shape[1]
    in_width, heads_width, hidden = local_heads * 3 * HD, local_heads * HD, up_weight.shape[1]

    own_tokens = tokens[0].astype(F32)
    centred = own_tokens - jnp.mean(own_tokens, axis=-1, keepdims=True)
    spread = lax.rsqrt(jnp.mean(centred * centred, axis=-1, keepdims=True) + NORM_EPS)
    normed = centred * spread
    own_grad = cotangent[0]

    flat_in = lax.optimization_barrier(in_weight.reshape(d, in_width))
    share = out_weight.shape[0] // groups
    out_full = lax.all_gather(
        lax.dynamic_slice_in_dim(out_weight, group * share, share, axis=0), ("mp", "dp"), axis=0, tiled=True
    )

    starts = document_starts(seq_lengths[0], length)
    first_of_block = starts[::t]
    low = first_of_block // KBLOCK
    last_key = (jnp.arange(length // KBLOCK, dtype=jnp.int32) + 1) * KBLOCK - 1
    high = jnp.sum((first_of_block[None, :] <= last_key[:, None]).astype(jnp.int32), axis=1)
    offsets = jnp.arange(length, dtype=jnp.int32) - starts
    inverse = 10000.0 ** (-jnp.arange(0, ROT, 2).astype(F32) / ROT)
    angles = offsets.astype(F32)[:, None] * inverse[None, :]
    cosine, sine = jnp.cos(angles), jnp.sin(angles)
    cosine = jnp.concatenate([cosine, cosine, jnp.ones((length, 128 - ROT), F32)], axis=1)
    sine = jnp.concatenate([-sine, sine, jnp.zeros((length, 128 - ROT), F32)], axis=1)
    start_row = starts[None, :]

    vectors = jnp.stack([attn_gain, attn_shift, mlp_gain, mlp_shift] * 2)
    x_rows, qkv, joint, slope, down_part = opening(
        n, normed.astype(BF16), flat_in, up_weight, down_weight, vectors, in_bias.reshape(1, in_width),
        up_bias[None, :], cosine, sine,
    )
    g_rows = lax.all_gather(after(own_grad, slope, out_full), "mp", axis=0, tiled=True)
    joint, logs = attend(t, low, qkv, start_row, joint)

    def rows_for(array):
        def part(position):
            return lax.dynamic_slice_in_dim(array, jnp.clip(position, 0, n - 1) * t, t, axis=0)

        return part

    heads_out = joint[:, :heads_width]
    heads_mine = exchange(rows_for(heads_out), rows_for(heads_out)(z), z, n)
    heads_mine = heads_mine.transpose(1, 0, 2).reshape(t, n * heads_width)
    attn_branch = dot(heads_mine, out_full) + out_bias
    mlp_branch = scatter_sum(rows_for(down_part), rows_for(down_part)(z).astype(F32), z, n) + down_bias
    block_out = (own_tokens + attn_branch + mlp_branch).astype(BF16)
    squares = jnp.stack([jnp.sum(attn_branch * attn_branch), jnp.sum(mlp_branch * mlp_branch)])

    back = up_back(in_width, heads_width, g_rows, down_weight, slope)
    heads_grad = dot(g_rows, out_weight, NT).astype(BF16)
    out_down_grad = dot(joint, g_rows, TN).astype(BF16)
    back = attend_back(
        t, high, qkv, heads_grad, joint, logs, start_row, cosine, sine, back, out_down_grad
    )
    out_down_grad = lax.psum(out_down_grad, "dp")
    norm_part = (
        dot(back[:, :in_width], flat_in, NT) * attn_gain + dot(back[:, in_width:], up_weight, NT) * mlp_gain
    ).astype(BF16)
    cross, row_sums, total = cross_products(heads_width, x_rows, back, flat_in, up_weight)
    total = total[0]
    attn_sums = row_sums[:, 0:2].T
    mlp_sums = row_sums[:, 2:4].T
    bias_sum = jnp.sum(own_grad.astype(F32), axis=0)
    small = jnp.concatenate(
        [
            attn_sums,
            mlp_sums,
            bias_sum[None],
            jnp.pad(squares, (0, d - 2))[None],
            jnp.zeros((2, d), F32),
            jnp.pad(total[:in_width], (0, d - in_width))[None],
            jnp.pad(total[in_width:], (0, d - hidden))[None],
            jnp.zeros((6, d), F32),
        ]
    )
    norm_grad, cross, small = closing_sums(n, groups, norm_part, cross, small)
    mean_grad = jnp.mean(norm_grad, axis=-1, keepdims=True)
    mean_normed = jnp.mean(norm_grad * normed, axis=-1, keepdims=True)
    tokens_grad = (own_grad.astype(F32) + spread * (norm_grad - mean_grad - normed * mean_normed)).astype(BF16)
    in_total, up_total = small[8, :in_width], small[9, :hidden]
    in_cross = lax.optimization_barrier(cross[:, :in_width].reshape(d, local_heads, 3 * HD))
    grad_in_weight = (
        in_cross.astype(F32) * attn_gain[:, None, None]
        + attn_shift[:, None, None] * in_total.reshape(local_heads, 3 * HD)[None]
    )
    grad_up_weight = cross[:, in_width:].astype(F32) * mlp_gain[:, None] + mlp_shift[:, None] * up_total[None, :]
    element_count = float(groups * n * t * d)
    return (
        block_out[None],
        tokens_grad[None],
        small[0],
        small[1],
        small[2],
        small[3],
        grad_in_weight,
        in_total.reshape(local_heads, 3 * HD),
        out_down_grad[:heads_width].astype(F32),
        small[4],
        grad_up_weight,
        up_total,
        out_down_grad[heads_width:].astype(F32),
        small[4],
        jnp.sqrt(small[5, :2] / element_count),
    )


def solution(mesh):
    rows, weights = P("dp", "mp", None), P(None, "mp", None)
    in_specs = (
        rows, P("dp", None), P(), P(), P(), P(), weights, P("mp", None), P("mp", None), P(),
        P(None, "mp"), P("mp"), P("mp", None), P(), rows,
    )
    out_specs = (
        rows, rows, P(), P(), P(), P(), weights, P("mp", None), P("mp", None), P(),
        P(None, "mp"), P("mp"), P("mp", None), P(), P(),
    )
    return jax.shard_map(per_device, mesh=mesh, in_specs=in_specs, out_specs=out_specs, check_vma=False)
```

```python
import functools

import jax
import jax.numpy as jnp
import numpy as np
from jax import lax
from jax.experimental import pallas as pl
from jax.experimental.pallas import tpu as pltpu
from jax.sharding import PartitionSpec as P

HD = 256
ROT = 64
KBLOCK = 256
NORM_EPS = 1e-05
NEG_FILL = -1000000000.0
VMEM_LIMIT = 56 * 1024 * 1024
BF16 = jnp.bfloat16
F32 = jnp.float32

NT = (((1,), (1,)), ((), ()))
NN = (((1,), (0,)), ((), ()))
TN = (((0,), (0,)), ((), ()))


def dot(a, b, dims=NN):
    return lax.dot_general(a, b, dims, preferred_element_type=F32)


def arrival_order(n):
    return [sorted(range(n), key=lambda p, z=z: (abs(p - z), p)) for z in range(n)]


def params():
    return pltpu.CompilerParams(vmem_limit_bytes=VMEM_LIMIT)


def turn(part, cosine, sine):
    lane = lax.broadcasted_iota(jnp.int32, part.shape, 1)
    swapped = jnp.where(
        lane < ROT // 2,
        pltpu.roll(part, 128 - ROT // 2, 1),
        pltpu.roll(part, ROT // 2, 1),
    )
    return part * cosine + swapped * sine


def after(array, *others):
    anywhere = pl.BlockSpec(memory_space=pl.ANY)
    return pl.pallas_call(
        lambda *refs: None,
        in_specs=[anywhere] * (1 + len(others)),
        out_specs=anywhere,
        out_shape=jax.ShapeDtypeStruct(array.shape, array.dtype),
        input_output_aliases={0: 0},
        name="after",
    )(array, *others)


def across(z, n, values):
    picked = jnp.int32(0)
    for at in range(n):
        picked = picked + jnp.where(z == at, values[at], 0)
    return picked


def greet_line(z, n):
    barrier = pltpu.get_barrier_semaphore()
    for way in (1, -1):

        @pl.when((z + way >= 0) & (z + way < n))
        def _():
            pl.semaphore_signal(barrier, inc=1, device_id={"mp": z + way}, device_id_type=pl.DeviceIdType.MESH)

    pl.semaphore_wait(barrier, 2 - jnp.where(z == 0, 1, 0) - jnp.where(z == n - 1, 1, 0))


def line_gather(z, n, t, own, rows_ref, send, recv):
    hops = {}
    for k in range(1, n):
        for way in (1, -1):
            origin, there = z - way * (k - 1), z + way
            goes = (origin >= 0) & (origin < n) & (there >= 0) & (there < n)
            rows = rows_ref.at[pl.ds(pl.multiple_of(jnp.clip(origin, 0, n - 1) * t, t), t)]
            at = 2 * (k - 1) + (way < 0)
            copy = pltpu.make_async_remote_copy(
                own if k == 1 else rows, rows, send.at[at], recv.at[at], {"mp": there}, pl.DeviceIdType.MESH
            )
            arrives = (z - way * k >= 0) & (z - way * k < n)
            hops[k, way] = (copy, goes, arrives)
    return hops


def gather_step(hops, k):
    for way in (1, -1):
        copy, goes, _ = hops[k, way]
        pl.when(goes)(copy.start)


def gather_wait(hops, k):
    for way in (1, -1):
        copy, _, arrives = hops[k, way]
        pl.when(arrives)(copy.wait_recv)


def gather_end(hops):
    for copy, goes, _ in hops.values():
        pl.when(goes)(copy.wait_send)


def slot_positions(z, n):
    order = arrival_order(n)
    return [across(z, n, [order[zz][s] for zz in range(n)]) for s in range(n)]


def opening_kernel(n, heads, *refs):
    x_ref, in_ref, up_ref, down_ref, vec_ref, in_bias_ref, up_bias_ref, cos_ref, sin_ref = refs[:9]
    x_rows, qkv_ref, joint_ref, slope_ref, part_ref = refs[9:14]
    w_in, w_up, w_down, chunk, attn_in, mlp_in, qkv_out, act_out, slope_out, part_out = refs[14:24]
    send, recv, load, store = refs[24:]
    z = lax.axis_index("mp")
    t, d = x_ref.shape
    in_width, hidden = in_ref.shape[1], up_ref.shape[1]
    greet_line(z, n)

    def rows_of(position):
        return pl.ds(pl.multiple_of(position * t, t), t)

    own = pltpu.make_async_copy(chunk, x_rows.at[rows_of(z)], load.at[0])
    gather = line_gather(z, n, t, x_ref, x_rows, send, recv)
    gather_step(gather, 1)
    weights = [
        pltpu.make_async_copy(source, target, load.at[1 + i])
        for i, (source, target) in enumerate(((in_ref, w_in), (up_ref, w_up), (down_ref, w_down)))
    ]
    for copy in weights:
        copy.start()
    positions = slot_positions(z, n)

    def slot(s, unused):
        position = jnp.int32(0)
        for at in range(n):
            position = position + jnp.where(s == at, positions[at], 0)
        rows = rows_of(position)
        for k in range(1, n):

            @pl.when(s == k)
            def _():
                gather_wait(gather, k)
                if k < n - 1:
                    gather_step(gather, k + 1)

        @pl.when(s == 0)
        def _():
            pltpu.make_async_copy(x_ref, chunk, load.at[4]).start()

        @pl.when(s > 0)
        def _():
            pltpu.make_async_copy(x_rows.at[rows], chunk, load.at[4]).start()

        pltpu.make_async_copy(x_ref, chunk, load.at[4]).wait()
        pl.when(s == 0)(own.start)

        def norm_rows(i, unused):
            block = pl.ds(pl.multiple_of(i * 32, 32), 32)
            x = chunk[block, :].astype(F32)
            attn_in[block, :] = (x * vec_ref[0:1, :] + vec_ref[1:2, :]).astype(BF16)
            mlp_in[block, :] = (x * vec_ref[2:3, :] + vec_ref[3:4, :]).astype(BF16)
            return unused

        lax.fori_loop(0, t // 32, norm_rows, 0)
        outs = [
            pltpu.make_async_copy(qkv_out, qkv_ref.at[rows], store.at[0]),
            pltpu.make_async_copy(act_out, joint_ref.at[rows, pl.ds(heads * HD, hidden)], store.at[1]),
            pltpu.make_async_copy(slope_out, slope_ref.at[rows], store.at[2]),
            pltpu.make_async_copy(part_out, part_ref.at[rows], store.at[3]),
        ]

        @pl.when(s == 0)
        def _():
            weights[0].wait()

        @pl.when(s > 0)
        def _():
            outs[0].wait()

        cosine, sine = cos_ref[rows, :], sin_ref[rows, :]
        for j in range(3 * heads):
            cols = slice(j * HD, (j + 1) * HD)
            acc = dot(attn_in[...], w_in[:, cols]) + in_bias_ref[:, cols]
            if j % 3 < 2:
                scale = HD**-0.5 if j % 3 == 0 else 1.0
                qkv_out[:, cols] = jnp.concatenate(
                    [turn(acc[:, :128], cosine, sine) * scale, acc[:, 128:] * scale], axis=1
                ).astype(BF16)
            else:
                qkv_out[:, cols] = acc.astype(BF16)
        outs[0].start()

        @pl.when(s == 0)
        def _():
            own.wait()
            weights[1].wait()
            weights[2].wait()

        @pl.when(s > 0)
        def _():
            for copy in outs[1:]:
                copy.wait()

        tile = min(512, hidden)
        for first in range(0, hidden, tile):
            cols = slice(first, first + tile)
            u = dot(mlp_in[...], w_up[:, cols]) + up_bias_ref[:, cols]
            below = 0.5 + 0.5 * lax.erf(u * (0.5**0.5))
            act_out[:, cols] = (u * below).astype(BF16)
            density = jnp.exp(u * u * -0.5) * ((2.0 * np.pi) ** -0.5)
            slope_out[:, cols] = (below + u * density).astype(BF16)
        outs[1].start()
        outs[2].start()
        for first in range(0, d, 512):
            cols = slice(first, first + 512)
            part_out[:, cols] = dot(act_out[...], w_down[:, cols]).astype(BF16)
        outs[3].start()

        @pl.when(s == n - 1)
        def _():
            for copy in outs:
                copy.wait()

        return unused

    lax.fori_loop(0, n, slot, 0)
    gather_end(gather)


def opening(n, x, flat_in, up_weight, down_weight, vectors, in_bias, up_bias, cosine, sine):
    t, d = x.shape
    in_width, hidden = flat_in.shape[1], up_weight.shape[1]
    heads, rows = in_width // (3 * HD), n * t
    anywhere, whole = pl.BlockSpec(memory_space=pl.ANY), pl.BlockSpec(memory_space=pltpu.VMEM)
    return pl.pallas_call(
        functools.partial(opening_kernel, n, heads),
        in_specs=[anywhere] * 4 + [whole] * 5,
        out_specs=[anywhere] * 5,
        out_shape=[
            jax.ShapeDtypeStruct(shape, BF16)
            for shape in (
                (rows, d), (rows, in_width), (rows, heads * HD + hidden), (rows, hidden), (rows, d),
            )
        ],
        scratch_shapes=[
            pltpu.VMEM(shape, BF16)
            for shape in (
                (d, in_width), (d, hidden), (hidden, d), (t, d), (t, d), (t, d),
                (t, in_width), (t, hidden), (t, hidden), (t, d),
            )
        ]
        + [pltpu.SemaphoreType.DMA((2 * (n - 1),))] * 2
        + [pltpu.SemaphoreType.DMA((5,)), pltpu.SemaphoreType.DMA((4,))],
        compiler_params=pltpu.CompilerParams(
            vmem_limit_bytes=VMEM_LIMIT, collective_id=1, has_side_effects=True
        ),
        cost_estimate=pl.CostEstimate(
            flops=16 * 2 * rows * d * (in_width + 2 * hidden), bytes_accessed=200 * 2**20, transcendentals=0
        ),
        name="opening",
    )(x, flat_in, up_weight, down_weight, vectors, in_bias, up_bias, cosine, sine)


def middle_kernel(n, in_width, *refs):
    g_ref, part_ref, joint_ref, slope_ref, out_ref, down_ref = refs[:6]
    g_rows, heads_grad, back, grads, to_right, to_left = refs[7:13]
    w_out, w_down, acc, chunk, hidden_in, slope_in, up_out, heads_out, stage, terms = refs[13:23]
    come = {1: refs[23], -1: refs[24]}
    send, recv, load, store = refs[25:]
    z = lax.axis_index("mp")
    t, d = g_ref.shape
    heads_width, hidden = out_ref.shape[0], down_ref.shape[0]
    ids = pl.DeviceIdType.MESH
    greet_line(z, n)

    def rows_of(position):
        return pl.ds(pl.multiple_of(position * t, t), t)

    gather = line_gather(z, n, t, g_ref, g_rows, send, recv)
    gather_step(gather, 1)
    weights = [
        pltpu.make_async_copy(out_ref, w_out, load.at[1]),
        pltpu.make_async_copy(down_ref, w_down, load.at[2]),
    ]
    for copy in weights:
        copy.start()
    positions = slot_positions(z, n)
    hops = {}
    for k in range(1, n):
        for way, target in ((1, to_right), (-1, to_left)):
            here = (z + k < n) if way == 1 else (z >= k)
            first = (z == 0) if way == 1 else (z == n - 1)
            source = part_ref.at[rows_of(jnp.clip(z + way * k, 0, n - 1))]
            buffer = come[way].at[k - 1] if k < n - 1 else None
            if k > 1:
                at = 2 * (n - 1) + 2 * (k - 2) + (way < 0)
                bare, passed = (
                    from_ref
                    and pltpu.make_async_remote_copy(
                        from_ref, come[way].at[k - 2], send.at[at], recv.at[at], {"mp": z + way}, ids
                    )
                    for from_ref in (source, buffer)
                )
            else:
                bare, passed = (pltpu.make_async_copy(from_ref, target, load.at[0]) for from_ref in (terms, buffer))
            terms_copy = pltpu.make_async_copy(source, terms, load.at[3])
            hops[k, way] = (here & first, here & jnp.logical_not(first), here, bare, passed, terms_copy, buffer)

    def line_step(k):
        for way in (1, -1):
            first, later, _, bare, passed, terms_copy, buffer = hops[k, way]

            @pl.when(first)
            def _():
                if k == 1:
                    terms_copy.start()
                    terms_copy.wait()
                bare.start()
                if k == 1:
                    bare.wait()

            if k < n - 1:

                @pl.when(later)
                def _():
                    hops[k + 1, way][3].wait_recv()
                    terms_copy.start()
                    terms_copy.wait()
                    add_rows(buffer, 0, terms, 0, t)
                    passed.start()
                    if k == 1:
                        passed.wait()

    def slot(s, unused):
        position = jnp.int32(0)
        for at in range(n):
            position = position + jnp.where(s == at, positions[at], 0)
        rows = rows_of(position)
        inputs = [
            pltpu.make_async_copy(joint_ref.at[rows], hidden_in, load.at[5]),
            pltpu.make_async_copy(slope_ref.at[rows], slope_in, load.at[6]),
        ]
        for copy in inputs:
            copy.start()
        for k in range(1, n):

            @pl.when(s == k)
            def _():
                gather_wait(gather, k)
                if k < n - 1:
                    gather_step(gather, k + 1)
                    line_step(n - k)

        @pl.when(s == 0)
        def _():
            pltpu.make_async_copy(g_ref, chunk, load.at[4]).start()
            weights[0].wait()
            weights[1].wait()

        @pl.when(s > 0)
        def _():
            pltpu.make_async_copy(g_rows.at[rows], chunk, load.at[4]).start()

        pltpu.make_async_copy(g_ref, chunk, load.at[4]).wait()
        for copy in inputs:
            copy.wait()
        outs = [
            pltpu.make_async_copy(heads_out, heads_grad.at[rows], store.at[0]),
            pltpu.make_async_copy(up_out, back.at[rows, pl.ds(in_width, hidden)], store.at[1]),
        ]

        @pl.when(s > 0)
        def _():
            for copy in outs:
                copy.wait()

        heads_out[...] = dot(chunk[...], w_out[...], NT).astype(BF16)
        outs[0].start()
        tile = min(512, hidden)
        for first in range(0, hidden, tile):
            cols = slice(first, first + tile)
            up_grad = dot(chunk[...], w_down[cols, :], NT) * slope_in[:, cols].astype(F32)
            up_out[:, cols] = up_grad.astype(BF16)
        outs[1].start()

        def grad_tile(j, unused):
            low = pl.multiple_of(j * heads_width, heads_width)
            turned = hidden_in[:, pl.ds(low, heads_width)].T
            into = pl.ds(low, heads_width)
            for first in range(0, d, 512):
                cols = slice(first, first + 512)
                product = dot(turned, chunk[:, cols])

                @pl.when(s == 0)
                def _():
                    acc[into, cols] = product

                @pl.when((s > 0) & (s < n - 1))
                def _():
                    acc[into, cols] += product

                @pl.when(s == n - 1)
                def _():
                    if first == 0:

                        @pl.when(j > 0)
                        def _():
                            pltpu.make_async_copy(stage, grads.at[into], store.at[2]).wait()

                    stage[:, cols] = (acc[into, cols] + product).astype(BF16)

            @pl.when(s == n - 1)
            def _():
                pltpu.make_async_copy(stage, grads.at[into], store.at[2]).start()

            return unused

        lax.fori_loop(0, (heads_width + hidden) // heads_width, grad_tile, 0)

        @pl.when(s == n - 1)
        def _():
            line_step(1)
            for copy in outs:
                copy.wait()
            pltpu.make_async_copy(stage, grads.at[pl.ds(0, heads_width)], store.at[2]).wait()

        return unused

    lax.fori_loop(0, n, slot, 0)
    gather_end(gather)
    for (k, _), (_, _, here, bare, _, _, _) in hops.items():
        if k > 1:
            pl.when(here)(bare.wait_send)


def middle(n, in_width, g, down_part, joint, slope, out_weight, down_weight, earlier):
    t, d = g.shape
    rows = n * t
    heads_width, hidden = out_weight.shape[0], down_weight.shape[0]
    anywhere = pl.BlockSpec(memory_space=pl.ANY)
    copies = 2 * (n - 1) + 2 * (n - 2)
    return pl.pallas_call(
        functools.partial(middle_kernel, n, in_width),
        in_specs=[anywhere] * 7,
        out_specs=[anywhere] * 6,
        out_shape=[
            jax.ShapeDtypeStruct(shape, BF16)
            for shape in (
                (rows, d), (rows, heads_width), (rows, in_width + hidden), (heads_width + hidden, d), (t, d), (t, d),
            )
        ],
        scratch_shapes=[
            pltpu.VMEM((heads_width, d), BF16),
            pltpu.VMEM((hidden, d), BF16),
            pltpu.VMEM((heads_width + hidden, d), F32),
            pltpu.VMEM((t, d), BF16),
            pltpu.VMEM((t, heads_width + hidden), BF16),
            pltpu.VMEM((t, hidden), BF16),
            pltpu.VMEM((t, hidden), BF16),
            pltpu.VMEM((t, heads_width), BF16),
            pltpu.VMEM((heads_width, d), BF16),
            pltpu.VMEM((t, d), BF16),
            pltpu.VMEM((n - 2, t, d), BF16),
            pltpu.VMEM((n - 2, t, d), BF16),
        ]
        + [pltpu.SemaphoreType.DMA((copies,))] * 2
        + [pltpu.SemaphoreType.DMA((7,)), pltpu.SemaphoreType.DMA((3,))],
        compiler_params=pltpu.CompilerParams(
            vmem_limit_bytes=60 * 1024 * 1024, collective_id=2, has_side_effects=True
        ),
        cost_estimate=pl.CostEstimate(
            flops=16 * 4 * rows * d * (heads_width + hidden), bytes_accessed=200 * 2**20, transcendentals=0
        ),
        name="middle",
    )(g, down_part, joint, slope, out_weight, down_weight, earlier)


def cross_kernel(heads_tile, x_ref, back_ref, in_ref, up_ref, cross_ref, sums_ref, total_ref, xt_ref):
    width, in_width = back_ref.shape[1], in_ref.shape[1]
    tile = heads_tile

    @pl.when(pl.program_id(0) == 0)
    def _():
        total_ref[...] = jnp.zeros_like(total_ref)
        step = 64

        def body(i, unused):
            rows = back_ref[pl.ds(pl.multiple_of(i * step, step), step), :].astype(F32)
            for r in range(0, step, 8):
                total_ref[...] += rows[r : r + 8]
            return unused

        lax.fori_loop(0, back_ref.shape[0] // step, body, 0)
        total_ref[...] = jnp.broadcast_to(jnp.sum(total_ref[...], axis=0, keepdims=True), total_ref.shape)

    xt_ref[...] = x_ref[...].T
    sums = [jnp.zeros((xt_ref.shape[0], 128), F32) for _ in range(4)]
    for first in range(0, width, tile):
        cols = slice(first, first + tile)
        product = dot(xt_ref[...], back_ref[:, cols])
        cross_ref[:, cols] = product.astype(BF16)
        inside = first < in_width
        wide = (in_ref[:, cols] if inside else up_ref[:, first - in_width : first - in_width + tile]).astype(F32)
        kind = 0 if inside else 2
        for at, term in ((kind, product * wide), (kind + 1, total_ref[0:1, cols] * wide)):
            for lane in range(0, tile, 128):
                sums[at] = sums[at] + term[:, lane : lane + 128]
    lane = lax.broadcasted_iota(jnp.int32, sums[0].shape, 1)
    out = jnp.zeros_like(sums[0])
    for at in range(4):
        out = out + jnp.where(lane == at, jnp.sum(sums[at], axis=1, keepdims=True), 0.0)
    sums_ref[...] = out


def cross_products(heads_tile, x_rows, back, flat_in, up_weight):
    rows, d = x_rows.shape
    width = back.shape[1]
    tile = 512
    once = pl.Buffered(1)
    return pl.pallas_call(
        functools.partial(cross_kernel, heads_tile),
        grid=(d // tile,),
        in_specs=[
            pl.BlockSpec((rows, tile), lambda i: (0, i)),
            pl.BlockSpec((rows, width), lambda i: (0, 0), pipeline_mode=once),
            pl.BlockSpec((tile, flat_in.shape[1]), lambda i: (i, 0)),
            pl.BlockSpec((tile, up_weight.shape[1]), lambda i: (i, 0)),
        ],
        out_specs=[
            pl.BlockSpec((tile, width), lambda i: (i, 0)),
            pl.BlockSpec((tile, 128), lambda i: (i, 0)),
            pl.BlockSpec((8, width), lambda i: (0, 0)),
        ],
        out_shape=[
            jax.ShapeDtypeStruct((d, width), BF16),
            jax.ShapeDtypeStruct((d, 128), F32),
            jax.ShapeDtypeStruct((8, width), F32),
        ],
        scratch_shapes=[pltpu.VMEM((tile, rows), BF16)],
        compiler_params=params(),
        cost_estimate=pl.CostEstimate(
            flops=2 * rows * d * width, bytes_accessed=2 * (rows * d + rows * width + 2 * d * width), transcendentals=0
        ),
        name="cross",
    )(x_rows, back, flat_in, up_weight)


def allowed(j, i, t, start):
    key = j * KBLOCK + lax.broadcasted_iota(jnp.int32, (KBLOCK, t), 0)
    query = i * t + lax.broadcasted_iota(jnp.int32, (1, t), 1)
    return (key >= start) & (key <= query)


def attend_kernel(t, heads, low_ref, qkv_ref, start_ref, held_ref, out_ref, log_ref, vt_ref, acc_ref):
    blocks = qkv_ref.shape[0] // t
    per = t // KBLOCK

    for h in range(heads):
        for c in range(blocks):
            rows = pl.ds(c * t, t)
            vt_ref[h, :, rows] = qkv_ref[rows, (3 * h + 2) * HD : (3 * h + 3) * HD].T

    def query_block(i, unused):
        row = pl.multiple_of(i * t, t)
        where = pl.ds(pl.multiple_of(i * t, t), t)
        start = start_ref[:, where]
        acc_ref[...] = jnp.zeros_like(acc_ref)

        def key_block(j, carried):
            place = pl.multiple_of(j * KBLOCK, KBLOCK)
            mask = allowed(j, i, t, start)
            new = []
            for h in range(heads):
                top, total = carried[h]
                query = qkv_ref[pl.ds(row, t), 3 * h * HD : (3 * h + 1) * HD]
                key = qkv_ref[pl.ds(place, KBLOCK), (3 * h + 1) * HD : (3 * h + 2) * HD]
                s = jnp.where(mask, dot(key, query, NT), NEG_FILL)
                higher = jnp.maximum(top, jnp.max(s, axis=0, keepdims=True))
                p = jnp.exp(s - higher)
                shrink = jnp.exp(top - higher)
                total = total * shrink + jnp.sum(p, axis=0, keepdims=True)
                vt = vt_ref[h, :, pl.ds(place, KBLOCK)]
                acc_ref[h] = acc_ref[h] * shrink + dot(vt, p.astype(BF16))
                new.append((higher, total))
            return tuple(new)

        first = (jnp.full((1, t), 2 * NEG_FILL, F32), jnp.zeros((1, t), F32))
        carried = lax.fori_loop(low_ref[i], (i + 1) * per, key_block, (first,) * heads)
        for h in range(heads):
            top, total = carried[h]
            log_ref[h : h + 1, where] = top + jnp.log(total)
            out_ref[pl.ds(row, t), h * HD : (h + 1) * HD] = (acc_ref[h] / total).T.astype(BF16)
        return unused

    lax.fori_loop(0, blocks, query_block, 0)


def attend(t, low, qkv, start, hidden):
    rows, width = qkv.shape
    heads = width // (3 * HD)
    whole = pl.BlockSpec(memory_space=pltpu.VMEM)
    return pl.pallas_call(
        functools.partial(attend_kernel, t, heads),
        grid=(1,),
        in_specs=[pl.BlockSpec(memory_space=pltpu.SMEM)] + [whole] * 2 + [pl.BlockSpec(memory_space=pl.ANY)],
        out_specs=[pl.BlockSpec((rows, heads * HD), lambda i: (0, 0)), whole],
        out_shape=[
            jax.ShapeDtypeStruct(hidden.shape, BF16),
            jax.ShapeDtypeStruct((heads, rows), F32),
        ],
        scratch_shapes=[pltpu.VMEM((heads, HD, rows), BF16), pltpu.VMEM((heads, HD, t), F32)],
        input_output_aliases={3: 0},
        compiler_params=params(),
        cost_estimate=pl.CostEstimate(
            flops=2 * rows * rows * HD * heads,
            bytes_accessed=2 * rows * width,
            transcendentals=rows * rows * heads // 2,
        ),
        name="attend",
    )(low, qkv, start, hidden)


def attend_back_kernel(
    t, heads, high_ref, qkv_ref, grad_ref, out_ref, log_ref, start_ref, cos_ref, sin_ref, held_ref, after_ref,
    proj_ref, query_grad, delta, key_grad, value_grad,
):
    rows = qkv_ref.shape[0]
    blocks = rows // t
    per = t // KBLOCK
    query_grad[...] = jnp.zeros_like(query_grad)

    def prepare(i, unused):
        row = pl.multiple_of(i * t, t)
        for h in range(heads):
            cols = slice(h * HD, (h + 1) * HD)
            both = grad_ref[pl.ds(row, t), cols].astype(F32) * out_ref[pl.ds(row, t), cols].astype(F32)
            delta[h : h + 1, pl.ds(pl.multiple_of(i * t, t), t)] = jnp.sum(both.T, axis=0, keepdims=True)
        return unused

    lax.fori_loop(0, blocks, prepare, 0)

    def turned_back(grad, place, count):
        cosine, sine = cos_ref[pl.ds(place, count), :], sin_ref[pl.ds(place, count), :]
        return turn(grad[:, :128], cosine, -sine)

    def key_block(j, unused):
        place = pl.multiple_of(j * KBLOCK, KBLOCK)
        key_grad[...] = jnp.zeros_like(key_grad)
        value_grad[...] = jnp.zeros_like(value_grad)

        def query_block(i, unused):
            row = pl.multiple_of(i * t, t)
            where = pl.ds(pl.multiple_of(i * t, t), t)
            mask = allowed(j, i, t, start_ref[:, where])
            for h in range(heads):
                query = qkv_ref[pl.ds(row, t), 3 * h * HD : (3 * h + 1) * HD]
                key = qkv_ref[pl.ds(place, KBLOCK), (3 * h + 1) * HD : (3 * h + 2) * HD]
                value = qkv_ref[pl.ds(place, KBLOCK), (3 * h + 2) * HD : (3 * h + 3) * HD]
                grad = grad_ref[pl.ds(row, t), h * HD : (h + 1) * HD]
                s = dot(key, query, NT) - log_ref[h : h + 1, where]
                p = jnp.exp(jnp.where(mask, s, NEG_FILL))
                p_grad = dot(value, grad, NT)
                value_grad[h] += dot(p.astype(BF16), grad)
                s_grad = (p * (p_grad - delta[h : h + 1, where])).astype(BF16)
                key_grad[h] += dot(s_grad, query)
                query_grad[pl.ds(row, t), h * HD : (h + 1) * HD] += dot(s_grad, key, TN)
            return unused

        lax.fori_loop(j // per, high_ref[j], query_block, 0)
        for h in range(heads):
            base = 3 * h * HD
            grad = key_grad[h]
            proj_ref[pl.ds(place, KBLOCK), base + HD : base + HD + 128] = turned_back(grad, place, KBLOCK).astype(BF16)
            proj_ref[pl.ds(place, KBLOCK), base + HD + 128 : base + 2 * HD] = grad[:, 128:].astype(BF16)
            proj_ref[pl.ds(place, KBLOCK), base + 2 * HD : base + 3 * HD] = value_grad[h].astype(BF16)
        return unused

    lax.fori_loop(0, rows // KBLOCK, key_block, 0)

    def finish(c, unused):
        place = pl.multiple_of(c * t, t)
        for h in range(heads):
            base = 3 * h * HD
            grad = query_grad[pl.ds(place, t), h * HD : (h + 1) * HD] * HD**-0.5
            proj_ref[pl.ds(place, t), base : base + 128] = turned_back(grad, place, t).astype(BF16)
            proj_ref[pl.ds(place, t), base + 128 : base + HD] = grad[:, 128:].astype(BF16)
        return unused

    lax.fori_loop(0, blocks, finish, 0)


def attend_back(t, high, qkv, heads_grad, hidden, logs, start, cosine, sine, buffer, after):
    rows, width = qkv.shape
    heads = width // (3 * HD)
    whole = pl.BlockSpec(memory_space=pltpu.VMEM)
    left = pl.BlockSpec((rows, heads * HD), lambda i: (0, 0))
    return pl.pallas_call(
        functools.partial(attend_back_kernel, t, heads),
        grid=(1,),
        in_specs=[pl.BlockSpec(memory_space=pltpu.SMEM)]
        + [whole, whole, left, whole, whole, whole, whole]
        + [pl.BlockSpec(memory_space=pl.ANY)] * 2,
        out_specs=pl.BlockSpec((rows, width), lambda i: (0, 0)),
        out_shape=jax.ShapeDtypeStruct(buffer.shape, BF16),
        scratch_shapes=[
            pltpu.VMEM((rows, heads * HD), F32),
            pltpu.VMEM((heads, rows), F32),
            pltpu.VMEM((heads, KBLOCK, HD), F32),
            pltpu.VMEM((heads, KBLOCK, HD), F32),
        ],
        input_output_aliases={8: 0},
        compiler_params=params(),
        cost_estimate=pl.CostEstimate(
            flops=5 * rows * rows * HD * heads,
            bytes_accessed=4 * rows * width,
            transcendentals=rows * rows * heads // 2,
        ),
        name="attend_back",
    )(high, qkv, heads_grad, hidden, logs, start, cosine, sine, buffer, after)


def add_rows(into, at, terms, terms_at, count):
    step = 32

    def body(i, unused):
        rows = pl.ds(pl.multiple_of(at + i * step, step), step)
        more = pl.ds(pl.multiple_of(terms_at + i * step, step), step)
        into[rows, :] = (into[rows, :].astype(F32) + terms[more, :].astype(F32)).astype(BF16)
        return unused

    lax.fori_loop(0, count // step, body, 0)


def closing_kernel(n, groups, *refs):
    bits, mp_bits = groups.bit_length() - 1, n.bit_length() - 1
    part_ref, cross_ref, small_ref, norm_ref, summed_ref, small_out = refs[:6]
    come = {1: refs[6], -1: refs[7]}
    keep, core_in = refs[8:10]
    stage_in = [refs[10 : 9 + bits], refs[9 + bits : 8 + 2 * bits]]
    small_in, small_sum, send, recv, load = refs[8 + 2 * bits :]
    z, group = lax.axis_index("mp"), lax.axis_index("dp")
    t = norm_ref.shape[0]
    half = keep.shape[0]
    quarter = half // 2
    ids = pl.DeviceIdType.MESH
    sems = iter(range(send.shape[0]))

    def bit_of(b):
        return lax.rem(group // 2**b, 2)

    def dp_peer(b):
        return {"dp": group + (1 - 2 * bit_of(b)) * 2**b}

    def mp_peer(b):
        return {"mp": z + (1 - 2 * lax.rem(z // 2**b, 2)) * 2**b}

    def remote(source, target, device):
        k = next(sems)
        return pltpu.make_async_remote_copy(source, target, send.at[k], recv.at[k], device, ids)

    barrier = pltpu.get_barrier_semaphore()
    for peer in [dp_peer(b) for b in range(bits)] + [mp_peer(b) for b in range(mp_bits)]:
        pl.semaphore_signal(barrier, inc=1, device_id=peer, device_id_type=ids)

    @pl.when(z + 1 < n)
    def _():
        pl.semaphore_signal(barrier, inc=1, device_id={"mp": z + 1}, device_id_type=ids)

    @pl.when(z >= 1)
    def _():
        pl.semaphore_signal(barrier, inc=1, device_id={"mp": z - 1}, device_id_type=ids)

    ends = jnp.where(z == 0, 1, 0) + jnp.where(z == n - 1, 1, 0)
    pl.semaphore_wait(barrier, bits + mp_bits + 2 - ends)

    small_peers = [dp_peer(b) for b in range(bits)] + [mp_peer(b) for b in range(mp_bits)]
    small_copies = []

    def small_step(i):
        if i == 0:
            small_sum[0] = small_ref[...]
        else:
            small_copies[i - 1].wait_recv()
            if i - 1 < bits:
                total = small_sum[i - 1] + small_in[i - 1]
            else:
                total = small_sum[i - 1]
                small_sum[i, 8:, :] = total[8:]
                total = total[:8] + small_in[i - 1, :8, :]
            small_sum[i, : total.shape[0], :] = total
        if i < len(small_peers):
            small_copies.append(remote(small_sum.at[i], small_in.at[i], small_peers[i]))
            small_copies[i].start()
        else:
            small_out[...] = small_sum[i]

    hops = {}

    def rows_at(distance):
        return pl.multiple_of(jnp.clip(z + distance, 0, n - 1) * t, t)

    def line_step(k):
        for way in (1, -1):
            buffer = come[way].at[k]
            here = (z + k < n) if way == 1 else (z >= k)
            first = (z == 0) if way == 1 else (z == n - 1)
            if k < n - 1:

                @pl.when(here & jnp.logical_not(first))
                def _():
                    hops[k + 1, way][0].wait_recv()
                    add_rows(buffer, 0, part_ref, rows_at(way * k), t) if k > 0 else None

            if k > 0:

                @pl.when(here & first)
                def _():
                    buffer[...] = part_ref[pl.ds(rows_at(way * k), t), :]

                hops[k, way] = (remote(buffer, come[way].at[k - 1], {"mp": z + way}), here)

                @pl.when(here)
                def _():
                    hops[k, way][0].start()

        if k == 0:
            step = 32

            def body(i, unused):
                rows = pl.ds(pl.multiple_of(i * step, step), step)
                total = part_ref[pl.ds(pl.multiple_of(z * t + i * step, step), step), :].astype(F32)
                for way in (1, -1):
                    first = (z == 0) if way == 1 else (z == n - 1)
                    total = total + jnp.where(first, 0.0, come[way][0, rows, :].astype(F32))
                norm_ref[rows, :] = total
                return unused

            lax.fori_loop(0, t // step, body, 0)

    mine, other = bit_of(0) * half, (1 - bit_of(0)) * half
    path = [list(range(1, bits)), list(range(bits - 1, 0, -1))]
    base = [0, quarter]
    size = quarter
    regions = [[], []]
    current = [None, None]

    def first_halving():
        own.wait()
        for p in (0, 1):
            core[p].wait_recv()
            add_rows(keep, p * quarter, core_in, p * quarter, quarter)
            halve(p, 0)

    def halve(p, s):
        b = path[p][s]
        part = quarter // 2 ** (s + 1)
        regions[p].append((base[p], 2 * part))
        away = pl.multiple_of(base[p] + (1 - bit_of(b)) * part, 32)
        current[p] = remote(keep.at[pl.ds(away, part)], stage_in[p][s], dp_peer(b))
        current[p].start()
        started.append(current[p])
        base[p] = base[p] + bit_of(b) * part

    def next_halving(s):
        for p in (0, 1):
            current[p].wait_recv()
            add_rows(keep, base[p], stage_in[p][s - 1], 0, quarter // 2**s)
            if s < bits - 1:
                halve(p, s)
            else:
                count = quarter // 2**s
                place = pl.ds(pl.multiple_of(base[p], 32), count)
                target = summed_ref.at[pl.ds(pl.multiple_of(mine + base[p], 32), count)]
                local = pltpu.make_async_copy(keep.at[place], target, load.at[1 + p])
                local.start()
                current[p] = remote(keep.at[place], target, dp_peer(path[p][s - 1]))
                current[p].start()
                started.append(current[p])
                locals_.append(local)

    def doubling(s):
        for p in (0, 1):
            current[p].wait_recv()
            if s == bits - 2:
                locals_[p].wait()
            at, count = regions[p][s]
            rows = summed_ref.at[pl.ds(pl.multiple_of(mine + at, 32), count)]
            current[p] = remote(rows, rows, dp_peer(path[p][s - 1] if s > 0 else 0))
            current[p].start()
            started.append(current[p])

    started, locals_ = [], []
    core = [
        remote(
            cross_ref.at[pl.ds(pl.multiple_of(other + p * quarter, 32), quarter)],
            core_in.at[pl.ds(p * quarter, quarter)],
            dp_peer(0),
        )
        for p in (0, 1)
    ]
    own = pltpu.make_async_copy(cross_ref.at[pl.ds(pl.multiple_of(mine, 32), half)], keep, load.at[0])
    for copy in core:
        copy.start()
    own.start()
    line_step(n - 1)
    small_step(0)

    sums = [first_halving]
    sums += [functools.partial(next_halving, s) for s in range(1, bits)]
    sums += [functools.partial(doubling, s) for s in range(bits - 2, -1, -1)]
    lines = list(range(n - 2, -1, -1))
    smalls = list(range(1, bits + mp_bits + 1))
    for at, step in enumerate(sums):
        step()
        if at in (0, bits - 1) or at >= bits:
            if lines:
                line_step(lines.pop(0))
        if smalls:
            small_step(smalls.pop(0))
    for k in lines:
        line_step(k)
    for i in smalls:
        small_step(i)
    for p in (0, 1):
        current[p].wait_recv()
    for copy in core + started + small_copies:
        copy.wait_send()
    for copy, here in hops.values():

        @pl.when(here)
        def _():
            copy.wait_send()


def closing_sums(n, groups, part, cross, small):
    rows, d = part.shape
    width = cross.shape[1]
    t, half = rows // n, d // 2
    bits, mp_bits = groups.bit_length() - 1, n.bit_length() - 1
    stages = [pltpu.VMEM((half // 2 // 2**s, width), BF16) for s in range(1, bits)]
    copies = 2 + 2 * (bits - 1) + 2 + 2 * (bits - 1) + 2 * (n - 1) + bits + mp_bits
    whole = pl.BlockSpec(memory_space=pltpu.VMEM)
    return pl.pallas_call(
        functools.partial(closing_kernel, n, groups),
        in_specs=[whole, pl.BlockSpec(memory_space=pl.ANY), whole],
        out_specs=[whole, pl.BlockSpec(memory_space=pl.ANY), whole],
        out_shape=[
            jax.ShapeDtypeStruct((t, d), F32),
            jax.ShapeDtypeStruct((d, width), BF16),
            jax.ShapeDtypeStruct(small.shape, F32),
        ],
        scratch_shapes=[pltpu.VMEM((n, t, d), BF16)] * 2
        + [pltpu.VMEM((half, width), BF16)] * 2
        + stages * 2
        + [pltpu.VMEM((bits + mp_bits,) + small.shape, F32), pltpu.VMEM((bits + mp_bits + 1,) + small.shape, F32)]
        + [pltpu.SemaphoreType.DMA((copies,))] * 2
        + [pltpu.SemaphoreType.DMA((3,))],
        compiler_params=pltpu.CompilerParams(
            vmem_limit_bytes=VMEM_LIMIT, collective_id=0, has_side_effects=True
        ),
        name="closing_sums",
    )(part, cross, small)


def last_hop(to_right, to_left, n):
    right = lax.ppermute(to_right, "mp", [(i, i + 1) for i in range(n - 1)])
    left = lax.ppermute(to_left, "mp", [(i, i - 1) for i in range(1, n)])
    return right.astype(F32) + left.astype(F32)


def exchange(part, own, z, n):
    came = [None] * (2 * n - 1)
    came[n - 1] = own
    for k in range(1, n):
        came[n - 1 - k] = lax.ppermute(part(z + k), "mp", [(i, i + k) for i in range(n - k)])
        came[n - 1 + k] = lax.ppermute(part(z - k), "mp", [(i, i - k) for i in range(k, n)])
    return lax.dynamic_slice_in_dim(jnp.stack(came), n - 1 - z, n, axis=0)


def document_starts(row_lengths, length):
    count = row_lengths.shape[0]
    before = np.tri(count, k=-1, dtype=np.int32)
    starts = jnp.sum(before * row_lengths[None, :], axis=1)
    places = jnp.arange(length, dtype=jnp.int32)
    return jnp.max(jnp.where(starts[None, :] <= places[:, None], starts[None, :], 0), axis=1)


def per_device(
    tokens, seq_lengths, attn_gain, attn_shift, mlp_gain, mlp_shift, in_weight, in_bias, out_weight, out_bias,
    up_weight, up_bias, down_weight, down_bias, cotangent,
):
    n, groups = lax.axis_size("mp"), lax.axis_size("dp")
    z, group = lax.axis_index("mp"), lax.axis_index("dp")
    t, d = tokens.shape[1:]
    length = n * t
    local_heads = in_weight.shape[1]
    in_width, heads_width, hidden = local_heads * 3 * HD, local_heads * HD, up_weight.shape[1]

    own_tokens = tokens[0].astype(F32)
    centred = own_tokens - jnp.mean(own_tokens, axis=-1, keepdims=True)
    spread = lax.rsqrt(jnp.mean(centred * centred, axis=-1, keepdims=True) + NORM_EPS)
    normed = centred * spread
    own_grad = cotangent[0]

    flat_in = lax.optimization_barrier(in_weight.reshape(d, in_width))
    share = out_weight.shape[0] // groups
    out_full = lax.all_gather(
        lax.dynamic_slice_in_dim(out_weight, group * share, share, axis=0), ("mp", "dp"), axis=0, tiled=True
    )

    starts = document_starts(seq_lengths[0], length)
    first_of_block = starts[::t]
    low = first_of_block // KBLOCK
    last_key = (jnp.arange(length // KBLOCK, dtype=jnp.int32) + 1) * KBLOCK - 1
    high = jnp.sum((first_of_block[None, :] <= last_key[:, None]).astype(jnp.int32), axis=1)
    offsets = jnp.arange(length, dtype=jnp.int32) - starts
    inverse = 10000.0 ** (-jnp.arange(0, ROT, 2).astype(F32) / ROT)
    angles = offsets.astype(F32)[:, None] * inverse[None, :]
    cosine, sine = jnp.cos(angles), jnp.sin(angles)
    cosine = jnp.concatenate([cosine, cosine, jnp.ones((length, 128 - ROT), F32)], axis=1)
    sine = jnp.concatenate([-sine, sine, jnp.zeros((length, 128 - ROT), F32)], axis=1)
    start_row = starts[None, :]

    vectors = jnp.stack([attn_gain, attn_shift, mlp_gain, mlp_shift] * 2)
    x_rows, qkv, joint, slope, down_part = opening(
        n, normed.astype(BF16), flat_in, up_weight, down_weight, vectors, in_bias.reshape(1, in_width),
        up_bias[None, :], cosine, sine,
    )
    joint, logs = attend(t, low, qkv, start_row, joint)
    unused, heads_grad, back, out_down_grad, to_right, to_left = middle(
        n, in_width, own_grad, down_part, joint, slope, out_weight, down_weight, out_full
    )

    def rows_for(array):
        def part(position):
            return lax.dynamic_slice_in_dim(array, jnp.clip(position, 0, n - 1) * t, t, axis=0)

        return part

    heads_out = after(joint[:, :heads_width], to_right)
    heads_mine = exchange(rows_for(heads_out), rows_for(heads_out)(z), z, n)
    heads_mine = heads_mine.transpose(1, 0, 2).reshape(t, n * heads_width)
    attn_branch = dot(heads_mine, out_full) + out_bias
    mlp_branch = last_hop(to_right, to_left, n) + rows_for(down_part)(z).astype(F32) + down_bias
    block_out = (own_tokens + attn_branch + mlp_branch).astype(BF16)
    squares = jnp.stack([jnp.sum(attn_branch * attn_branch), jnp.sum(mlp_branch * mlp_branch)])

    back = attend_back(
        t, high, qkv, heads_grad, joint, logs, start_row, cosine, sine, back, out_down_grad
    )
    out_down_grad = lax.psum(out_down_grad, "dp")
    norm_part = (
        dot(back[:, :in_width], flat_in, NT) * attn_gain + dot(back[:, in_width:], up_weight, NT) * mlp_gain
    ).astype(BF16)
    cross, row_sums, total = cross_products(heads_width, x_rows, back, flat_in, up_weight)
    total = total[0]
    attn_sums = row_sums[:, 0:2].T
    mlp_sums = row_sums[:, 2:4].T
    bias_sum = jnp.sum(own_grad.astype(F32), axis=0)
    small = jnp.concatenate(
        [
            attn_sums,
            mlp_sums,
            bias_sum[None],
            jnp.pad(squares, (0, d - 2))[None],
            jnp.zeros((2, d), F32),
            jnp.pad(total[:in_width], (0, d - in_width))[None],
            jnp.pad(total[in_width:], (0, d - hidden))[None],
            jnp.zeros((6, d), F32),
        ]
    )
    norm_grad, cross, small = closing_sums(n, groups, norm_part, cross, small)
    mean_grad = jnp.mean(norm_grad, axis=-1, keepdims=True)
    mean_normed = jnp.mean(norm_grad * normed, axis=-1, keepdims=True)
    tokens_grad = (own_grad.astype(F32) + spread * (norm_grad - mean_grad - normed * mean_normed)).astype(BF16)
    in_total, up_total = small[8, :in_width], small[9, :hidden]
    in_cross = lax.optimization_barrier(cross[:, :in_width].reshape(d, local_heads, 3 * HD))
    grad_in_weight = (
        in_cross.astype(F32) * attn_gain[:, None, None]
        + attn_shift[:, None, None] * in_total.reshape(local_heads, 3 * HD)[None]
    )
    grad_up_weight = cross[:, in_width:].astype(F32) * mlp_gain[:, None] + mlp_shift[:, None] * up_total[None, :]
    element_count = float(groups * n * t * d)
    return (
        block_out[None],
        tokens_grad[None],
        small[0],
        small[1],
        small[2],
        small[3],
        grad_in_weight,
        in_total.reshape(local_heads, 3 * HD),
        out_down_grad[:heads_width].astype(F32),
        small[4],
        grad_up_weight,
        up_total,
        out_down_grad[heads_width:].astype(F32),
        small[4],
        jnp.sqrt(small[5, :2] / element_count),
    )


def solution(mesh):
    rows, weights = P("dp", "mp", None), P(None, "mp", None)
    in_specs = (
        rows, P("dp", None), P(), P(), P(), P(), weights, P("mp", None), P("mp", None), P(),
        P(None, "mp"), P("mp"), P("mp", None), P(), rows,
    )
    out_specs = (
        rows, rows, P(), P(), P(), P(), weights, P("mp", None), P("mp", None), P(),
        P(None, "mp"), P("mp"), P("mp", None), P(), P(),
    )
    return jax.shard_map(per_device, mesh=mesh, in_specs=in_specs, out_specs=out_specs, check_vma=False)
```

```python
import functools

import jax
import jax.numpy as jnp
import numpy as np
from jax import lax
from jax.experimental import pallas as pl
from jax.experimental.pallas import tpu as pltpu
from jax.sharding import PartitionSpec as P

HD = 256
ROT = 64
KBLOCK = 256
NORM_EPS = 1e-05
NEG_FILL = -1000000000.0
VMEM_LIMIT = 56 * 1024 * 1024
BF16 = jnp.bfloat16
F32 = jnp.float32

NT = (((1,), (1,)), ((), ()))
NN = (((1,), (0,)), ((), ()))
TN = (((0,), (0,)), ((), ()))


def dot(a, b, dims=NN):
    return lax.dot_general(a, b, dims, preferred_element_type=F32)


def arrival_order(n):
    return [sorted(range(n), key=lambda p, z=z: (abs(p - z), p)) for z in range(n)]


def params():
    return pltpu.CompilerParams(vmem_limit_bytes=VMEM_LIMIT)


def turn(part, cosine, sine):
    lane = lax.broadcasted_iota(jnp.int32, part.shape, 1)
    swapped = jnp.where(
        lane < ROT // 2,
        pltpu.roll(part, 128 - ROT // 2, 1),
        pltpu.roll(part, ROT // 2, 1),
    )
    return part * cosine + swapped * sine


def after(array, *others):
    anywhere = pl.BlockSpec(memory_space=pl.ANY)
    return pl.pallas_call(
        lambda *refs: None,
        in_specs=[anywhere] * (1 + len(others)),
        out_specs=anywhere,
        out_shape=jax.ShapeDtypeStruct(array.shape, array.dtype),
        input_output_aliases={0: 0},
        name="after",
    )(array, *others)


def across(z, n, values):
    picked = jnp.int32(0)
    for at in range(n):
        picked = picked + jnp.where(z == at, values[at], 0)
    return picked


def greet_line(z, n):
    barrier = pltpu.get_barrier_semaphore()
    for way in (1, -1):

        @pl.when((z + way >= 0) & (z + way < n))
        def _():
            pl.semaphore_signal(barrier, inc=1, device_id={"mp": z + way}, device_id_type=pl.DeviceIdType.MESH)

    pl.semaphore_wait(barrier, 2 - jnp.where(z == 0, 1, 0) - jnp.where(z == n - 1, 1, 0))


def line_gather(z, n, t, own, rows_ref, send, recv):
    hops = {}
    for k in range(1, n):
        for way in (1, -1):
            origin, there = z - way * (k - 1), z + way
            goes = (origin >= 0) & (origin < n) & (there >= 0) & (there < n)
            rows = rows_ref.at[pl.ds(pl.multiple_of(jnp.clip(origin, 0, n - 1) * t, t), t)]
            at = 2 * (k - 1) + (way < 0)
            copy = pltpu.make_async_remote_copy(
                own if k == 1 else rows, rows, send.at[at], recv.at[at], {"mp": there}, pl.DeviceIdType.MESH
            )
            arrives = (z - way * k >= 0) & (z - way * k < n)
            hops[k, way] = (copy, goes, arrives)
    return hops


def gather_step(hops, k):
    for way in (1, -1):
        copy, goes, _ = hops[k, way]
        pl.when(goes)(copy.start)


def gather_wait(hops, k):
    for way in (1, -1):
        copy, _, arrives = hops[k, way]
        pl.when(arrives)(copy.wait_recv)


def gather_end(hops):
    for copy, goes, _ in hops.values():
        pl.when(goes)(copy.wait_send)


def slot_positions(z, n):
    order = arrival_order(n)
    return [across(z, n, [order[zz][s] for zz in range(n)]) for s in range(n)]


def opening_kernel(n, heads, *refs):
    x_ref, in_ref, up_ref, down_ref, vec_ref, in_bias_ref, up_bias_ref, cos_ref, sin_ref = refs[:9]
    x_rows, qkv_ref, joint_ref, slope_ref, part_ref = refs[9:14]
    w_in, w_up, w_down, chunk, attn_in, mlp_in, qkv_out, act_out, slope_out, part_out = refs[14:24]
    send, recv, load, store = refs[24:]
    z = lax.axis_index("mp")
    t, d = x_ref.shape
    in_width, hidden = in_ref.shape[1], up_ref.shape[1]
    greet_line(z, n)

    def rows_of(position):
        return pl.ds(pl.multiple_of(position * t, t), t)

    own = pltpu.make_async_copy(chunk, x_rows.at[rows_of(z)], load.at[0])
    gather = line_gather(z, n, t, x_ref, x_rows, send, recv)
    gather_step(gather, 1)
    weights = [
        pltpu.make_async_copy(source, target, load.at[1 + i])
        for i, (source, target) in enumerate(((in_ref, w_in), (up_ref, w_up), (down_ref, w_down)))
    ]
    for copy in weights:
        copy.start()
    positions = slot_positions(z, n)

    def slot(s, unused):
        position = jnp.int32(0)
        for at in range(n):
            position = position + jnp.where(s == at, positions[at], 0)
        rows = rows_of(position)
        for k in range(1, n):

            @pl.when(s == k)
            def _():
                gather_wait(gather, k)
                if k < n - 1:
                    gather_step(gather, k + 1)

        @pl.when(s == 0)
        def _():
            pltpu.make_async_copy(x_ref, chunk, load.at[4]).start()

        @pl.when(s > 0)
        def _():
            pltpu.make_async_copy(x_rows.at[rows], chunk, load.at[4]).start()

        pltpu.make_async_copy(x_ref, chunk, load.at[4]).wait()
        pl.when(s == 0)(own.start)

        def norm_rows(i, unused):
            block = pl.ds(pl.multiple_of(i * 32, 32), 32)
            x = chunk[block, :].astype(F32)
            attn_in[block, :] = (x * vec_ref[0:1, :] + vec_ref[1:2, :]).astype(BF16)
            mlp_in[block, :] = (x * vec_ref[2:3, :] + vec_ref[3:4, :]).astype(BF16)
            return unused

        lax.fori_loop(0, t // 32, norm_rows, 0)
        outs = [
            pltpu.make_async_copy(qkv_out, qkv_ref.at[rows], store.at[0]),
            pltpu.make_async_copy(act_out, joint_ref.at[rows, pl.ds(heads * HD, hidden)], store.at[1]),
            pltpu.make_async_copy(slope_out, slope_ref.at[rows], store.at[2]),
            pltpu.make_async_copy(part_out, part_ref.at[rows], store.at[3]),
        ]

        @pl.when(s == 0)
        def _():
            weights[0].wait()

        @pl.when(s > 0)
        def _():
            outs[0].wait()

        cosine, sine = cos_ref[rows, :], sin_ref[rows, :]
        for j in range(3 * heads):
            cols = slice(j * HD, (j + 1) * HD)
            acc = dot(attn_in[...], w_in[:, cols]) + in_bias_ref[:, cols]
            if j % 3 < 2:
                scale = HD**-0.5 if j % 3 == 0 else 1.0
                qkv_out[:, cols] = jnp.concatenate(
                    [turn(acc[:, :128], cosine, sine) * scale, acc[:, 128:] * scale], axis=1
                ).astype(BF16)
            else:
                qkv_out[:, cols] = acc.astype(BF16)
        outs[0].start()

        @pl.when(s == 0)
        def _():
            own.wait()
            weights[1].wait()
            weights[2].wait()

        @pl.when(s > 0)
        def _():
            for copy in outs[1:]:
                copy.wait()

        tile = min(512, hidden)
        for first in range(0, hidden, tile):
            cols = slice(first, first + tile)
            u = dot(mlp_in[...], w_up[:, cols]) + up_bias_ref[:, cols]
            below = 0.5 + 0.5 * lax.erf(u * (0.5**0.5))
            act_out[:, cols] = (u * below).astype(BF16)
            density = jnp.exp(u * u * -0.5) * ((2.0 * np.pi) ** -0.5)
            slope_out[:, cols] = (below + u * density).astype(BF16)
        outs[1].start()
        outs[2].start()
        for first in range(0, d, 512):
            cols = slice(first, first + 512)
            part_out[:, cols] = dot(act_out[...], w_down[:, cols]).astype(BF16)
        outs[3].start()

        @pl.when(s == n - 1)
        def _():
            for copy in outs:
                copy.wait()

        return unused

    lax.fori_loop(0, n, slot, 0)
    gather_end(gather)


def opening(n, x, flat_in, up_weight, down_weight, vectors, in_bias, up_bias, cosine, sine):
    t, d = x.shape
    in_width, hidden = flat_in.shape[1], up_weight.shape[1]
    heads, rows = in_width // (3 * HD), n * t
    anywhere, whole = pl.BlockSpec(memory_space=pl.ANY), pl.BlockSpec(memory_space=pltpu.VMEM)
    return pl.pallas_call(
        functools.partial(opening_kernel, n, heads),
        in_specs=[anywhere] * 4 + [whole] * 5,
        out_specs=[anywhere] * 5,
        out_shape=[
            jax.ShapeDtypeStruct(shape, BF16)
            for shape in (
                (rows, d), (rows, in_width), (rows, heads * HD + hidden), (rows, hidden), (rows, d),
            )
        ],
        scratch_shapes=[
            pltpu.VMEM(shape, BF16)
            for shape in (
                (d, in_width), (d, hidden), (hidden, d), (t, d), (t, d), (t, d),
                (t, in_width), (t, hidden), (t, hidden), (t, d),
            )
        ]
        + [pltpu.SemaphoreType.DMA((2 * (n - 1),))] * 2
        + [pltpu.SemaphoreType.DMA((5,)), pltpu.SemaphoreType.DMA((4,))],
        compiler_params=pltpu.CompilerParams(
            vmem_limit_bytes=VMEM_LIMIT, collective_id=1, has_side_effects=True
        ),
        cost_estimate=pl.CostEstimate(
            flops=16 * 2 * rows * d * (in_width + 2 * hidden), bytes_accessed=200 * 2**20, transcendentals=0
        ),
        name="opening",
    )(x, flat_in, up_weight, down_weight, vectors, in_bias, up_bias, cosine, sine)


def middle_kernel(n, in_width, *refs):
    g_ref, part_ref, joint_ref, slope_ref, out_ref, down_ref = refs[:6]
    g_rows, heads_grad, back, grads, to_right, to_left = refs[7:13]
    w_out, w_down, acc, chunk, hidden_in, slope_in, up_out, heads_out, stage, terms = refs[13:23]
    come = {1: refs[23], -1: refs[24]}
    send, recv, load, store = refs[25:]
    z = lax.axis_index("mp")
    t, d = g_ref.shape
    heads_width, hidden = out_ref.shape[0], down_ref.shape[0]
    ids = pl.DeviceIdType.MESH
    greet_line(z, n)

    def rows_of(position):
        return pl.ds(pl.multiple_of(position * t, t), t)

    gather = line_gather(z, n, t, g_ref, g_rows, send, recv)
    gather_step(gather, 1)
    weights = [
        pltpu.make_async_copy(out_ref, w_out, load.at[1]),
        pltpu.make_async_copy(down_ref, w_down, load.at[2]),
    ]
    for copy in weights:
        copy.start()
    positions = slot_positions(z, n)
    hops = {}
    for k in range(1, n):
        for way, target in ((1, to_right), (-1, to_left)):
            here = (z + k < n) if way == 1 else (z >= k)
            first = (z == 0) if way == 1 else (z == n - 1)
            source = part_ref.at[rows_of(jnp.clip(z + way * k, 0, n - 1))]
            buffer = come[way].at[k - 1] if k < n - 1 else None
            if k > 1:
                at = 2 * (n - 1) + 2 * (k - 2) + (way < 0)
                bare, passed = (
                    from_ref
                    and pltpu.make_async_remote_copy(
                        from_ref, come[way].at[k - 2], send.at[at], recv.at[at], {"mp": z + way}, ids
                    )
                    for from_ref in (source, buffer)
                )
            else:
                bare, passed = (pltpu.make_async_copy(from_ref, target, load.at[0]) for from_ref in (terms, buffer))
            terms_copy = pltpu.make_async_copy(source, terms, load.at[3])
            hops[k, way] = (here & first, here & jnp.logical_not(first), here, bare, passed, terms_copy, buffer)

    def line_step(k):
        for way in (1, -1):
            first, later, _, bare, passed, terms_copy, buffer = hops[k, way]

            @pl.when(first)
            def _():
                if k == 1:
                    terms_copy.start()
                    terms_copy.wait()
                bare.start()
                if k == 1:
                    bare.wait()

            if k < n - 1:

                @pl.when(later)
                def _():
                    hops[k + 1, way][3].wait_recv()
                    terms_copy.start()
                    terms_copy.wait()
                    add_rows(buffer, 0, terms, 0, t)
                    passed.start()
                    if k == 1:
                        passed.wait()

    def slot(s, unused):
        position = jnp.int32(0)
        for at in range(n):
            position = position + jnp.where(s == at, positions[at], 0)
        rows = rows_of(position)
        inputs = [
            pltpu.make_async_copy(joint_ref.at[rows], hidden_in, load.at[5]),
            pltpu.make_async_copy(slope_ref.at[rows], slope_in, load.at[6]),
        ]
        for copy in inputs:
            copy.start()
        for k in range(1, n):

            @pl.when(s == k)
            def _():
                gather_wait(gather, k)
                if k < n - 1:
                    gather_step(gather, k + 1)
                    line_step(n - k)

        @pl.when(s == 0)
        def _():
            pltpu.make_async_copy(g_ref, chunk, load.at[4]).start()
            weights[0].wait()
            weights[1].wait()

        @pl.when(s > 0)
        def _():
            pltpu.make_async_copy(g_rows.at[rows], chunk, load.at[4]).start()

        pltpu.make_async_copy(g_ref, chunk, load.at[4]).wait()
        for copy in inputs:
            copy.wait()
        outs = [
            pltpu.make_async_copy(heads_out, heads_grad.at[rows], store.at[0]),
            pltpu.make_async_copy(up_out, back.at[rows, pl.ds(in_width, hidden)], store.at[1]),
        ]

        @pl.when(s > 0)
        def _():
            for copy in outs:
                copy.wait()

        heads_out[...] = dot(chunk[...], w_out[...], NT).astype(BF16)
        outs[0].start()
        tile = min(512, hidden)
        for first in range(0, hidden, tile):
            cols = slice(first, first + tile)
            up_grad = dot(chunk[...], w_down[cols, :], NT) * slope_in[:, cols].astype(F32)
            up_out[:, cols] = up_grad.astype(BF16)
        outs[1].start()

        def grad_tile(j, unused):
            low = pl.multiple_of(j * heads_width, heads_width)
            turned = hidden_in[:, pl.ds(low, heads_width)].T
            into = pl.ds(low, heads_width)
            for first in range(0, d, 512):
                cols = slice(first, first + 512)
                product = dot(turned, chunk[:, cols])

                @pl.when(s == 0)
                def _():
                    acc[into, cols] = product

                @pl.when((s > 0) & (s < n - 1))
                def _():
                    acc[into, cols] += product

                @pl.when(s == n - 1)
                def _():
                    if first == 0:

                        @pl.when(j > 0)
                        def _():
                            pltpu.make_async_copy(stage, grads.at[into], store.at[2]).wait()

                    stage[:, cols] = (acc[into, cols] + product).astype(BF16)

            @pl.when(s == n - 1)
            def _():
                pltpu.make_async_copy(stage, grads.at[into], store.at[2]).start()

            return unused

        lax.fori_loop(0, (heads_width + hidden) // heads_width, grad_tile, 0)

        @pl.when(s == n - 1)
        def _():
            line_step(1)
            for copy in outs:
                copy.wait()
            pltpu.make_async_copy(stage, grads.at[pl.ds(0, heads_width)], store.at[2]).wait()

        return unused

    lax.fori_loop(0, n, slot, 0)
    gather_end(gather)
    for (k, _), (_, _, here, bare, _, _, _) in hops.items():
        if k > 1:
            pl.when(here)(bare.wait_send)


def middle(n, in_width, g, down_part, joint, slope, out_weight, down_weight, earlier):
    t, d = g.shape
    rows = n * t
    heads_width, hidden = out_weight.shape[0], down_weight.shape[0]
    anywhere = pl.BlockSpec(memory_space=pl.ANY)
    copies = 2 * (n - 1) + 2 * (n - 2)
    return pl.pallas_call(
        functools.partial(middle_kernel, n, in_width),
        in_specs=[anywhere] * 7,
        out_specs=[anywhere] * 6,
        out_shape=[
            jax.ShapeDtypeStruct(shape, BF16)
            for shape in (
                (rows, d), (rows, heads_width), (rows, in_width + hidden), (heads_width + hidden, d), (t, d), (t, d),
            )
        ],
        scratch_shapes=[
            pltpu.VMEM((heads_width, d), BF16),
            pltpu.VMEM((hidden, d), BF16),
            pltpu.VMEM((heads_width + hidden, d), F32),
            pltpu.VMEM((t, d), BF16),
            pltpu.VMEM((t, heads_width + hidden), BF16),
            pltpu.VMEM((t, hidden), BF16),
            pltpu.VMEM((t, hidden), BF16),
            pltpu.VMEM((t, heads_width), BF16),
            pltpu.VMEM((heads_width, d), BF16),
            pltpu.VMEM((t, d), BF16),
            pltpu.VMEM((n - 2, t, d), BF16),
            pltpu.VMEM((n - 2, t, d), BF16),
        ]
        + [pltpu.SemaphoreType.DMA((copies,))] * 2
        + [pltpu.SemaphoreType.DMA((7,)), pltpu.SemaphoreType.DMA((3,))],
        compiler_params=pltpu.CompilerParams(
            vmem_limit_bytes=60 * 1024 * 1024, collective_id=2, has_side_effects=True
        ),
        cost_estimate=pl.CostEstimate(
            flops=16 * 4 * rows * d * (heads_width + hidden), bytes_accessed=200 * 2**20, transcendentals=0
        ),
        name="middle",
    )(g, down_part, joint, slope, out_weight, down_weight, earlier)


def cross_kernel(heads_tile, x_ref, back_ref, in_ref, up_ref, cross_ref, sums_ref, total_ref, xt_ref):
    width, in_width = back_ref.shape[1], in_ref.shape[1]
    tile = heads_tile

    @pl.when(pl.program_id(0) == 0)
    def _():
        total_ref[...] = jnp.zeros_like(total_ref)
        step = 64

        def body(i, unused):
            rows = back_ref[pl.ds(pl.multiple_of(i * step, step), step), :].astype(F32)
            for r in range(0, step, 8):
                total_ref[...] += rows[r : r + 8]
            return unused

        lax.fori_loop(0, back_ref.shape[0] // step, body, 0)
        total_ref[...] = jnp.broadcast_to(jnp.sum(total_ref[...], axis=0, keepdims=True), total_ref.shape)

    xt_ref[...] = x_ref[...].T
    sums = [jnp.zeros((xt_ref.shape[0], 128), F32) for _ in range(4)]
    for first in range(0, width, tile):
        cols = slice(first, first + tile)
        product = dot(xt_ref[...], back_ref[:, cols])
        cross_ref[:, cols] = product.astype(BF16)
        inside = first < in_width
        wide = (in_ref[:, cols] if inside else up_ref[:, first - in_width : first - in_width + tile]).astype(F32)
        kind = 0 if inside else 2
        for at, term in ((kind, product * wide), (kind + 1, total_ref[0:1, cols] * wide)):
            for lane in range(0, tile, 128):
                sums[at] = sums[at] + term[:, lane : lane + 128]
    lane = lax.broadcasted_iota(jnp.int32, sums[0].shape, 1)
    out = jnp.zeros_like(sums[0])
    for at in range(4):
        out = out + jnp.where(lane == at, jnp.sum(sums[at], axis=1, keepdims=True), 0.0)
    sums_ref[...] = out


def cross_products(heads_tile, x_rows, back, flat_in, up_weight):
    rows, d = x_rows.shape
    width = back.shape[1]
    tile = 512
    once = pl.Buffered(1)
    return pl.pallas_call(
        functools.partial(cross_kernel, heads_tile),
        grid=(d // tile,),
        in_specs=[
            pl.BlockSpec((rows, tile), lambda i: (0, i)),
            pl.BlockSpec((rows, width), lambda i: (0, 0), pipeline_mode=once),
            pl.BlockSpec((tile, flat_in.shape[1]), lambda i: (i, 0)),
            pl.BlockSpec((tile, up_weight.shape[1]), lambda i: (i, 0)),
        ],
        out_specs=[
            pl.BlockSpec((tile, width), lambda i: (i, 0)),
            pl.BlockSpec((tile, 128), lambda i: (i, 0)),
            pl.BlockSpec((8, width), lambda i: (0, 0)),
        ],
        out_shape=[
            jax.ShapeDtypeStruct((d, width), BF16),
            jax.ShapeDtypeStruct((d, 128), F32),
            jax.ShapeDtypeStruct((8, width), F32),
        ],
        scratch_shapes=[pltpu.VMEM((tile, rows), BF16)],
        compiler_params=params(),
        cost_estimate=pl.CostEstimate(
            flops=2 * rows * d * width, bytes_accessed=2 * (rows * d + rows * width + 2 * d * width), transcendentals=0
        ),
        name="cross",
    )(x_rows, back, flat_in, up_weight)


def allowed(j, i, t, start):
    key = j * KBLOCK + lax.broadcasted_iota(jnp.int32, (KBLOCK, t), 0)
    query = i * t + lax.broadcasted_iota(jnp.int32, (1, t), 1)
    return (key >= start) & (key <= query)


def attend_kernel(t, heads, low_ref, qkv_ref, start_ref, held_ref, out_ref, log_ref, vt_ref, acc_ref):
    blocks = qkv_ref.shape[0] // t
    per = t // KBLOCK

    for h in range(heads):
        for c in range(blocks):
            rows = pl.ds(c * t, t)
            vt_ref[h, :, rows] = qkv_ref[rows, (3 * h + 2) * HD : (3 * h + 3) * HD].T

    def query_block(i, unused):
        row = pl.multiple_of(i * t, t)
        where = pl.ds(pl.multiple_of(i * t, t), t)
        start = start_ref[:, where]
        acc_ref[...] = jnp.zeros_like(acc_ref)

        def key_block(j, carried):
            place = pl.multiple_of(j * KBLOCK, KBLOCK)
            mask = allowed(j, i, t, start)
            new = []
            for h in range(heads):
                top, total = carried[h]
                query = qkv_ref[pl.ds(row, t), 3 * h * HD : (3 * h + 1) * HD]
                key = qkv_ref[pl.ds(place, KBLOCK), (3 * h + 1) * HD : (3 * h + 2) * HD]
                s = jnp.where(mask, dot(key, query, NT), NEG_FILL)
                higher = jnp.maximum(top, jnp.max(s, axis=0, keepdims=True))
                p = jnp.exp(s - higher)
                shrink = jnp.exp(top - higher)
                total = total * shrink + jnp.sum(p, axis=0, keepdims=True)
                vt = vt_ref[h, :, pl.ds(place, KBLOCK)]
                acc_ref[h] = acc_ref[h] * shrink + dot(vt, p.astype(BF16))
                new.append((higher, total))
            return tuple(new)

        first = (jnp.full((1, t), 2 * NEG_FILL, F32), jnp.zeros((1, t), F32))
        carried = lax.fori_loop(low_ref[i], (i + 1) * per, key_block, (first,) * heads)
        for h in range(heads):
            top, total = carried[h]
            log_ref[h : h + 1, where] = top + jnp.log(total)
            out_ref[pl.ds(row, t), h * HD : (h + 1) * HD] = (acc_ref[h] / total).T.astype(BF16)
        return unused

    lax.fori_loop(0, blocks, query_block, 0)


def attend(t, low, qkv, start, hidden):
    rows, width = qkv.shape
    heads = width // (3 * HD)
    whole = pl.BlockSpec(memory_space=pltpu.VMEM)
    return pl.pallas_call(
        functools.partial(attend_kernel, t, heads),
        grid=(1,),
        in_specs=[pl.BlockSpec(memory_space=pltpu.SMEM)] + [whole] * 2 + [pl.BlockSpec(memory_space=pl.ANY)],
        out_specs=[pl.BlockSpec((rows, heads * HD), lambda i: (0, 0)), whole],
        out_shape=[
            jax.ShapeDtypeStruct(hidden.shape, BF16),
            jax.ShapeDtypeStruct((heads, rows), F32),
        ],
        scratch_shapes=[pltpu.VMEM((heads, HD, rows), BF16), pltpu.VMEM((heads, HD, t), F32)],
        input_output_aliases={3: 0},
        compiler_params=params(),
        cost_estimate=pl.CostEstimate(
            flops=2 * rows * rows * HD * heads,
            bytes_accessed=2 * rows * width,
            transcendentals=rows * rows * heads // 2,
        ),
        name="attend",
    )(low, qkv, start, hidden)


def attend_back_kernel(
    t, heads, high_ref, qkv_ref, grad_ref, out_ref, log_ref, start_ref, cos_ref, sin_ref, held_ref, after_ref,
    proj_ref, query_grad, delta, key_grad, value_grad,
):
    rows = qkv_ref.shape[0]
    blocks = rows // t
    per = t // KBLOCK
    query_grad[...] = jnp.zeros_like(query_grad)

    def prepare(i, unused):
        row = pl.multiple_of(i * t, t)
        for h in range(heads):
            cols = slice(h * HD, (h + 1) * HD)
            both = grad_ref[pl.ds(row, t), cols].astype(F32) * out_ref[pl.ds(row, t), cols].astype(F32)
            delta[h : h + 1, pl.ds(pl.multiple_of(i * t, t), t)] = jnp.sum(both.T, axis=0, keepdims=True)
        return unused

    lax.fori_loop(0, blocks, prepare, 0)

    def turned_back(grad, place, count):
        cosine, sine = cos_ref[pl.ds(place, count), :], sin_ref[pl.ds(place, count), :]
        return turn(grad[:, :128], cosine, -sine)

    def key_block(j, unused):
        place = pl.multiple_of(j * KBLOCK, KBLOCK)
        key_grad[...] = jnp.zeros_like(key_grad)
        value_grad[...] = jnp.zeros_like(value_grad)

        def query_block(i, unused):
            row = pl.multiple_of(i * t, t)
            where = pl.ds(pl.multiple_of(i * t, t), t)
            mask = allowed(j, i, t, start_ref[:, where])
            for h in range(heads):
                query = qkv_ref[pl.ds(row, t), 3 * h * HD : (3 * h + 1) * HD]
                key = qkv_ref[pl.ds(place, KBLOCK), (3 * h + 1) * HD : (3 * h + 2) * HD]
                value = qkv_ref[pl.ds(place, KBLOCK), (3 * h + 2) * HD : (3 * h + 3) * HD]
                grad = grad_ref[pl.ds(row, t), h * HD : (h + 1) * HD]
                s = dot(key, query, NT) - log_ref[h : h + 1, where]
                p = jnp.exp(jnp.where(mask, s, NEG_FILL))
                p_grad = dot(value, grad, NT)
                value_grad[h] += dot(p.astype(BF16), grad)
                s_grad = (p * (p_grad - delta[h : h + 1, where])).astype(BF16)
                key_grad[h] += dot(s_grad, query)
                query_grad[pl.ds(row, t), h * HD : (h + 1) * HD] += dot(s_grad, key, TN)
            return unused

        lax.fori_loop(j // per, high_ref[j], query_block, 0)
        for h in range(heads):
            base = 3 * h * HD
            grad = key_grad[h]
            proj_ref[pl.ds(place, KBLOCK), base + HD : base + HD + 128] = turned_back(grad, place, KBLOCK).astype(BF16)
            proj_ref[pl.ds(place, KBLOCK), base + HD + 128 : base + 2 * HD] = grad[:, 128:].astype(BF16)
            proj_ref[pl.ds(place, KBLOCK), base + 2 * HD : base + 3 * HD] = value_grad[h].astype(BF16)
        return unused

    lax.fori_loop(0, rows // KBLOCK, key_block, 0)

    def finish(c, unused):
        place = pl.multiple_of(c * t, t)
        for h in range(heads):
            base = 3 * h * HD
            grad = query_grad[pl.ds(place, t), h * HD : (h + 1) * HD] * HD**-0.5
            proj_ref[pl.ds(place, t), base : base + 128] = turned_back(grad, place, t).astype(BF16)
            proj_ref[pl.ds(place, t), base + 128 : base + HD] = grad[:, 128:].astype(BF16)
        return unused

    lax.fori_loop(0, blocks, finish, 0)


def attend_back(t, high, qkv, heads_grad, hidden, logs, start, cosine, sine, buffer, after):
    rows, width = qkv.shape
    heads = width // (3 * HD)
    whole = pl.BlockSpec(memory_space=pltpu.VMEM)
    left = pl.BlockSpec((rows, heads * HD), lambda i: (0, 0))
    return pl.pallas_call(
        functools.partial(attend_back_kernel, t, heads),
        grid=(1,),
        in_specs=[pl.BlockSpec(memory_space=pltpu.SMEM)]
        + [whole, whole, left, whole, whole, whole, whole]
        + [pl.BlockSpec(memory_space=pl.ANY)] * 2,
        out_specs=pl.BlockSpec((rows, width), lambda i: (0, 0)),
        out_shape=jax.ShapeDtypeStruct(buffer.shape, BF16),
        scratch_shapes=[
            pltpu.VMEM((rows, heads * HD), F32),
            pltpu.VMEM((heads, rows), F32),
            pltpu.VMEM((heads, KBLOCK, HD), F32),
            pltpu.VMEM((heads, KBLOCK, HD), F32),
        ],
        input_output_aliases={8: 0},
        compiler_params=params(),
        cost_estimate=pl.CostEstimate(
            flops=5 * rows * rows * HD * heads,
            bytes_accessed=4 * rows * width,
            transcendentals=rows * rows * heads // 2,
        ),
        name="attend_back",
    )(high, qkv, heads_grad, hidden, logs, start, cosine, sine, buffer, after)


def add_rows(into, at, terms, terms_at, count):
    step = 32

    def body(i, unused):
        rows = pl.ds(pl.multiple_of(at + i * step, step), step)
        more = pl.ds(pl.multiple_of(terms_at + i * step, step), step)
        into[rows, :] = (into[rows, :].astype(F32) + terms[more, :].astype(F32)).astype(BF16)
        return unused

    lax.fori_loop(0, count // step, body, 0)


def closing_kernel(n, groups, *refs):
    bits, mp_bits = groups.bit_length() - 1, n.bit_length() - 1
    back_ref, cross_ref, small_ref, in_ref, up_ref, vec_ref, norm_ref, summed_ref, small_out = refs[:9]
    part = refs[9]
    come = {1: refs[10], -1: refs[11]}
    keep, core_in, chunk, in_tiles, up_tiles = refs[12:17]
    stage_in = [refs[17 : 16 + bits], refs[16 + bits : 15 + 2 * bits]]
    small_in, small_sum, send, recv, load, fetch = refs[15 + 2 * bits :]
    z, group = lax.axis_index("mp"), lax.axis_index("dp")
    t, d = norm_ref.shape
    in_width = in_ref.shape[1]
    half = keep.shape[0]
    quarter = half // 2
    ids = pl.DeviceIdType.MESH
    sems = iter(range(send.shape[0]))

    def bit_of(b):
        return lax.rem(group // 2**b, 2)

    def dp_peer(b):
        return {"dp": group + (1 - 2 * bit_of(b)) * 2**b}

    def mp_peer(b):
        return {"mp": z + (1 - 2 * lax.rem(z // 2**b, 2)) * 2**b}

    def remote(source, target, device):
        k = next(sems)
        return pltpu.make_async_remote_copy(source, target, send.at[k], recv.at[k], device, ids)

    barrier = pltpu.get_barrier_semaphore()
    for peer in [dp_peer(b) for b in range(bits)] + [mp_peer(b) for b in range(mp_bits)]:
        pl.semaphore_signal(barrier, inc=1, device_id=peer, device_id_type=ids)
    for way in (1, -1):

        @pl.when((z + way >= 0) & (z + way < n))
        def _():
            pl.semaphore_signal(barrier, inc=1, device_id={"mp": z + way}, device_id_type=ids)

    ends = jnp.where(z == 0, 1, 0) + jnp.where(z == n - 1, 1, 0)
    pl.semaphore_wait(barrier, bits + mp_bits + 2 - ends)

    mine, other = bit_of(0) * half, (1 - bit_of(0)) * half

    def summed_rows(at, count):
        return summed_ref.at[pl.ds(pl.multiple_of(mine + at, 32), count)]

    core = [
        remote(
            cross_ref.at[pl.ds(pl.multiple_of(other + p * quarter, 32), quarter)],
            core_in.at[pl.ds(p * quarter, quarter)],
            dp_peer(0),
        )
        for p in (0, 1)
    ]
    own = pltpu.make_async_copy(cross_ref.at[pl.ds(pl.multiple_of(mine, 32), half)], keep, load.at[0])
    plans = []
    for p, path in enumerate((list(range(1, bits)), list(range(bits - 1, 0, -1)))):
        at, count = p * quarter, quarter
        halvings, regions = [], []
        for s, b in enumerate(path):
            regions.append((at, count))
            count //= 2
            away = keep.at[pl.ds(pl.multiple_of(at + (1 - bit_of(b)) * count, 32), count)]
            at = at + bit_of(b) * count
            halvings.append((remote(away, stage_in[p][s], dp_peer(b)), at, count))
        place = keep.at[pl.ds(pl.multiple_of(at, 32), count)]
        local = pltpu.make_async_copy(place, summed_rows(at, count), load.at[1 + p])
        doublings = [remote(place, summed_rows(at, count), dp_peer(path[-1]))]
        for s in range(bits - 2, -1, -1):
            rows = summed_rows(*regions[s])
            doublings.append(remote(rows, rows, dp_peer(path[s - 1] if s > 0 else 0)))
        plans.append((halvings, local, doublings))

    def first_halving():
        own.wait()
        for p, (halvings, _, _) in enumerate(plans):
            core[p].wait_recv()
            add_rows(keep, p * quarter, core_in, p * quarter, quarter)
            halvings[0][0].start()

    def next_halving(s):
        for p, (halvings, local, doublings) in enumerate(plans):
            copy, at, count = halvings[s - 1]
            copy.wait_recv()
            add_rows(keep, at, stage_in[p][s - 1], 0, count)
            if s < bits - 1:
                halvings[s][0].start()
            else:
                local.start()
                doublings[0].start()

    def doubling(s):
        for _, local, doublings in plans:
            doublings[s - 1].wait_recv()
            if s == 1:
                local.wait()
            doublings[s].start()

    small_peers = [dp_peer(b) for b in range(bits)] + [mp_peer(b) for b in range(mp_bits)]
    small_copies = [remote(small_sum.at[i], small_in.at[i], peer) for i, peer in enumerate(small_peers)]

    def small_step(i):
        if i == 0:
            small_sum[0] = small_ref[...]
        else:
            small_copies[i - 1].wait_recv()
            if i - 1 < bits:
                small_sum[i] = small_sum[i - 1] + small_in[i - 1]
            else:
                small_sum[i, 8:, :] = small_sum[i - 1, 8:, :]
                small_sum[i, :8, :] = small_sum[i - 1, :8, :] + small_in[i - 1, :8, :]
        if i < len(small_peers):
            small_copies[i].start()
        else:
            small_out[...] = small_sum[i]

    def part_rows(position):
        return pl.ds(pl.multiple_of(jnp.clip(position, 0, n - 1) * t, t), t)

    hops = {}
    for k in range(1, n):
        for way in (1, -1):
            here = (z + k < n) if way == 1 else (z >= k)
            first = (z == 0) if way == 1 else (z == n - 1)
            target, device = come[way].at[k - 1], {"mp": z + way}
            at = next(sems)
            bare, passed = (
                pltpu.make_async_remote_copy(source, target, send.at[at], recv.at[at], device, ids)
                for source in (part.at[part_rows(z + way * k)], come[way].at[min(k, n - 2)])
            )
            hops[k, way] = (here & first, here & jnp.logical_not(first), here, bare, passed)

    def line_step(k):
        for way in (1, -1):
            first, later, _, bare, passed = hops[k, way]
            pl.when(first)(bare.start)
            if k < n - 1:

                @pl.when(later)
                def _():
                    hops[k + 1, way][3].wait_recv()
                    begin = pl.multiple_of(jnp.clip(z + way * k, 0, n - 1) * t, t)
                    add_rows(come[way].at[k], 0, part, begin, t)
                    passed.start()

    def line_end():
        for way, first in ((1, z == 0), (-1, z == n - 1)):
            pl.when(jnp.logical_not(first))(hops[1, way][3].wait_recv)
        step = 32

        def body(i, unused):
            rows = pl.ds(pl.multiple_of(i * step, step), step)
            total = part[pl.ds(pl.multiple_of(z * t + i * step, step), step), :].astype(F32)
            for way, first in ((1, z == 0), (-1, z == n - 1)):
                total = total + jnp.where(first, 0.0, come[way][0, rows, :].astype(F32))
            norm_ref[rows, :] = total
            return unused

        lax.fori_loop(0, t // step, body, 0)

    tile = in_tiles.shape[1]
    tiles = d // tile

    def fetches(j, slot):
        rows = pl.ds(pl.multiple_of(j * tile, tile), tile)
        return (
            pltpu.make_async_copy(in_ref.at[rows], in_tiles.at[slot], fetch.at[slot]),
            pltpu.make_async_copy(up_ref.at[rows], up_tiles.at[slot], fetch.at[2 + slot]),
        )

    def product(position):
        rows = part_rows(position)
        copy = pltpu.make_async_copy(back_ref.at[rows], chunk, load.at[3])
        copy.start()
        copy.wait()

        def one_tile(j, unused):
            slot = lax.rem(j, 2)
            for copy in fetches(j, slot):
                copy.wait()
            for copy in fetches(lax.rem(j + 1, tiles), 1 - slot):
                copy.start()
            cols = pl.ds(pl.multiple_of(j * tile, tile), tile)
            total = dot(chunk[:, :in_width], in_tiles[slot], NT) * vec_ref[0:1, cols]
            total = total + dot(chunk[:, in_width:], up_tiles[slot], NT) * vec_ref[2:3, cols]
            part[rows, cols] = total.astype(BF16)
            return unused

        lax.fori_loop(0, tiles, one_tile, 0)

    for copy in core:
        copy.start()
    own.start()
    for copy in fetches(0, 0):
        copy.start()
    small_step(0)

    def one_product(i, unused):
        distance = (n - 1 - i // 2) * (1 - 2 * lax.rem(i, 2))
        position = z + distance

        @pl.when(i == 2)
        def _():
            line_step(n - 1)
            first_halving()

        @pl.when((position >= 0) & (position < n))
        def _():
            product(position)

        return unused

    lax.fori_loop(0, 2 * (n - 1) + 1, one_product, 0)
    for copy in fetches(0, 0):
        copy.wait()
    sums = [functools.partial(next_halving, s) for s in range(1, bits)]
    sums += [functools.partial(doubling, s) for s in range(1, bits)]
    lines = [functools.partial(line_step, k) for k in range(n - 2, 0, -1)] + [line_end]
    smalls = [functools.partial(small_step, i) for i in range(1, bits + mp_bits + 1)]
    lines.pop(0)()
    for at, step in enumerate(sums):
        step()
        if at >= bits - 2 and lines:
            lines.pop(0)()
        if smalls:
            smalls.pop(0)()
    for step in lines + smalls:
        step()
    for _, _, doublings in plans:
        doublings[-1].wait_recv()
    sent = core + small_copies
    for halvings, _, doublings in plans:
        sent = sent + [copy for copy, _, _ in halvings] + doublings
    for copy in sent:
        copy.wait_send()
    for _, _, here, bare, _ in hops.values():
        pl.when(here)(bare.wait_send)


def closing_sums(n, groups, back, cross, small, flat_in, up_weight, vectors):
    rows, width = back.shape
    d = cross.shape[0]
    t, half, tile = rows // n, d // 2, 256
    bits, mp_bits = groups.bit_length() - 1, n.bit_length() - 1
    stages = [pltpu.VMEM((half // 2 // 2**s, width), BF16) for s in range(1, bits)]
    copies = 2 + 4 * (bits - 1) + 2 + 2 * (n - 1) + bits + mp_bits
    whole, anywhere = pl.BlockSpec(memory_space=pltpu.VMEM), pl.BlockSpec(memory_space=pl.ANY)
    return pl.pallas_call(
        functools.partial(closing_kernel, n, groups),
        in_specs=[anywhere, anywhere, whole, anywhere, anywhere, whole],
        out_specs=[whole, anywhere, whole],
        out_shape=[
            jax.ShapeDtypeStruct((t, d), F32),
            jax.ShapeDtypeStruct((d, width), BF16),
            jax.ShapeDtypeStruct(small.shape, F32),
        ],
        scratch_shapes=[pltpu.VMEM((rows, d), BF16)]
        + [pltpu.VMEM((n - 1, t, d), BF16)] * 2
        + [pltpu.VMEM((half, width), BF16)] * 2
        + [pltpu.VMEM((t, width), BF16)]
        + [pltpu.VMEM((2, tile, flat_in.shape[1]), BF16), pltpu.VMEM((2, tile, up_weight.shape[1]), BF16)]
        + stages * 2
        + [pltpu.VMEM((bits + mp_bits,) + small.shape, F32), pltpu.VMEM((bits + mp_bits + 1,) + small.shape, F32)]
        + [pltpu.SemaphoreType.DMA((copies,))] * 2
        + [pltpu.SemaphoreType.DMA((4,))] * 2,
        compiler_params=pltpu.CompilerParams(
            vmem_limit_bytes=60 * 1024 * 1024, collective_id=0, has_side_effects=True
        ),
        name="closing_sums",
    )(back, cross, small, flat_in, up_weight, vectors)


def finish_kernel(heads, summed_ref, total_ref, vec_ref, in_ref, up_ref):
    in_width = heads * 3 * HD
    for h in range(heads):
        cols = slice(h * 3 * HD, (h + 1) * 3 * HD)
        wide = summed_ref[:, cols].astype(F32)
        in_ref[:, h, :] = wide * vec_ref[:, 0:1] + vec_ref[:, 1:2] * total_ref[0:1, cols]
    wide = summed_ref[:, in_width:].astype(F32)
    up_ref[...] = wide * vec_ref[:, 2:3] + vec_ref[:, 3:4] * total_ref[0:1, in_width:]


def finish(heads, summed, totals, vectors):
    d, width = summed.shape
    in_width = heads * 3 * HD
    block = 256
    return pl.pallas_call(
        functools.partial(finish_kernel, heads),
        grid=(d // block,),
        in_specs=[
            pl.BlockSpec((block, width), lambda i: (i, 0)),
            pl.BlockSpec((8, width), lambda i: (0, 0)),
            pl.BlockSpec((block, 8), lambda i: (i, 0)),
        ],
        out_specs=[
            pl.BlockSpec((block, heads, 3 * HD), lambda i: (i, 0, 0)),
            pl.BlockSpec((block, width - in_width), lambda i: (i, 0)),
        ],
        out_shape=[
            jax.ShapeDtypeStruct((d, heads, 3 * HD), F32),
            jax.ShapeDtypeStruct((d, width - in_width), F32),
        ],
        compiler_params=params(),
        name="finish",
    )(summed, totals, vectors)


def last_hop(to_right, to_left, n):
    right = lax.ppermute(to_right, "mp", [(i, i + 1) for i in range(n - 1)])
    left = lax.ppermute(to_left, "mp", [(i, i - 1) for i in range(1, n)])
    return right.astype(F32) + left.astype(F32)


def document_starts(row_lengths, length):
    count = row_lengths.shape[0]
    before = np.tri(count, k=-1, dtype=np.int32)
    starts = jnp.sum(before * row_lengths[None, :], axis=1)
    places = jnp.arange(length, dtype=jnp.int32)
    return jnp.max(jnp.where(starts[None, :] <= places[:, None], starts[None, :], 0), axis=1)


def per_device(
    tokens, seq_lengths, attn_gain, attn_shift, mlp_gain, mlp_shift, in_weight, in_bias, out_weight, out_bias,
    up_weight, up_bias, down_weight, down_bias, cotangent,
):
    n, groups = lax.axis_size("mp"), lax.axis_size("dp")
    z, group = lax.axis_index("mp"), lax.axis_index("dp")
    t, d = tokens.shape[1:]
    length = n * t
    local_heads = in_weight.shape[1]
    in_width, heads_width, hidden = local_heads * 3 * HD, local_heads * HD, up_weight.shape[1]

    own_tokens = tokens[0].astype(F32)
    centred = own_tokens - jnp.mean(own_tokens, axis=-1, keepdims=True)
    spread = lax.rsqrt(jnp.mean(centred * centred, axis=-1, keepdims=True) + NORM_EPS)
    normed = centred * spread
    own_grad = cotangent[0]

    flat_in = lax.optimization_barrier(in_weight.reshape(d, in_width))
    share = out_weight.shape[0] // groups
    out_share = lax.dynamic_slice_in_dim(out_weight, group * share, share, axis=0)

    starts = document_starts(seq_lengths[0], length)
    first_of_block = starts[::t]
    low = first_of_block // KBLOCK
    last_key = (jnp.arange(length // KBLOCK, dtype=jnp.int32) + 1) * KBLOCK - 1
    high = jnp.sum((first_of_block[None, :] <= last_key[:, None]).astype(jnp.int32), axis=1)
    offsets = jnp.arange(length, dtype=jnp.int32) - starts
    inverse = 10000.0 ** (-jnp.arange(0, ROT, 2).astype(F32) / ROT)
    angles = offsets.astype(F32)[:, None] * inverse[None, :]
    cosine, sine = jnp.cos(angles), jnp.sin(angles)
    cosine = jnp.concatenate([cosine, cosine, jnp.ones((length, 128 - ROT), F32)], axis=1)
    sine = jnp.concatenate([-sine, sine, jnp.zeros((length, 128 - ROT), F32)], axis=1)
    start_row = starts[None, :]

    vectors = jnp.stack([attn_gain, attn_shift, mlp_gain, mlp_shift] * 2)
    x_rows, qkv, joint, slope, down_part = opening(
        n, normed.astype(BF16), flat_in, up_weight, down_weight, vectors, in_bias.reshape(1, in_width),
        up_bias[None, :], cosine, sine,
    )
    out_part = lax.all_gather(after(out_share, slope), "mp", axis=0, tiled=True)
    out_full = lax.all_gather(out_part, "dp", axis=0, tiled=True)
    joint, logs = attend(t, low, qkv, start_row, joint)
    unused, heads_grad, back, out_down_grad, to_right, to_left = middle(
        n, in_width, own_grad, down_part, joint, slope, out_weight, down_weight, out_part
    )

    def rows_for(array):
        def part(position):
            return lax.dynamic_slice_in_dim(array, jnp.clip(position, 0, n - 1) * t, t, axis=0)

        return part

    back = attend_back(
        t, high, qkv, heads_grad, joint, logs, start_row, cosine, sine, back, out_full
    )
    heads_out = after(joint[:, :heads_width], back)
    heads_mine = lax.all_to_all(heads_out.reshape(n, t, heads_width), "mp", 0, 0)
    heads_mine = heads_mine.reshape(n, t, groups, share).transpose(1, 2, 0, 3).reshape(t, n * heads_width)
    attn_branch = dot(heads_mine, out_full) + out_bias
    mlp_branch = last_hop(to_right, to_left, n) + rows_for(down_part)(z).astype(F32) + down_bias
    block_out = (own_tokens + attn_branch + mlp_branch).astype(BF16)
    squares = jnp.stack([jnp.sum(attn_branch * attn_branch), jnp.sum(mlp_branch * mlp_branch)])

    out_down_grad = lax.psum(after(out_down_grad, out_full), "dp")
    cross, row_sums, total = cross_products(heads_width, x_rows, back, flat_in, up_weight)
    total = total[0]
    attn_sums = row_sums[:, 0:2].T
    mlp_sums = row_sums[:, 2:4].T
    bias_sum = jnp.sum(own_grad.astype(F32), axis=0)
    small = jnp.concatenate(
        [
            attn_sums,
            mlp_sums,
            bias_sum[None],
            jnp.pad(squares, (0, d - 2))[None],
            jnp.zeros((2, d), F32),
            jnp.pad(total[:in_width], (0, d - in_width))[None],
            jnp.pad(total[in_width:], (0, d - hidden))[None],
            jnp.zeros((6, d), F32),
        ]
    )
    norm_grad, cross, small = closing_sums(n, groups, back, cross, small, flat_in, up_weight, vectors)
    mean_grad = jnp.mean(norm_grad, axis=-1, keepdims=True)
    mean_normed = jnp.mean(norm_grad * normed, axis=-1, keepdims=True)
    tokens_grad = (own_grad.astype(F32) + spread * (norm_grad - mean_grad - normed * mean_normed)).astype(BF16)
    in_total, up_total = small[8, :in_width], small[9, :hidden]
    totals = jnp.broadcast_to(jnp.concatenate([in_total, up_total])[None], (8, in_width + hidden))
    grad_in_weight, grad_up_weight = finish(local_heads, cross, totals, vectors.T)
    element_count = float(groups * n * t * d)
    return (
        block_out[None],
        tokens_grad[None],
        small[0],
        small[1],
        small[2],
        small[3],
        grad_in_weight,
        in_total.reshape(local_heads, 3 * HD),
        out_down_grad[:heads_width].astype(F32),
        small[4],
        grad_up_weight,
        up_total,
        out_down_grad[heads_width:].astype(F32),
        small[4],
        jnp.sqrt(small[5, :2] / element_count),
    )


def solution(mesh):
    rows, weights = P("dp", "mp", None), P(None, "mp", None)
    in_specs = (
        rows, P("dp", None), P(), P(), P(), P(), weights, P("mp", None), P("mp", None), P(),
        P(None, "mp"), P("mp"), P("mp", None), P(), rows,
    )
    out_specs = (
        rows, rows, P(), P(), P(), P(), weights, P("mp", None), P("mp", None), P(),
        P(None, "mp"), P("mp"), P("mp", None), P(), P(),
    )
    return jax.shard_map(per_device, mesh=mesh, in_specs=in_specs, out_specs=out_specs, check_vma=False)
```

```python
import functools

import jax
import jax.numpy as jnp
import numpy as np
from jax import lax
from jax.experimental import pallas as pl
from jax.experimental.pallas import tpu as pltpu
from jax.sharding import PartitionSpec as P

HD = 256
ROT = 64
KBLOCK = 256
NORM_EPS = 1e-05
NEG_FILL = -1000000000.0
VMEM_LIMIT = 56 * 1024 * 1024
BF16 = jnp.bfloat16
F32 = jnp.float32

NT = (((1,), (1,)), ((), ()))
NN = (((1,), (0,)), ((), ()))
TN = (((0,), (0,)), ((), ()))


def dot(a, b, dims=NN):
    return lax.dot_general(a, b, dims, preferred_element_type=F32)


def arrival_order(n):
    return [sorted(range(n), key=lambda p, z=z: (abs(p - z), p)) for z in range(n)]


def params():
    return pltpu.CompilerParams(vmem_limit_bytes=VMEM_LIMIT)


def turn(part, cosine, sine):
    lane = lax.broadcasted_iota(jnp.int32, part.shape, 1)
    swapped = jnp.where(
        lane < ROT // 2,
        pltpu.roll(part, 128 - ROT // 2, 1),
        pltpu.roll(part, ROT // 2, 1),
    )
    return part * cosine + swapped * sine


def after(array, *others):
    anywhere = pl.BlockSpec(memory_space=pl.ANY)
    return pl.pallas_call(
        lambda *refs: None,
        in_specs=[anywhere] * (1 + len(others)),
        out_specs=anywhere,
        out_shape=jax.ShapeDtypeStruct(array.shape, array.dtype),
        input_output_aliases={0: 0},
        name="after",
    )(array, *others)


def across(z, n, values):
    picked = jnp.int32(0)
    for at in range(n):
        picked = picked + jnp.where(z == at, values[at], 0)
    return picked


def greet_line(z, n):
    barrier = pltpu.get_barrier_semaphore()
    for way in (1, -1):

        @pl.when((z + way >= 0) & (z + way < n))
        def _():
            pl.semaphore_signal(barrier, inc=1, device_id={"mp": z + way}, device_id_type=pl.DeviceIdType.MESH)

    pl.semaphore_wait(barrier, 2 - jnp.where(z == 0, 1, 0) - jnp.where(z == n - 1, 1, 0))


def line_gather(z, n, t, own, rows_ref, send, recv):
    hops = {}
    for k in range(1, n):
        for way in (1, -1):
            origin, there = z - way * (k - 1), z + way
            goes = (origin >= 0) & (origin < n) & (there >= 0) & (there < n)
            rows = rows_ref.at[pl.ds(pl.multiple_of(jnp.clip(origin, 0, n - 1) * t, t), t)]
            at = 2 * (k - 1) + (way < 0)
            copy = pltpu.make_async_remote_copy(
                own if k == 1 else rows, rows, send.at[at], recv.at[at], {"mp": there}, pl.DeviceIdType.MESH
            )
            arrives = (z - way * k >= 0) & (z - way * k < n)
            hops[k, way] = (copy, goes, arrives)
    return hops


def gather_step(hops, k):
    for way in (1, -1):
        copy, goes, _ = hops[k, way]
        pl.when(goes)(copy.start)


def gather_wait(hops, k):
    for way in (1, -1):
        copy, _, arrives = hops[k, way]
        pl.when(arrives)(copy.wait_recv)


def gather_end(hops):
    for copy, goes, _ in hops.values():
        pl.when(goes)(copy.wait_send)


def slot_positions(z, n):
    order = arrival_order(n)
    return [across(z, n, [order[zz][s] for zz in range(n)]) for s in range(n)]


def opening_kernel(n, heads, *refs):
    x_ref, in_ref, up_ref, down_ref, vec_ref, in_bias_ref, up_bias_ref, cos_ref, sin_ref = refs[:9]
    x_rows, qkv_ref, joint_ref, slope_ref, part_ref = refs[9:14]
    w_in, w_up, w_down, chunk, attn_in, mlp_in, qkv_out, act_out, slope_out, part_out = refs[14:24]
    send, recv, load, store = refs[24:]
    z = lax.axis_index("mp")
    t, d = x_ref.shape
    in_width, hidden = in_ref.shape[1], up_ref.shape[1]
    greet_line(z, n)

    def rows_of(position):
        return pl.ds(pl.multiple_of(position * t, t), t)

    own = pltpu.make_async_copy(chunk, x_rows.at[rows_of(z)], load.at[0])
    gather = line_gather(z, n, t, x_ref, x_rows, send, recv)
    gather_step(gather, 1)
    weights = [
        pltpu.make_async_copy(source, target, load.at[1 + i])
        for i, (source, target) in enumerate(((in_ref, w_in), (up_ref, w_up), (down_ref, w_down)))
    ]
    for copy in weights:
        copy.start()
    positions = slot_positions(z, n)

    def slot(s, unused):
        position = jnp.int32(0)
        for at in range(n):
            position = position + jnp.where(s == at, positions[at], 0)
        rows = rows_of(position)
        for k in range(1, n):

            @pl.when(s == k)
            def _():
                gather_wait(gather, k)
                if k < n - 1:
                    gather_step(gather, k + 1)

        @pl.when(s == 0)
        def _():
            pltpu.make_async_copy(x_ref, chunk, load.at[4]).start()

        @pl.when(s > 0)
        def _():
            pltpu.make_async_copy(x_rows.at[rows], chunk, load.at[4]).start()

        pltpu.make_async_copy(x_ref, chunk, load.at[4]).wait()
        pl.when(s == 0)(own.start)

        def norm_rows(i, unused):
            block = pl.ds(pl.multiple_of(i * 32, 32), 32)
            x = chunk[block, :].astype(F32)
            attn_in[block, :] = (x * vec_ref[0:1, :] + vec_ref[1:2, :]).astype(BF16)
            mlp_in[block, :] = (x * vec_ref[2:3, :] + vec_ref[3:4, :]).astype(BF16)
            return unused

        lax.fori_loop(0, t // 32, norm_rows, 0)
        outs = [
            pltpu.make_async_copy(qkv_out, qkv_ref.at[rows], store.at[0]),
            pltpu.make_async_copy(act_out, joint_ref.at[rows, pl.ds(heads * HD, hidden)], store.at[1]),
            pltpu.make_async_copy(slope_out, slope_ref.at[rows], store.at[2]),
            pltpu.make_async_copy(part_out, part_ref.at[rows], store.at[3]),
        ]

        @pl.when(s == 0)
        def _():
            weights[0].wait()

        @pl.when(s > 0)
        def _():
            outs[0].wait()

        cosine, sine = cos_ref[rows, :], sin_ref[rows, :]
        for j in range(3 * heads):
            cols = slice(j * HD, (j + 1) * HD)
            acc = dot(attn_in[...], w_in[:, cols]) + in_bias_ref[:, cols]
            if j % 3 < 2:
                scale = HD**-0.5 if j % 3 == 0 else 1.0
                qkv_out[:, cols] = jnp.concatenate(
                    [turn(acc[:, :128], cosine, sine) * scale, acc[:, 128:] * scale], axis=1
                ).astype(BF16)
            else:
                qkv_out[:, cols] = acc.astype(BF16)
        outs[0].start()

        @pl.when(s == 0)
        def _():
            own.wait()
            weights[1].wait()
            weights[2].wait()

        @pl.when(s > 0)
        def _():
            for copy in outs[1:]:
                copy.wait()

        tile = min(512, hidden)
        for first in range(0, hidden, tile):
            cols = slice(first, first + tile)
            u = dot(mlp_in[...], w_up[:, cols]) + up_bias_ref[:, cols]
            below = 0.5 + 0.5 * lax.erf(u * (0.5**0.5))
            act_out[:, cols] = (u * below).astype(BF16)
            density = jnp.exp(u * u * -0.5) * ((2.0 * np.pi) ** -0.5)
            slope_out[:, cols] = (below + u * density).astype(BF16)
        outs[1].start()
        outs[2].start()
        for first in range(0, d, 512):
            cols = slice(first, first + 512)
            part_out[:, cols] = dot(act_out[...], w_down[:, cols]).astype(BF16)
        outs[3].start()

        @pl.when(s == n - 1)
        def _():
            for copy in outs:
                copy.wait()

        return unused

    lax.fori_loop(0, n, slot, 0)
    gather_end(gather)


def opening(n, x, flat_in, up_weight, down_weight, vectors, in_bias, up_bias, cosine, sine):
    t, d = x.shape
    in_width, hidden = flat_in.shape[1], up_weight.shape[1]
    heads, rows = in_width // (3 * HD), n * t
    anywhere, whole = pl.BlockSpec(memory_space=pl.ANY), pl.BlockSpec(memory_space=pltpu.VMEM)
    return pl.pallas_call(
        functools.partial(opening_kernel, n, heads),
        in_specs=[anywhere] * 4 + [whole] * 5,
        out_specs=[anywhere] * 5,
        out_shape=[
            jax.ShapeDtypeStruct(shape, BF16)
            for shape in (
                (rows, d), (rows, in_width), (rows, heads * HD + hidden), (rows, hidden), (rows, d),
            )
        ],
        scratch_shapes=[
            pltpu.VMEM(shape, BF16)
            for shape in (
                (d, in_width), (d, hidden), (hidden, d), (t, d), (t, d), (t, d),
                (t, in_width), (t, hidden), (t, hidden), (t, d),
            )
        ]
        + [pltpu.SemaphoreType.DMA((2 * (n - 1),))] * 2
        + [pltpu.SemaphoreType.DMA((5,)), pltpu.SemaphoreType.DMA((4,))],
        compiler_params=pltpu.CompilerParams(
            vmem_limit_bytes=VMEM_LIMIT, collective_id=1, has_side_effects=True
        ),
        cost_estimate=pl.CostEstimate(
            flops=16 * 2 * rows * d * (in_width + 2 * hidden), bytes_accessed=200 * 2**20, transcendentals=0
        ),
        name="opening",
    )(x, flat_in, up_weight, down_weight, vectors, in_bias, up_bias, cosine, sine)


def middle_kernel(n, in_width, *refs):
    g_ref, part_ref, joint_ref, slope_ref, out_ref, down_ref = refs[:6]
    g_rows, heads_grad, back, grads, to_right, to_left = refs[7:13]
    w_out, w_down, acc, chunk, hidden_in, slope_in, up_out, heads_out, stage, terms = refs[13:23]
    come = {1: refs[23], -1: refs[24]}
    send, recv, load, store = refs[25:]
    z = lax.axis_index("mp")
    t, d = g_ref.shape
    heads_width, hidden = out_ref.shape[0], down_ref.shape[0]
    ids = pl.DeviceIdType.MESH
    greet_line(z, n)

    def rows_of(position):
        return pl.ds(pl.multiple_of(position * t, t), t)

    gather = line_gather(z, n, t, g_ref, g_rows, send, recv)
    gather_step(gather, 1)
    weights = [
        pltpu.make_async_copy(out_ref, w_out, load.at[1]),
        pltpu.make_async_copy(down_ref, w_down, load.at[2]),
    ]
    for copy in weights:
        copy.start()
    positions = slot_positions(z, n)
    hops = {}
    for k in range(1, n):
        for way, target in ((1, to_right), (-1, to_left)):
            here = (z + k < n) if way == 1 else (z >= k)
            first = (z == 0) if way == 1 else (z == n - 1)
            source = part_ref.at[rows_of(jnp.clip(z + way * k, 0, n - 1))]
            buffer = come[way].at[k - 1] if k < n - 1 else None
            if k > 1:
                at = 2 * (n - 1) + 2 * (k - 2) + (way < 0)
                bare, passed = (
                    from_ref
                    and pltpu.make_async_remote_copy(
                        from_ref, come[way].at[k - 2], send.at[at], recv.at[at], {"mp": z + way}, ids
                    )
                    for from_ref in (source, buffer)
                )
            else:
                bare, passed = (pltpu.make_async_copy(from_ref, target, load.at[0]) for from_ref in (terms, buffer))
            terms_copy = pltpu.make_async_copy(source, terms, load.at[3])
            hops[k, way] = (here & first, here & jnp.logical_not(first), here, bare, passed, terms_copy, buffer)

    def line_step(k):
        for way in (1, -1):
            first, later, _, bare, passed, terms_copy, buffer = hops[k, way]

            @pl.when(first)
            def _():
                if k == 1:
                    terms_copy.start()
                    terms_copy.wait()
                bare.start()
                if k == 1:
                    bare.wait()

            if k < n - 1:

                @pl.when(later)
                def _():
                    hops[k + 1, way][3].wait_recv()
                    terms_copy.start()
                    terms_copy.wait()
                    add_rows(buffer, 0, terms, 0, t)
                    passed.start()
                    if k == 1:
                        passed.wait()

    def slot(s, unused):
        position = jnp.int32(0)
        for at in range(n):
            position = position + jnp.where(s == at, positions[at], 0)
        rows = rows_of(position)
        inputs = [
            pltpu.make_async_copy(joint_ref.at[rows], hidden_in, load.at[5]),
            pltpu.make_async_copy(slope_ref.at[rows], slope_in, load.at[6]),
        ]
        for copy in inputs:
            copy.start()
        for k in range(1, n):

            @pl.when(s == k)
            def _():
                gather_wait(gather, k)
                if k < n - 1:
                    gather_step(gather, k + 1)
                    line_step(n - k)

        @pl.when(s == 0)
        def _():
            pltpu.make_async_copy(g_ref, chunk, load.at[4]).start()
            weights[0].wait()
            weights[1].wait()

        @pl.when(s > 0)
        def _():
            pltpu.make_async_copy(g_rows.at[rows], chunk, load.at[4]).start()

        pltpu.make_async_copy(g_ref, chunk, load.at[4]).wait()
        for copy in inputs:
            copy.wait()
        outs = [
            pltpu.make_async_copy(heads_out, heads_grad.at[rows], store.at[0]),
            pltpu.make_async_copy(up_out, back.at[rows, pl.ds(in_width, hidden)], store.at[1]),
        ]

        @pl.when(s > 0)
        def _():
            for copy in outs:
                copy.wait()

        heads_out[...] = dot(chunk[...], w_out[...], NT).astype(BF16)
        outs[0].start()
        tile = min(512, hidden)
        for first in range(0, hidden, tile):
            cols = slice(first, first + tile)
            up_grad = dot(chunk[...], w_down[cols, :], NT) * slope_in[:, cols].astype(F32)
            up_out[:, cols] = up_grad.astype(BF16)
        outs[1].start()

        def grad_tile(j, unused):
            low = pl.multiple_of(j * heads_width, heads_width)
            turned = hidden_in[:, pl.ds(low, heads_width)].T
            into = pl.ds(low, heads_width)
            for first in range(0, d, 512):
                cols = slice(first, first + 512)
                product = dot(turned, chunk[:, cols])

                @pl.when(s == 0)
                def _():
                    acc[into, cols] = product

                @pl.when((s > 0) & (s < n - 1))
                def _():
                    acc[into, cols] += product

                @pl.when(s == n - 1)
                def _():
                    if first == 0:

                        @pl.when(j > 0)
                        def _():
                            pltpu.make_async_copy(stage, grads.at[into], store.at[2]).wait()

                    stage[:, cols] = (acc[into, cols] + product).astype(BF16)

            @pl.when(s == n - 1)
            def _():
                pltpu.make_async_copy(stage, grads.at[into], store.at[2]).start()

            return unused

        lax.fori_loop(0, (heads_width + hidden) // heads_width, grad_tile, 0)

        @pl.when(s == n - 1)
        def _():
            line_step(1)
            for copy in outs:
                copy.wait()
            pltpu.make_async_copy(stage, grads.at[pl.ds(0, heads_width)], store.at[2]).wait()

        return unused

    lax.fori_loop(0, n, slot, 0)
    gather_end(gather)
    for (k, _), (_, _, here, bare, _, _, _) in hops.items():
        if k > 1:
            pl.when(here)(bare.wait_send)


def middle(n, in_width, g, down_part, joint, slope, out_weight, down_weight, earlier):
    t, d = g.shape
    rows = n * t
    heads_width, hidden = out_weight.shape[0], down_weight.shape[0]
    anywhere = pl.BlockSpec(memory_space=pl.ANY)
    copies = 2 * (n - 1) + 2 * (n - 2)
    return pl.pallas_call(
        functools.partial(middle_kernel, n, in_width),
        in_specs=[anywhere] * 7,
        out_specs=[anywhere] * 6,
        out_shape=[
            jax.ShapeDtypeStruct(shape, BF16)
            for shape in (
                (rows, d), (rows, heads_width), (rows, in_width + hidden), (heads_width + hidden, d), (t, d), (t, d),
            )
        ],
        scratch_shapes=[
            pltpu.VMEM((heads_width, d), BF16),
            pltpu.VMEM((hidden, d), BF16),
            pltpu.VMEM((heads_width + hidden, d), F32),
            pltpu.VMEM((t, d), BF16),
            pltpu.VMEM((t, heads_width + hidden), BF16),
            pltpu.VMEM((t, hidden), BF16),
            pltpu.VMEM((t, hidden), BF16),
            pltpu.VMEM((t, heads_width), BF16),
            pltpu.VMEM((heads_width, d), BF16),
            pltpu.VMEM((t, d), BF16),
            pltpu.VMEM((n - 2, t, d), BF16),
            pltpu.VMEM((n - 2, t, d), BF16),
        ]
        + [pltpu.SemaphoreType.DMA((copies,))] * 2
        + [pltpu.SemaphoreType.DMA((7,)), pltpu.SemaphoreType.DMA((3,))],
        compiler_params=pltpu.CompilerParams(
            vmem_limit_bytes=60 * 1024 * 1024, collective_id=2, has_side_effects=True
        ),
        cost_estimate=pl.CostEstimate(
            flops=16 * 4 * rows * d * (heads_width + hidden), bytes_accessed=200 * 2**20, transcendentals=0
        ),
        name="middle",
    )(g, down_part, joint, slope, out_weight, down_weight, earlier)


def cross_kernel(heads_tile, x_ref, back_ref, in_ref, up_ref, earlier_ref, cross_ref, sums_ref, total_ref, xt_ref):
    width, in_width = back_ref.shape[1], in_ref.shape[1]
    tile = heads_tile

    @pl.when(pl.program_id(0) == 0)
    def _():
        total_ref[...] = jnp.zeros_like(total_ref)
        step = 64

        def body(i, unused):
            rows = back_ref[pl.ds(pl.multiple_of(i * step, step), step), :].astype(F32)
            for r in range(0, step, 8):
                total_ref[...] += rows[r : r + 8]
            return unused

        lax.fori_loop(0, back_ref.shape[0] // step, body, 0)
        total_ref[...] = jnp.broadcast_to(jnp.sum(total_ref[...], axis=0, keepdims=True), total_ref.shape)

    xt_ref[...] = x_ref[...].T
    sums = [jnp.zeros((xt_ref.shape[0], 128), F32) for _ in range(4)]
    for first in range(0, width, tile):
        cols = slice(first, first + tile)
        product = dot(xt_ref[...], back_ref[:, cols])
        cross_ref[:, cols] = product.astype(BF16)
        inside = first < in_width
        wide = (in_ref[:, cols] if inside else up_ref[:, first - in_width : first - in_width + tile]).astype(F32)
        kind = 0 if inside else 2
        for at, term in ((kind, product * wide), (kind + 1, total_ref[0:1, cols] * wide)):
            for lane in range(0, tile, 128):
                sums[at] = sums[at] + term[:, lane : lane + 128]
    lane = lax.broadcasted_iota(jnp.int32, sums[0].shape, 1)
    out = jnp.zeros_like(sums[0])
    for at in range(4):
        out = out + jnp.where(lane == at, jnp.sum(sums[at], axis=1, keepdims=True), 0.0)
    sums_ref[...] = out


def cross_products(heads_tile, x_rows, back, flat_in, up_weight, earlier):
    rows, d = x_rows.shape
    width = back.shape[1]
    tile = 512
    once = pl.Buffered(1)
    return pl.pallas_call(
        functools.partial(cross_kernel, heads_tile),
        grid=(d // tile,),
        in_specs=[
            pl.BlockSpec((rows, tile), lambda i: (0, i)),
            pl.BlockSpec((rows, width), lambda i: (0, 0), pipeline_mode=once),
            pl.BlockSpec((tile, flat_in.shape[1]), lambda i: (i, 0)),
            pl.BlockSpec((tile, up_weight.shape[1]), lambda i: (i, 0)),
            pl.BlockSpec(memory_space=pl.ANY),
        ],
        out_specs=[
            pl.BlockSpec((tile, width), lambda i: (i, 0)),
            pl.BlockSpec((tile, 128), lambda i: (i, 0)),
            pl.BlockSpec((8, width), lambda i: (0, 0)),
        ],
        out_shape=[
            jax.ShapeDtypeStruct((d, width), BF16),
            jax.ShapeDtypeStruct((d, 128), F32),
            jax.ShapeDtypeStruct((8, width), F32),
        ],
        scratch_shapes=[pltpu.VMEM((tile, rows), BF16)],
        compiler_params=params(),
        cost_estimate=pl.CostEstimate(
            flops=2 * rows * d * width, bytes_accessed=2 * (rows * d + rows * width + 2 * d * width), transcendentals=0
        ),
        name="cross",
    )(x_rows, back, flat_in, up_weight, earlier)


def allowed(j, i, t, start):
    key = j * KBLOCK + lax.broadcasted_iota(jnp.int32, (KBLOCK, t), 0)
    query = i * t + lax.broadcasted_iota(jnp.int32, (1, t), 1)
    return (key >= start) & (key <= query)


def attend_kernel(t, heads, low_ref, qkv_ref, start_ref, held_ref, out_ref, log_ref, vt_ref, acc_ref):
    blocks = qkv_ref.shape[0] // t
    per = t // KBLOCK

    for h in range(heads):
        for c in range(blocks):
            rows = pl.ds(c * t, t)
            vt_ref[h, :, rows] = qkv_ref[rows, (3 * h + 2) * HD : (3 * h + 3) * HD].T

    def query_block(i, unused):
        row = pl.multiple_of(i * t, t)
        where = pl.ds(pl.multiple_of(i * t, t), t)
        start = start_ref[:, where]
        acc_ref[...] = jnp.zeros_like(acc_ref)

        def key_block(j, carried):
            place = pl.multiple_of(j * KBLOCK, KBLOCK)
            mask = allowed(j, i, t, start)
            new = []
            for h in range(heads):
                top, total = carried[h]
                query = qkv_ref[pl.ds(row, t), 3 * h * HD : (3 * h + 1) * HD]
                key = qkv_ref[pl.ds(place, KBLOCK), (3 * h + 1) * HD : (3 * h + 2) * HD]
                s = jnp.where(mask, dot(key, query, NT), NEG_FILL)
                higher = jnp.maximum(top, jnp.max(s, axis=0, keepdims=True))
                p = jnp.exp(s - higher)
                shrink = jnp.exp(top - higher)
                total = total * shrink + jnp.sum(p, axis=0, keepdims=True)
                vt = vt_ref[h, :, pl.ds(place, KBLOCK)]
                acc_ref[h] = acc_ref[h] * shrink + dot(vt, p.astype(BF16))
                new.append((higher, total))
            return tuple(new)

        first = (jnp.full((1, t), 2 * NEG_FILL, F32), jnp.zeros((1, t), F32))
        carried = lax.fori_loop(low_ref[i], (i + 1) * per, key_block, (first,) * heads)
        for h in range(heads):
            top, total = carried[h]
            log_ref[h : h + 1, where] = top + jnp.log(total)
            out_ref[pl.ds(row, t), h * HD : (h + 1) * HD] = (acc_ref[h] / total).T.astype(BF16)
        return unused

    lax.fori_loop(0, blocks, query_block, 0)


def attend(t, low, qkv, start, hidden):
    rows, width = qkv.shape
    heads = width // (3 * HD)
    whole = pl.BlockSpec(memory_space=pltpu.VMEM)
    return pl.pallas_call(
        functools.partial(attend_kernel, t, heads),
        grid=(1,),
        in_specs=[pl.BlockSpec(memory_space=pltpu.SMEM)] + [whole] * 2 + [pl.BlockSpec(memory_space=pl.ANY)],
        out_specs=[pl.BlockSpec((rows, heads * HD), lambda i: (0, 0)), whole],
        out_shape=[
            jax.ShapeDtypeStruct(hidden.shape, BF16),
            jax.ShapeDtypeStruct((heads, rows), F32),
        ],
        scratch_shapes=[pltpu.VMEM((heads, HD, rows), BF16), pltpu.VMEM((heads, HD, t), F32)],
        input_output_aliases={3: 0},
        compiler_params=params(),
        cost_estimate=pl.CostEstimate(
            flops=2 * rows * rows * HD * heads,
            bytes_accessed=2 * rows * width,
            transcendentals=rows * rows * heads // 2,
        ),
        name="attend",
    )(low, qkv, start, hidden)


def attend_back_kernel(
    t, heads, high_ref, qkv_ref, grad_ref, out_ref, log_ref, start_ref, cos_ref, sin_ref, held_ref, after_ref,
    proj_ref, query_grad, delta, key_grad, value_grad,
):
    rows = qkv_ref.shape[0]
    blocks = rows // t
    per = t // KBLOCK
    query_grad[...] = jnp.zeros_like(query_grad)

    def prepare(i, unused):
        row = pl.multiple_of(i * t, t)
        for h in range(heads):
            cols = slice(h * HD, (h + 1) * HD)
            both = grad_ref[pl.ds(row, t), cols].astype(F32) * out_ref[pl.ds(row, t), cols].astype(F32)
            delta[h : h + 1, pl.ds(pl.multiple_of(i * t, t), t)] = jnp.sum(both.T, axis=0, keepdims=True)
        return unused

    lax.fori_loop(0, blocks, prepare, 0)

    def turned_back(grad, place, count):
        cosine, sine = cos_ref[pl.ds(place, count), :], sin_ref[pl.ds(place, count), :]
        return turn(grad[:, :128], cosine, -sine)

    def key_block(j, unused):
        place = pl.multiple_of(j * KBLOCK, KBLOCK)
        key_grad[...] = jnp.zeros_like(key_grad)
        value_grad[...] = jnp.zeros_like(value_grad)

        def query_block(i, unused):
            row = pl.multiple_of(i * t, t)
            where = pl.ds(pl.multiple_of(i * t, t), t)
            mask = allowed(j, i, t, start_ref[:, where])
            for h in range(heads):
                query = qkv_ref[pl.ds(row, t), 3 * h * HD : (3 * h + 1) * HD]
                key = qkv_ref[pl.ds(place, KBLOCK), (3 * h + 1) * HD : (3 * h + 2) * HD]
                value = qkv_ref[pl.ds(place, KBLOCK), (3 * h + 2) * HD : (3 * h + 3) * HD]
                grad = grad_ref[pl.ds(row, t), h * HD : (h + 1) * HD]
                s = dot(key, query, NT) - log_ref[h : h + 1, where]
                p = jnp.exp(jnp.where(mask, s, NEG_FILL))
                p_grad = dot(value, grad, NT)
                value_grad[h] += dot(p.astype(BF16), grad)
                s_grad = (p * (p_grad - delta[h : h + 1, where])).astype(BF16)
                key_grad[h] += dot(s_grad, query)
                query_grad[pl.ds(row, t), h * HD : (h + 1) * HD] += dot(s_grad, key, TN)
            return unused

        lax.fori_loop(j // per, high_ref[j], query_block, 0)
        for h in range(heads):
            base = 3 * h * HD
            grad = key_grad[h]
            proj_ref[pl.ds(place, KBLOCK), base + HD : base + HD + 128] = turned_back(grad, place, KBLOCK).astype(BF16)
            proj_ref[pl.ds(place, KBLOCK), base + HD + 128 : base + 2 * HD] = grad[:, 128:].astype(BF16)
            proj_ref[pl.ds(place, KBLOCK), base + 2 * HD : base + 3 * HD] = value_grad[h].astype(BF16)
        return unused

    lax.fori_loop(0, rows // KBLOCK, key_block, 0)

    def finish(c, unused):
        place = pl.multiple_of(c * t, t)
        for h in range(heads):
            base = 3 * h * HD
            grad = query_grad[pl.ds(place, t), h * HD : (h + 1) * HD] * HD**-0.5
            proj_ref[pl.ds(place, t), base : base + 128] = turned_back(grad, place, t).astype(BF16)
            proj_ref[pl.ds(place, t), base + 128 : base + HD] = grad[:, 128:].astype(BF16)
        return unused

    lax.fori_loop(0, blocks, finish, 0)


def attend_back(t, high, qkv, heads_grad, hidden, logs, start, cosine, sine, buffer, after):
    rows, width = qkv.shape
    heads = width // (3 * HD)
    whole = pl.BlockSpec(memory_space=pltpu.VMEM)
    left = pl.BlockSpec((rows, heads * HD), lambda i: (0, 0))
    return pl.pallas_call(
        functools.partial(attend_back_kernel, t, heads),
        grid=(1,),
        in_specs=[pl.BlockSpec(memory_space=pltpu.SMEM)]
        + [whole, whole, left, whole, whole, whole, whole]
        + [pl.BlockSpec(memory_space=pl.ANY)] * 2,
        out_specs=pl.BlockSpec((rows, width), lambda i: (0, 0)),
        out_shape=jax.ShapeDtypeStruct(buffer.shape, BF16),
        scratch_shapes=[
            pltpu.VMEM((rows, heads * HD), F32),
            pltpu.VMEM((heads, rows), F32),
            pltpu.VMEM((heads, KBLOCK, HD), F32),
            pltpu.VMEM((heads, KBLOCK, HD), F32),
        ],
        input_output_aliases={8: 0},
        compiler_params=params(),
        cost_estimate=pl.CostEstimate(
            flops=5 * rows * rows * HD * heads,
            bytes_accessed=4 * rows * width,
            transcendentals=rows * rows * heads // 2,
        ),
        name="attend_back",
    )(high, qkv, heads_grad, hidden, logs, start, cosine, sine, buffer, after)


def add_rows(into, at, terms, terms_at, count):
    step = 32

    def body(i, unused):
        rows = pl.ds(pl.multiple_of(at + i * step, step), step)
        more = pl.ds(pl.multiple_of(terms_at + i * step, step), step)
        into[rows, :] = (into[rows, :].astype(F32) + terms[more, :].astype(F32)).astype(BF16)
        return unused

    lax.fori_loop(0, count // step, body, 0)


def closing_kernel(n, groups, *refs):
    bits, mp_bits = groups.bit_length() - 1, n.bit_length() - 1
    refs = refs[:6] + refs[7:]
    back_ref, cross_ref, small_ref, in_ref, up_ref, vec_ref, norm_ref, summed_ref, small_out = refs[:9]
    part = refs[9]
    come = {1: refs[10], -1: refs[11]}
    keep, core_in, chunk, in_tiles, up_tiles = refs[12:17]
    stage_in = [refs[17 : 16 + bits], refs[16 + bits : 15 + 2 * bits]]
    small_in, small_sum, send, recv, load, fetch = refs[15 + 2 * bits :]
    z, group = lax.axis_index("mp"), lax.axis_index("dp")
    t, d = norm_ref.shape
    in_width = in_ref.shape[1]
    half = keep.shape[0]
    quarter = half // 2
    ids = pl.DeviceIdType.MESH
    sems = iter(range(send.shape[0]))

    def bit_of(b):
        return lax.rem(group // 2**b, 2)

    def dp_peer(b):
        return {"dp": group + (1 - 2 * bit_of(b)) * 2**b}

    def mp_peer(b):
        return {"mp": z + (1 - 2 * lax.rem(z // 2**b, 2)) * 2**b}

    def remote(source, target, device):
        k = next(sems)
        return pltpu.make_async_remote_copy(source, target, send.at[k], recv.at[k], device, ids)

    barrier = pltpu.get_barrier_semaphore()
    for peer in [dp_peer(b) for b in range(bits)] + [mp_peer(b) for b in range(mp_bits)]:
        pl.semaphore_signal(barrier, inc=1, device_id=peer, device_id_type=ids)
    for way in (1, -1):

        @pl.when((z + way >= 0) & (z + way < n))
        def _():
            pl.semaphore_signal(barrier, inc=1, device_id={"mp": z + way}, device_id_type=ids)

    ends = jnp.where(z == 0, 1, 0) + jnp.where(z == n - 1, 1, 0)
    pl.semaphore_wait(barrier, bits + mp_bits + 2 - ends)

    mine, other = bit_of(0) * half, (1 - bit_of(0)) * half

    def summed_rows(at, count):
        return summed_ref.at[pl.ds(pl.multiple_of(mine + at, 32), count)]

    core = [
        remote(
            cross_ref.at[pl.ds(pl.multiple_of(other + p * quarter, 32), quarter)],
            core_in.at[pl.ds(p * quarter, quarter)],
            dp_peer(0),
        )
        for p in (0, 1)
    ]
    own = pltpu.make_async_copy(cross_ref.at[pl.ds(pl.multiple_of(mine, 32), half)], keep, load.at[0])
    plans = []
    for p, path in enumerate((list(range(1, bits)), list(range(bits - 1, 0, -1)))):
        at, count = p * quarter, quarter
        halvings, regions = [], []
        for s, b in enumerate(path):
            regions.append((at, count))
            count //= 2
            away = keep.at[pl.ds(pl.multiple_of(at + (1 - bit_of(b)) * count, 32), count)]
            at = at + bit_of(b) * count
            halvings.append((remote(away, stage_in[p][s], dp_peer(b)), at, count))
        place = keep.at[pl.ds(pl.multiple_of(at, 32), count)]
        local = pltpu.make_async_copy(place, summed_rows(at, count), load.at[1 + p])
        doublings = [remote(place, summed_rows(at, count), dp_peer(path[-1]))]
        for s in range(bits - 2, -1, -1):
            rows = summed_rows(*regions[s])
            doublings.append(remote(rows, rows, dp_peer(path[s - 1] if s > 0 else 0)))
        plans.append((halvings, local, doublings))

    def first_halving():
        own.wait()
        for p, (halvings, _, _) in enumerate(plans):
            core[p].wait_recv()
            add_rows(keep, p * quarter, core_in, p * quarter, quarter)
            halvings[0][0].start()

    def next_halving(s):
        for p, (halvings, local, doublings) in enumerate(plans):
            copy, at, count = halvings[s - 1]
            copy.wait_recv()
            add_rows(keep, at, stage_in[p][s - 1], 0, count)
            if s < bits - 1:
                halvings[s][0].start()
            else:
                local.start()
                doublings[0].start()

    def doubling(s):
        for _, local, doublings in plans:
            doublings[s - 1].wait_recv()
            if s == 1:
                local.wait()
            doublings[s].start()

    small_peers = [dp_peer(b) for b in range(bits)] + [mp_peer(b) for b in range(mp_bits)]
    small_copies = [remote(small_sum.at[i], small_in.at[i], peer) for i, peer in enumerate(small_peers)]

    def small_step(i):
        if i == 0:
            small_sum[0] = small_ref[...]
        else:
            small_copies[i - 1].wait_recv()
            if i - 1 < bits:
                small_sum[i] = small_sum[i - 1] + small_in[i - 1]
            else:
                small_sum[i, 8:, :] = small_sum[i - 1, 8:, :]
                small_sum[i, :8, :] = small_sum[i - 1, :8, :] + small_in[i - 1, :8, :]
        if i < len(small_peers):
            small_copies[i].start()
        else:
            small_out[...] = small_sum[i]

    def part_rows(position):
        return pl.ds(pl.multiple_of(jnp.clip(position, 0, n - 1) * t, t), t)

    hops = {}
    for k in range(1, n):
        for way in (1, -1):
            here = (z + k < n) if way == 1 else (z >= k)
            first = (z == 0) if way == 1 else (z == n - 1)
            target, device = come[way].at[k - 1], {"mp": z + way}
            at = next(sems)
            bare, passed = (
                pltpu.make_async_remote_copy(source, target, send.at[at], recv.at[at], device, ids)
                for source in (part.at[part_rows(z + way * k)], come[way].at[min(k, n - 2)])
            )
            hops[k, way] = (here & first, here & jnp.logical_not(first), here, bare, passed)

    def line_step(k):
        for way in (1, -1):
            first, later, _, bare, passed = hops[k, way]
            pl.when(first)(bare.start)
            if k < n - 1:

                @pl.when(later)
                def _():
                    hops[k + 1, way][3].wait_recv()
                    begin = pl.multiple_of(jnp.clip(z + way * k, 0, n - 1) * t, t)
                    add_rows(come[way].at[k], 0, part, begin, t)
                    passed.start()

    def line_end():
        for way, first in ((1, z == 0), (-1, z == n - 1)):
            pl.when(jnp.logical_not(first))(hops[1, way][3].wait_recv)
        step = 32

        def body(i, unused):
            rows = pl.ds(pl.multiple_of(i * step, step), step)
            total = part[pl.ds(pl.multiple_of(z * t + i * step, step), step), :].astype(F32)
            for way, first in ((1, z == 0), (-1, z == n - 1)):
                total = total + jnp.where(first, 0.0, come[way][0, rows, :].astype(F32))
            norm_ref[rows, :] = total
            return unused

        lax.fori_loop(0, t // step, body, 0)

    tile = in_tiles.shape[1]
    tiles = d // tile

    def fetches(j, slot):
        rows = pl.ds(pl.multiple_of(j * tile, tile), tile)
        return (
            pltpu.make_async_copy(in_ref.at[rows], in_tiles.at[slot], fetch.at[slot]),
            pltpu.make_async_copy(up_ref.at[rows], up_tiles.at[slot], fetch.at[2 + slot]),
        )

    def product(position):
        rows = part_rows(position)
        copy = pltpu.make_async_copy(back_ref.at[rows], chunk, load.at[3])
        copy.start()
        copy.wait()

        def one_tile(j, unused):
            slot = lax.rem(j, 2)
            for copy in fetches(j, slot):
                copy.wait()
            for copy in fetches(lax.rem(j + 1, tiles), 1 - slot):
                copy.start()
            cols = pl.ds(pl.multiple_of(j * tile, tile), tile)
            total = dot(chunk[:, :in_width], in_tiles[slot], NT) * vec_ref[0:1, cols]
            total = total + dot(chunk[:, in_width:], up_tiles[slot], NT) * vec_ref[2:3, cols]
            part[rows, cols] = total.astype(BF16)
            return unused

        lax.fori_loop(0, tiles, one_tile, 0)

    for copy in core:
        copy.start()
    own.start()
    for copy in fetches(0, 0):
        copy.start()
    small_step(0)

    def one_product(i, unused):
        distance = (n - 1 - i // 2) * (1 - 2 * lax.rem(i, 2))
        position = z + distance

        @pl.when(i == 2)
        def _():
            line_step(n - 1)
            first_halving()

        @pl.when((position >= 0) & (position < n))
        def _():
            product(position)

        return unused

    lax.fori_loop(0, 2 * (n - 1) + 1, one_product, 0)
    for copy in fetches(0, 0):
        copy.wait()
    sums = [functools.partial(next_halving, s) for s in range(1, bits)]
    sums += [functools.partial(doubling, s) for s in range(1, bits)]
    lines = [functools.partial(line_step, k) for k in range(n - 2, 0, -1)] + [line_end]
    smalls = [functools.partial(small_step, i) for i in range(1, bits + mp_bits + 1)]
    lines.pop(0)()
    for at, step in enumerate(sums):
        step()
        if at >= bits - 2 and lines:
            lines.pop(0)()
        if smalls:
            smalls.pop(0)()
    for step in lines + smalls:
        step()
    for _, _, doublings in plans:
        doublings[-1].wait_recv()
    sent = core + small_copies
    for halvings, _, doublings in plans:
        sent = sent + [copy for copy, _, _ in halvings] + doublings
    for copy in sent:
        copy.wait_send()
    for _, _, here, bare, _ in hops.values():
        pl.when(here)(bare.wait_send)


def closing_sums(n, groups, back, cross, small, flat_in, up_weight, vectors, earlier):
    rows, width = back.shape
    d = cross.shape[0]
    t, half, tile = rows // n, d // 2, 256
    bits, mp_bits = groups.bit_length() - 1, n.bit_length() - 1
    stages = [pltpu.VMEM((half // 2 // 2**s, width), BF16) for s in range(1, bits)]
    copies = 2 + 4 * (bits - 1) + 2 + 2 * (n - 1) + bits + mp_bits
    whole, anywhere = pl.BlockSpec(memory_space=pltpu.VMEM), pl.BlockSpec(memory_space=pl.ANY)
    return pl.pallas_call(
        functools.partial(closing_kernel, n, groups),
        in_specs=[anywhere, anywhere, whole, anywhere, anywhere, whole, anywhere],
        out_specs=[whole, anywhere, whole],
        out_shape=[
            jax.ShapeDtypeStruct((t, d), F32),
            jax.ShapeDtypeStruct((d, width), BF16),
            jax.ShapeDtypeStruct(small.shape, F32),
        ],
        scratch_shapes=[pltpu.VMEM((rows, d), BF16)]
        + [pltpu.VMEM((n - 1, t, d), BF16)] * 2
        + [pltpu.VMEM((half, width), BF16)] * 2
        + [pltpu.VMEM((t, width), BF16)]
        + [pltpu.VMEM((2, tile, flat_in.shape[1]), BF16), pltpu.VMEM((2, tile, up_weight.shape[1]), BF16)]
        + stages * 2
        + [pltpu.VMEM((bits + mp_bits,) + small.shape, F32), pltpu.VMEM((bits + mp_bits + 1,) + small.shape, F32)]
        + [pltpu.SemaphoreType.DMA((copies,))] * 2
        + [pltpu.SemaphoreType.DMA((4,))] * 2,
        compiler_params=pltpu.CompilerParams(
            vmem_limit_bytes=60 * 1024 * 1024, collective_id=0, has_side_effects=True
        ),
        name="closing_sums",
    )(back, cross, small, flat_in, up_weight, vectors, earlier)


def finish_kernel(heads, summed_ref, total_ref, vec_ref, out_low, down_low, in_ref, up_ref, out_ref, down_ref):
    in_width = heads * 3 * HD
    for h in range(heads):
        cols = slice(h * 3 * HD, (h + 1) * 3 * HD)
        wide = summed_ref[:, cols].astype(F32)
        in_ref[:, h, :] = wide * vec_ref[:, 0:1] + vec_ref[:, 1:2] * total_ref[0:1, cols]
    wide = summed_ref[:, in_width:].astype(F32)
    up_ref[...] = wide * vec_ref[:, 2:3] + vec_ref[:, 3:4] * total_ref[0:1, in_width:]
    out_ref[...] = out_low[...].astype(F32)
    down_ref[...] = down_low[...].astype(F32)


def finish(heads, summed, totals, vectors, out_down):
    d, width = summed.shape
    in_width, heads_width = heads * 3 * HD, heads * HD
    block = 256
    steps = d // block
    hidden = width - in_width
    out_rows, down_rows = heads_width // steps, hidden // steps
    first = heads_width // down_rows
    return pl.pallas_call(
        functools.partial(finish_kernel, heads),
        grid=(d // block,),
        in_specs=[
            pl.BlockSpec((block, width), lambda i: (i, 0)),
            pl.BlockSpec((8, width), lambda i: (0, 0)),
            pl.BlockSpec((block, 8), lambda i: (i, 0)),
            pl.BlockSpec((out_rows, d), lambda i: (i, 0)),
            pl.BlockSpec((down_rows, d), lambda i: (first + i, 0)),
        ],
        out_specs=[
            pl.BlockSpec((block, heads, 3 * HD), lambda i: (i, 0, 0)),
            pl.BlockSpec((block, hidden), lambda i: (i, 0)),
            pl.BlockSpec((out_rows, d), lambda i: (i, 0)),
            pl.BlockSpec((down_rows, d), lambda i: (i, 0)),
        ],
        out_shape=[
            jax.ShapeDtypeStruct((d, heads, 3 * HD), F32),
            jax.ShapeDtypeStruct((d, hidden), F32),
            jax.ShapeDtypeStruct((heads_width, d), F32),
            jax.ShapeDtypeStruct((hidden, d), F32),
        ],
        compiler_params=params(),
        name="finish",
    )(summed, totals, vectors, out_down, out_down)


def last_hop(to_right, to_left, n):
    right = lax.ppermute(to_right, "mp", [(i, i + 1) for i in range(n - 1)])
    left = lax.ppermute(to_left, "mp", [(i, i - 1) for i in range(1, n)])
    return right, left


def document_starts(row_lengths, length):
    count = row_lengths.shape[0]
    before = np.tri(count, k=-1, dtype=np.int32)
    starts = jnp.sum(before * row_lengths[None, :], axis=1)
    places = jnp.arange(length, dtype=jnp.int32)
    return jnp.max(jnp.where(starts[None, :] <= places[:, None], starts[None, :], 0), axis=1)


def per_device(
    tokens, seq_lengths, attn_gain, attn_shift, mlp_gain, mlp_shift, in_weight, in_bias, out_weight, out_bias,
    up_weight, up_bias, down_weight, down_bias, cotangent,
):
    n, groups = lax.axis_size("mp"), lax.axis_size("dp")
    z, group = lax.axis_index("mp"), lax.axis_index("dp")
    t, d = tokens.shape[1:]
    length = n * t
    local_heads = in_weight.shape[1]
    in_width, heads_width, hidden = local_heads * 3 * HD, local_heads * HD, up_weight.shape[1]

    own_tokens = tokens[0].astype(F32)
    centred = own_tokens - jnp.mean(own_tokens, axis=-1, keepdims=True)
    spread = lax.rsqrt(jnp.mean(centred * centred, axis=-1, keepdims=True) + NORM_EPS)
    normed = centred * spread
    own_grad = cotangent[0]

    flat_in = lax.optimization_barrier(in_weight.reshape(d, in_width))
    share = out_weight.shape[0] // groups
    out_share = lax.dynamic_slice_in_dim(out_weight, group * share, share, axis=0)

    starts = document_starts(seq_lengths[0], length)
    first_of_block = starts[::t]
    low = first_of_block // KBLOCK
    last_key = (jnp.arange(length // KBLOCK, dtype=jnp.int32) + 1) * KBLOCK - 1
    high = jnp.sum((first_of_block[None, :] <= last_key[:, None]).astype(jnp.int32), axis=1)
    offsets = jnp.arange(length, dtype=jnp.int32) - starts
    inverse = 10000.0 ** (-jnp.arange(0, ROT, 2).astype(F32) / ROT)
    angles = offsets.astype(F32)[:, None] * inverse[None, :]
    cosine, sine = jnp.cos(angles), jnp.sin(angles)
    cosine = jnp.concatenate([cosine, cosine, jnp.ones((length, 128 - ROT), F32)], axis=1)
    sine = jnp.concatenate([-sine, sine, jnp.zeros((length, 128 - ROT), F32)], axis=1)
    start_row = starts[None, :]

    vectors = jnp.stack([attn_gain, attn_shift, mlp_gain, mlp_shift] * 2)
    x_rows, qkv, joint, slope, down_part = opening(
        n, normed.astype(BF16), flat_in, up_weight, down_weight, vectors, in_bias.reshape(1, in_width),
        up_bias[None, :], cosine, sine,
    )
    out_part = lax.all_gather(after(out_share, slope), "mp", axis=0, tiled=True)
    out_full = lax.all_gather(out_part, "dp", axis=0, tiled=True)
    joint, logs = attend(t, low, qkv, start_row, joint)
    unused, heads_grad, back, out_down_grad, to_right, to_left = middle(
        n, in_width, own_grad, down_part, joint, slope, out_weight, down_weight, out_part
    )

    def rows_for(array):
        def part(position):
            return lax.dynamic_slice_in_dim(array, jnp.clip(position, 0, n - 1) * t, t, axis=0)

        return part

    back = attend_back(
        t, high, qkv, heads_grad, joint, logs, start_row, cosine, sine, back, out_full
    )
    from_left, from_right = last_hop(to_right, to_left, n)
    heads_out = after(joint[:, :heads_width], back, from_left, from_right)
    heads_here = lax.all_to_all(heads_out.reshape(n, t, heads_width), "mp", 0, 0)
    heads_mine = heads_here.reshape(n, t, groups, share).transpose(1, 2, 0, 3).reshape(t, n * heads_width)
    attn_branch = dot(heads_mine, out_full) + out_bias
    mlp_branch = from_left.astype(F32) + from_right.astype(F32) + rows_for(down_part)(z).astype(F32) + down_bias
    block_out = (own_tokens + attn_branch + mlp_branch).astype(BF16)
    squares = jnp.stack([jnp.sum(attn_branch * attn_branch), jnp.sum(mlp_branch * mlp_branch)])

    grad_share = lax.psum_scatter(after(out_down_grad, out_full), "dp", scatter_dimension=0, tiled=True)
    cross, row_sums, total = cross_products(heads_width, x_rows, back, flat_in, up_weight, heads_out)
    grad_share = after(grad_share, row_sums, heads_here)
    out_down_grad = lax.all_gather(grad_share, "dp", axis=0, tiled=True)
    total = total[0]
    attn_sums = row_sums[:, 0:2].T
    mlp_sums = row_sums[:, 2:4].T
    bias_sum = jnp.sum(own_grad.astype(F32), axis=0)
    small = jnp.concatenate(
        [
            attn_sums,
            mlp_sums,
            bias_sum[None],
            jnp.pad(squares, (0, d - 2))[None],
            jnp.zeros((2, d), F32),
            jnp.pad(total[:in_width], (0, d - in_width))[None],
            jnp.pad(total[in_width:], (0, d - hidden))[None],
            jnp.zeros((6, d), F32),
        ]
    )
    norm_grad, cross, small = closing_sums(n, groups, back, cross, small, flat_in, up_weight, vectors, grad_share)
    mean_grad = jnp.mean(norm_grad, axis=-1, keepdims=True)
    mean_normed = jnp.mean(norm_grad * normed, axis=-1, keepdims=True)
    tokens_grad = (own_grad.astype(F32) + spread * (norm_grad - mean_grad - normed * mean_normed)).astype(BF16)
    in_total, up_total = small[8, :in_width], small[9, :hidden]
    totals = jnp.broadcast_to(jnp.concatenate([in_total, up_total])[None], (8, in_width + hidden))
    grad_in_weight, grad_up_weight, grad_out_weight, grad_down_weight = finish(
        local_heads, cross, totals, vectors.T, out_down_grad
    )
    element_count = float(groups * n * t * d)
    return (
        block_out[None],
        tokens_grad[None],
        small[0],
        small[1],
        small[2],
        small[3],
        grad_in_weight,
        in_total.reshape(local_heads, 3 * HD),
        grad_out_weight,
        small[4],
        grad_up_weight,
        up_total,
        grad_down_weight,
        small[4],
        jnp.sqrt(small[5, :2] / element_count),
    )


def solution(mesh):
    rows, weights = P("dp", "mp", None), P(None, "mp", None)
    in_specs = (
        rows, P("dp", None), P(), P(), P(), P(), weights, P("mp", None), P("mp", None), P(),
        P(None, "mp"), P("mp"), P("mp", None), P(), rows,
    )
    out_specs = (
        rows, rows, P(), P(), P(), P(), weights, P("mp", None), P("mp", None), P(),
        P(None, "mp"), P("mp"), P("mp", None), P(), P(),
    )
    return jax.shard_map(per_device, mesh=mesh, in_specs=in_specs, out_specs=out_specs, check_vma=False)
```

```python
import functools

import jax
import jax.numpy as jnp
import numpy as np
from jax import lax
from jax.experimental import pallas as pl
from jax.experimental.pallas import tpu as pltpu
from jax.sharding import PartitionSpec as P

HD = 256
ROT = 64
NORM_EPS = 1e-05
NEG_FILL = -1000000000.0
VMEM_LIMIT = 56 * 1024 * 1024
BF16 = jnp.bfloat16
F32 = jnp.float32

NT = (((1,), (1,)), ((), ()))
NN = (((1,), (0,)), ((), ()))
TN = (((0,), (0,)), ((), ()))


def dot(a, b, dims=NN):
    return lax.dot_general(a, b, dims, preferred_element_type=F32)


def arrival_order(n):
    return [sorted(range(n), key=lambda p, z=z: (abs(p - z), p)) for z in range(n)]


def params():
    return pltpu.CompilerParams(vmem_limit_bytes=VMEM_LIMIT)


def turn(part, cosine, sine):
    lane = lax.broadcasted_iota(jnp.int32, part.shape, 1)
    swapped = jnp.where(
        lane < ROT // 2,
        pltpu.roll(part, 128 - ROT // 2, 1),
        pltpu.roll(part, ROT // 2, 1),
    )
    return part * cosine + swapped * sine


def after(array, *others):
    anywhere = pl.BlockSpec(memory_space=pl.ANY)
    return pl.pallas_call(
        lambda *refs: None,
        in_specs=[anywhere] * (1 + len(others)),
        out_specs=anywhere,
        out_shape=jax.ShapeDtypeStruct(array.shape, array.dtype),
        input_output_aliases={0: 0},
        name="after",
    )(array, *others)


def across(z, n, values):
    picked = jnp.int32(0)
    for at in range(n):
        picked = picked + jnp.where(z == at, values[at], 0)
    return picked


def greet_line(z, n):
    barrier = pltpu.get_barrier_semaphore()
    for way in (1, -1):

        @pl.when((z + way >= 0) & (z + way < n))
        def _():
            pl.semaphore_signal(barrier, inc=1, device_id={"mp": z + way}, device_id_type=pl.DeviceIdType.MESH)

    pl.semaphore_wait(barrier, 2 - jnp.where(z == 0, 1, 0) - jnp.where(z == n - 1, 1, 0))


def line_gather(z, n, t, own, rows_ref, send, recv):
    hops = {}
    for k in range(1, n):
        for way in (1, -1):
            origin, there = z - way * (k - 1), z + way
            goes = (origin >= 0) & (origin < n) & (there >= 0) & (there < n)
            rows = rows_ref.at[pl.ds(pl.multiple_of(jnp.clip(origin, 0, n - 1) * t, t), t)]
            at = 2 * (k - 1) + (way < 0)
            copy = pltpu.make_async_remote_copy(
                own if k == 1 else rows, rows, send.at[at], recv.at[at], {"mp": there}, pl.DeviceIdType.MESH
            )
            arrives = (z - way * k >= 0) & (z - way * k < n)
            hops[k, way] = (copy, goes, arrives)
    return hops


def gather_step(hops, k):
    for way in (1, -1):
        copy, goes, _ = hops[k, way]
        pl.when(goes)(copy.start)


def gather_wait(hops, k):
    for way in (1, -1):
        copy, _, arrives = hops[k, way]
        pl.when(arrives)(copy.wait_recv)


def gather_end(hops):
    for copy, goes, _ in hops.values():
        pl.when(goes)(copy.wait_send)


def slot_positions(z, n):
    order = arrival_order(n)
    return [across(z, n, [order[zz][s] for zz in range(n)]) for s in range(n)]


def opening_kernel(n, heads, *refs):
    x_ref, in_ref, up_ref, down_ref, vec_ref, in_bias_ref, up_bias_ref, cos_ref, sin_ref = refs[:9]
    x_rows, qkv_ref, joint_ref, slope_ref, part_ref = refs[9:14]
    w_in, w_up, w_down, chunk, attn_in, mlp_in, qkv_out, act_out, slope_out, part_out = refs[14:24]
    send, recv, load, store = refs[24:]
    z = lax.axis_index("mp")
    t, d = x_ref.shape
    in_width, hidden = in_ref.shape[1], up_ref.shape[1]
    greet_line(z, n)

    def rows_of(position):
        return pl.ds(pl.multiple_of(position * t, t), t)

    own = pltpu.make_async_copy(chunk, x_rows.at[rows_of(z)], load.at[0])
    gather = line_gather(z, n, t, x_ref, x_rows, send, recv)
    gather_step(gather, 1)
    weights = [
        pltpu.make_async_copy(source, target, load.at[1 + i])
        for i, (source, target) in enumerate(((in_ref, w_in), (up_ref, w_up), (down_ref, w_down)))
    ]
    for copy in weights:
        copy.start()
    positions = slot_positions(z, n)

    def slot(s, unused):
        position = jnp.int32(0)
        for at in range(n):
            position = position + jnp.where(s == at, positions[at], 0)
        rows = rows_of(position)
        for k in range(1, n):

            @pl.when(s == k)
            def _():
                gather_wait(gather, k)
                if k < n - 1:
                    gather_step(gather, k + 1)

        @pl.when(s == 0)
        def _():
            pltpu.make_async_copy(x_ref, chunk, load.at[4]).start()

        @pl.when(s > 0)
        def _():
            pltpu.make_async_copy(x_rows.at[rows], chunk, load.at[4]).start()

        pltpu.make_async_copy(x_ref, chunk, load.at[4]).wait()
        pl.when(s == 0)(own.start)

        def norm_rows(i, unused):
            block = pl.ds(pl.multiple_of(i * 32, 32), 32)
            x = chunk[block, :].astype(F32)
            attn_in[block, :] = (x * vec_ref[0:1, :] + vec_ref[1:2, :]).astype(BF16)
            mlp_in[block, :] = (x * vec_ref[2:3, :] + vec_ref[3:4, :]).astype(BF16)
            return unused

        lax.fori_loop(0, t // 32, norm_rows, 0)
        outs = [
            pltpu.make_async_copy(qkv_out, qkv_ref.at[rows], store.at[0]),
            pltpu.make_async_copy(act_out, joint_ref.at[rows, pl.ds(heads * HD, hidden)], store.at[1]),
            pltpu.make_async_copy(slope_out, slope_ref.at[rows], store.at[2]),
            pltpu.make_async_copy(part_out, part_ref.at[rows], store.at[3]),
        ]

        @pl.when(s == 0)
        def _():
            weights[0].wait()

        @pl.when(s > 0)
        def _():
            outs[0].wait()

        cosine, sine = cos_ref[rows, :], sin_ref[rows, :]
        for j in range(3 * heads):
            cols = slice(j * HD, (j + 1) * HD)
            acc = dot(attn_in[...], w_in[:, cols]) + in_bias_ref[:, cols]
            if j % 3 < 2:
                scale = HD**-0.5 if j % 3 == 0 else 1.0
                qkv_out[:, cols] = jnp.concatenate(
                    [turn(acc[:, :128], cosine, sine) * scale, acc[:, 128:] * scale], axis=1
                ).astype(BF16)
            else:
                qkv_out[:, cols] = acc.astype(BF16)
        outs[0].start()

        @pl.when(s == 0)
        def _():
            own.wait()
            weights[1].wait()
            weights[2].wait()

        @pl.when(s > 0)
        def _():
            for copy in outs[1:]:
                copy.wait()

        tile = min(512, hidden)
        for first in range(0, hidden, tile):
            cols = slice(first, first + tile)
            u = dot(mlp_in[...], w_up[:, cols]) + up_bias_ref[:, cols]
            below = 0.5 + 0.5 * lax.erf(u * (0.5**0.5))
            act_out[:, cols] = (u * below).astype(BF16)
            density = jnp.exp(u * u * -0.5) * ((2.0 * np.pi) ** -0.5)
            slope_out[:, cols] = (below + u * density).astype(BF16)
        outs[1].start()
        outs[2].start()
        for first in range(0, d, 512):
            cols = slice(first, first + 512)
            part_out[:, cols] = dot(act_out[...], w_down[:, cols]).astype(BF16)
        outs[3].start()

        @pl.when(s == n - 1)
        def _():
            for copy in outs:
                copy.wait()

        return unused

    lax.fori_loop(0, n, slot, 0)
    gather_end(gather)


def opening(n, x, flat_in, up_weight, down_weight, vectors, in_bias, up_bias, cosine, sine):
    t, d = x.shape
    in_width, hidden = flat_in.shape[1], up_weight.shape[1]
    heads, rows = in_width // (3 * HD), n * t
    anywhere, whole = pl.BlockSpec(memory_space=pl.ANY), pl.BlockSpec(memory_space=pltpu.VMEM)
    return pl.pallas_call(
        functools.partial(opening_kernel, n, heads),
        in_specs=[anywhere] * 4 + [whole] * 5,
        out_specs=[anywhere] * 5,
        out_shape=[
            jax.ShapeDtypeStruct(shape, BF16)
            for shape in (
                (rows, d), (rows, in_width), (rows, heads * HD + hidden), (rows, hidden), (rows, d),
            )
        ],
        scratch_shapes=[
            pltpu.VMEM(shape, BF16)
            for shape in (
                (d, in_width), (d, hidden), (hidden, d), (t, d), (t, d), (t, d),
                (t, in_width), (t, hidden), (t, hidden), (t, d),
            )
        ]
        + [pltpu.SemaphoreType.DMA((2 * (n - 1),))] * 2
        + [pltpu.SemaphoreType.DMA((5,)), pltpu.SemaphoreType.DMA((4,))],
        compiler_params=pltpu.CompilerParams(
            vmem_limit_bytes=VMEM_LIMIT, collective_id=1, has_side_effects=True
        ),
        cost_estimate=pl.CostEstimate(
            flops=16 * 2 * rows * d * (in_width + 2 * hidden), bytes_accessed=200 * 2**20, transcendentals=0
        ),
        name="opening",
    )(x, flat_in, up_weight, down_weight, vectors, in_bias, up_bias, cosine, sine)


def middle_kernel(n, in_width, *refs):
    g_ref, part_ref, joint_ref, slope_ref, out_ref, down_ref = refs[:6]
    g_rows, heads_grad, back, grads, to_right, to_left = refs[7:13]
    w_out, w_down, acc, chunk, hidden_in, slope_in, up_out, heads_out, stage, terms = refs[13:23]
    come = {1: refs[23], -1: refs[24]}
    send, recv, load, store = refs[25:]
    z = lax.axis_index("mp")
    t, d = g_ref.shape
    heads_width, hidden = out_ref.shape[0], down_ref.shape[0]
    ids = pl.DeviceIdType.MESH
    greet_line(z, n)

    def rows_of(position):
        return pl.ds(pl.multiple_of(position * t, t), t)

    gather = line_gather(z, n, t, g_ref, g_rows, send, recv)
    gather_step(gather, 1)
    weights = [
        pltpu.make_async_copy(out_ref, w_out, load.at[1]),
        pltpu.make_async_copy(down_ref, w_down, load.at[2]),
    ]
    for copy in weights:
        copy.start()
    positions = slot_positions(z, n)
    hops = {}
    for k in range(1, n):
        for way, target in ((1, to_right), (-1, to_left)):
            here = (z + k < n) if way == 1 else (z >= k)
            first = (z == 0) if way == 1 else (z == n - 1)
            source = part_ref.at[rows_of(jnp.clip(z + way * k, 0, n - 1))]
            buffer = come[way].at[k - 1] if k < n - 1 else None
            if k > 1:
                at = 2 * (n - 1) + 2 * (k - 2) + (way < 0)
                bare, passed = (
                    from_ref
                    and pltpu.make_async_remote_copy(
                        from_ref, come[way].at[k - 2], send.at[at], recv.at[at], {"mp": z + way}, ids
                    )
                    for from_ref in (source, buffer)
                )
            else:
                bare, passed = (pltpu.make_async_copy(from_ref, target, load.at[0]) for from_ref in (terms, buffer))
            terms_copy = pltpu.make_async_copy(source, terms, load.at[3])
            hops[k, way] = (here & first, here & jnp.logical_not(first), here, bare, passed, terms_copy, buffer)

    def line_step(k):
        for way in (1, -1):
            first, later, _, bare, passed, terms_copy, buffer = hops[k, way]

            @pl.when(first)
            def _():
                if k == 1:
                    terms_copy.start()
                    terms_copy.wait()
                bare.start()
                if k == 1:
                    bare.wait()

            if k < n - 1:

                @pl.when(later)
                def _():
                    hops[k + 1, way][3].wait_recv()
                    terms_copy.start()
                    terms_copy.wait()
                    add_rows(buffer, 0, terms, 0, t)
                    passed.start()
                    if k == 1:
                        passed.wait()

    def slot(s, unused):
        position = jnp.int32(0)
        for at in range(n):
            position = position + jnp.where(s == at, positions[at], 0)
        rows = rows_of(position)
        inputs = [
            pltpu.make_async_copy(joint_ref.at[rows], hidden_in, load.at[5]),
            pltpu.make_async_copy(slope_ref.at[rows], slope_in, load.at[6]),
        ]
        for copy in inputs:
            copy.start()
        for k in range(1, n):

            @pl.when(s == k)
            def _():
                gather_wait(gather, k)
                if k < n - 1:
                    gather_step(gather, k + 1)
                    line_step(n - k)

        @pl.when(s == 0)
        def _():
            pltpu.make_async_copy(g_ref, chunk, load.at[4]).start()
            weights[0].wait()
            weights[1].wait()

        @pl.when(s > 0)
        def _():
            pltpu.make_async_copy(g_rows.at[rows], chunk, load.at[4]).start()

        pltpu.make_async_copy(g_ref, chunk, load.at[4]).wait()
        for copy in inputs:
            copy.wait()
        outs = [
            pltpu.make_async_copy(heads_out, heads_grad.at[rows], store.at[0]),
            pltpu.make_async_copy(up_out, back.at[rows, pl.ds(in_width, hidden)], store.at[1]),
        ]

        @pl.when(s > 0)
        def _():
            for copy in outs:
                copy.wait()

        heads_out[...] = dot(chunk[...], w_out[...], NT).astype(BF16)
        outs[0].start()
        tile = min(512, hidden)
        for first in range(0, hidden, tile):
            cols = slice(first, first + tile)
            up_grad = dot(chunk[...], w_down[cols, :], NT) * slope_in[:, cols].astype(F32)
            up_out[:, cols] = up_grad.astype(BF16)
        outs[1].start()

        def grad_tile(j, unused):
            low = pl.multiple_of(j * heads_width, heads_width)
            turned = hidden_in[:, pl.ds(low, heads_width)].T
            into = pl.ds(low, heads_width)
            for first in range(0, d, 512):
                cols = slice(first, first + 512)
                product = dot(turned, chunk[:, cols])

                @pl.when(s == 0)
                def _():
                    acc[into, cols] = product

                @pl.when((s > 0) & (s < n - 1))
                def _():
                    acc[into, cols] += product

                @pl.when(s == n - 1)
                def _():
                    if first == 0:

                        @pl.when(j > 0)
                        def _():
                            pltpu.make_async_copy(stage, grads.at[into], store.at[2]).wait()

                    stage[:, cols] = (acc[into, cols] + product).astype(BF16)

            @pl.when(s == n - 1)
            def _():
                pltpu.make_async_copy(stage, grads.at[into], store.at[2]).start()

            return unused

        lax.fori_loop(0, (heads_width + hidden) // heads_width, grad_tile, 0)

        @pl.when(s == n - 1)
        def _():
            line_step(1)
            for copy in outs:
                copy.wait()
            pltpu.make_async_copy(stage, grads.at[pl.ds(0, heads_width)], store.at[2]).wait()

        return unused

    lax.fori_loop(0, n, slot, 0)
    gather_end(gather)
    for (k, _), (_, _, here, bare, _, _, _) in hops.items():
        if k > 1:
            pl.when(here)(bare.wait_send)


def middle(n, in_width, g, down_part, joint, slope, out_weight, down_weight, earlier):
    t, d = g.shape
    rows = n * t
    heads_width, hidden = out_weight.shape[0], down_weight.shape[0]
    anywhere = pl.BlockSpec(memory_space=pl.ANY)
    copies = 2 * (n - 1) + 2 * (n - 2)
    return pl.pallas_call(
        functools.partial(middle_kernel, n, in_width),
        in_specs=[anywhere] * 7,
        out_specs=[anywhere] * 6,
        out_shape=[
            jax.ShapeDtypeStruct(shape, BF16)
            for shape in (
                (rows, d), (rows, heads_width), (rows, in_width + hidden), (heads_width + hidden, d), (t, d), (t, d),
            )
        ],
        scratch_shapes=[
            pltpu.VMEM((heads_width, d), BF16),
            pltpu.VMEM((hidden, d), BF16),
            pltpu.VMEM((heads_width + hidden, d), F32),
            pltpu.VMEM((t, d), BF16),
            pltpu.VMEM((t, heads_width + hidden), BF16),
            pltpu.VMEM((t, hidden), BF16),
            pltpu.VMEM((t, hidden), BF16),
            pltpu.VMEM((t, heads_width), BF16),
            pltpu.VMEM((heads_width, d), BF16),
            pltpu.VMEM((t, d), BF16),
            pltpu.VMEM((n - 2, t, d), BF16),
            pltpu.VMEM((n - 2, t, d), BF16),
        ]
        + [pltpu.SemaphoreType.DMA((copies,))] * 2
        + [pltpu.SemaphoreType.DMA((7,)), pltpu.SemaphoreType.DMA((3,))],
        compiler_params=pltpu.CompilerParams(
            vmem_limit_bytes=60 * 1024 * 1024, collective_id=2, has_side_effects=True
        ),
        cost_estimate=pl.CostEstimate(
            flops=16 * 4 * rows * d * (heads_width + hidden), bytes_accessed=200 * 2**20, transcendentals=0
        ),
        name="middle",
    )(g, down_part, joint, slope, out_weight, down_weight, earlier)


def cross_kernel(heads_tile, x_ref, back_ref, in_ref, up_ref, earlier_ref, cross_ref, sums_ref, total_ref, xt_ref):
    width, in_width = back_ref.shape[1], in_ref.shape[1]
    tile = heads_tile

    @pl.when(pl.program_id(0) == 0)
    def _():
        total_ref[...] = jnp.zeros_like(total_ref)
        step = 64

        def body(i, unused):
            rows = back_ref[pl.ds(pl.multiple_of(i * step, step), step), :].astype(F32)
            for r in range(0, step, 8):
                total_ref[...] += rows[r : r + 8]
            return unused

        lax.fori_loop(0, back_ref.shape[0] // step, body, 0)
        total_ref[...] = jnp.broadcast_to(jnp.sum(total_ref[...], axis=0, keepdims=True), total_ref.shape)

    xt_ref[...] = x_ref[...].T
    sums = [jnp.zeros((xt_ref.shape[0], 128), F32) for _ in range(4)]
    for first in range(0, width, tile):
        cols = slice(first, first + tile)
        product = dot(xt_ref[...], back_ref[:, cols])
        cross_ref[:, cols] = product.astype(BF16)
        inside = first < in_width
        wide = (in_ref[:, cols] if inside else up_ref[:, first - in_width : first - in_width + tile]).astype(F32)
        kind = 0 if inside else 2
        for at, term in ((kind, product * wide), (kind + 1, total_ref[0:1, cols] * wide)):
            for lane in range(0, tile, 128):
                sums[at] = sums[at] + term[:, lane : lane + 128]
    lane = lax.broadcasted_iota(jnp.int32, sums[0].shape, 1)
    out = jnp.zeros_like(sums[0])
    for at in range(4):
        out = out + jnp.where(lane == at, jnp.sum(sums[at], axis=1, keepdims=True), 0.0)
    sums_ref[...] = out


def cross_products(heads_tile, x_rows, back, flat_in, up_weight, earlier):
    rows, d = x_rows.shape
    width = back.shape[1]
    tile = 512
    once = pl.Buffered(1)
    return pl.pallas_call(
        functools.partial(cross_kernel, heads_tile),
        grid=(d // tile,),
        in_specs=[
            pl.BlockSpec((rows, tile), lambda i: (0, i)),
            pl.BlockSpec((rows, width), lambda i: (0, 0), pipeline_mode=once),
            pl.BlockSpec((tile, flat_in.shape[1]), lambda i: (i, 0)),
            pl.BlockSpec((tile, up_weight.shape[1]), lambda i: (i, 0)),
            pl.BlockSpec(memory_space=pl.ANY),
        ],
        out_specs=[
            pl.BlockSpec((tile, width), lambda i: (i, 0)),
            pl.BlockSpec((tile, 128), lambda i: (i, 0)),
            pl.BlockSpec((8, width), lambda i: (0, 0)),
        ],
        out_shape=[
            jax.ShapeDtypeStruct((d, width), BF16),
            jax.ShapeDtypeStruct((d, 128), F32),
            jax.ShapeDtypeStruct((8, width), F32),
        ],
        scratch_shapes=[pltpu.VMEM((tile, rows), BF16)],
        compiler_params=params(),
        cost_estimate=pl.CostEstimate(
            flops=2 * rows * d * width, bytes_accessed=2 * (rows * d + rows * width + 2 * d * width), transcendentals=0
        ),
        name="cross",
    )(x_rows, back, flat_in, up_weight, earlier)


def key_block(t):
    return min(512, t)


def allowed(j, i, t, start):
    key = j * key_block(t) + lax.broadcasted_iota(jnp.int32, (key_block(t), t), 0)
    query = i * t + lax.broadcasted_iota(jnp.int32, (1, t), 1)
    return (key >= start) & (key <= query)


def attend_kernel(t, heads, low_ref, qkv_ref, start_ref, held_ref, out_ref, log_ref, vt_ref, acc_ref):
    blocks = qkv_ref.shape[0] // t
    per = t // key_block(t)

    for h in range(heads):
        for c in range(blocks):
            rows = pl.ds(c * t, t)
            vt_ref[h, :, rows] = qkv_ref[rows, (3 * h + 2) * HD : (3 * h + 3) * HD].T

    def query_block(i, unused):
        row = pl.multiple_of(i * t, t)
        where = pl.ds(pl.multiple_of(i * t, t), t)
        start = start_ref[:, where]
        acc_ref[...] = jnp.zeros_like(acc_ref)

        def keys_step(j, carried):
            place = pl.multiple_of(j * key_block(t), key_block(t))
            mask = allowed(j, i, t, start)
            new = []
            for h in range(heads):
                top, total = carried[h]
                query = qkv_ref[pl.ds(row, t), 3 * h * HD : (3 * h + 1) * HD]
                key = qkv_ref[pl.ds(place, key_block(t)), (3 * h + 1) * HD : (3 * h + 2) * HD]
                s = jnp.where(mask, dot(key, query, NT), NEG_FILL)
                higher = jnp.maximum(top, jnp.max(s, axis=0, keepdims=True))
                p = jnp.exp(s - higher)
                shrink = jnp.exp(top - higher)
                total = total * shrink + jnp.sum(p, axis=0, keepdims=True)
                vt = vt_ref[h, :, pl.ds(place, key_block(t))]
                acc_ref[h] = acc_ref[h] * shrink + dot(vt, p.astype(BF16))
                new.append((higher, total))
            return tuple(new)

        first = (jnp.full((1, t), 2 * NEG_FILL, F32), jnp.zeros((1, t), F32))
        carried = lax.fori_loop(low_ref[i], (i + 1) * per, keys_step, (first,) * heads)
        for h in range(heads):
            top, total = carried[h]
            log_ref[h : h + 1, where] = top + jnp.log(total)
            out_ref[pl.ds(row, t), h * HD : (h + 1) * HD] = (acc_ref[h] / total).T.astype(BF16)
        return unused

    lax.fori_loop(0, blocks, query_block, 0)


def attend(t, low, qkv, start, hidden):
    rows, width = qkv.shape
    heads = width // (3 * HD)
    whole = pl.BlockSpec(memory_space=pltpu.VMEM)
    return pl.pallas_call(
        functools.partial(attend_kernel, t, heads),
        grid=(1,),
        in_specs=[pl.BlockSpec(memory_space=pltpu.SMEM)] + [whole] * 2 + [pl.BlockSpec(memory_space=pl.ANY)],
        out_specs=[pl.BlockSpec((rows, heads * HD), lambda i: (0, 0)), whole],
        out_shape=[
            jax.ShapeDtypeStruct(hidden.shape, BF16),
            jax.ShapeDtypeStruct((heads, rows), F32),
        ],
        scratch_shapes=[pltpu.VMEM((heads, HD, rows), BF16), pltpu.VMEM((heads, HD, t), F32)],
        input_output_aliases={3: 0},
        compiler_params=params(),
        cost_estimate=pl.CostEstimate(
            flops=2 * rows * rows * HD * heads,
            bytes_accessed=2 * rows * width,
            transcendentals=rows * rows * heads // 2,
        ),
        name="attend",
    )(low, qkv, start, hidden)


def attend_back_kernel(
    t, heads, high_ref, qkv_ref, grad_ref, out_ref, log_ref, start_ref, cos_ref, sin_ref, held_ref, after_ref,
    proj_ref, query_grad, delta, key_grad, value_grad,
):
    rows = qkv_ref.shape[0]
    blocks = rows // t
    per = t // key_block(t)
    query_grad[...] = jnp.zeros_like(query_grad)

    def prepare(i, unused):
        row = pl.multiple_of(i * t, t)
        for h in range(heads):
            cols = slice(h * HD, (h + 1) * HD)
            both = grad_ref[pl.ds(row, t), cols].astype(F32) * out_ref[pl.ds(row, t), cols].astype(F32)
            delta[h : h + 1, pl.ds(pl.multiple_of(i * t, t), t)] = jnp.sum(both.T, axis=0, keepdims=True)
        return unused

    lax.fori_loop(0, blocks, prepare, 0)

    def turned_back(grad, place, count):
        cosine, sine = cos_ref[pl.ds(place, count), :], sin_ref[pl.ds(place, count), :]
        return turn(grad[:, :128], cosine, -sine)

    def keys_step(j, unused):
        place = pl.multiple_of(j * key_block(t), key_block(t))
        key_grad[...] = jnp.zeros_like(key_grad)
        value_grad[...] = jnp.zeros_like(value_grad)

        def query_block(i, unused):
            row = pl.multiple_of(i * t, t)
            where = pl.ds(pl.multiple_of(i * t, t), t)
            mask = allowed(j, i, t, start_ref[:, where])
            for h in range(heads):
                query = qkv_ref[pl.ds(row, t), 3 * h * HD : (3 * h + 1) * HD]
                key = qkv_ref[pl.ds(place, key_block(t)), (3 * h + 1) * HD : (3 * h + 2) * HD]
                value = qkv_ref[pl.ds(place, key_block(t)), (3 * h + 2) * HD : (3 * h + 3) * HD]
                grad = grad_ref[pl.ds(row, t), h * HD : (h + 1) * HD]
                s = dot(key, query, NT) - log_ref[h : h + 1, where]
                p = jnp.exp(jnp.where(mask, s, NEG_FILL))
                p_grad = dot(value, grad, NT)
                value_grad[h] += dot(p.astype(BF16), grad)
                s_grad = (p * (p_grad - delta[h : h + 1, where])).astype(BF16)
                key_grad[h] += dot(s_grad, query)
                query_grad[pl.ds(row, t), h * HD : (h + 1) * HD] += dot(s_grad, key, TN)
            return unused

        lax.fori_loop(j // per, high_ref[j], query_block, 0)
        for h in range(heads):
            base = 3 * h * HD
            grad = key_grad[h]
            proj_ref[pl.ds(place, key_block(t)), base + HD : base + HD + 128] = turned_back(grad, place, key_block(t)).astype(BF16)
            proj_ref[pl.ds(place, key_block(t)), base + HD + 128 : base + 2 * HD] = grad[:, 128:].astype(BF16)
            proj_ref[pl.ds(place, key_block(t)), base + 2 * HD : base + 3 * HD] = value_grad[h].astype(BF16)
        return unused

    lax.fori_loop(0, rows // key_block(t), keys_step, 0)

    def finish(c, unused):
        place = pl.multiple_of(c * t, t)
        for h in range(heads):
            base = 3 * h * HD
            grad = query_grad[pl.ds(place, t), h * HD : (h + 1) * HD] * HD**-0.5
            proj_ref[pl.ds(place, t), base : base + 128] = turned_back(grad, place, t).astype(BF16)
            proj_ref[pl.ds(place, t), base + 128 : base + HD] = grad[:, 128:].astype(BF16)
        return unused

    lax.fori_loop(0, blocks, finish, 0)


def attend_back(t, high, qkv, heads_grad, hidden, logs, start, cosine, sine, buffer, after):
    rows, width = qkv.shape
    heads = width // (3 * HD)
    whole = pl.BlockSpec(memory_space=pltpu.VMEM)
    left = pl.BlockSpec((rows, heads * HD), lambda i: (0, 0))
    return pl.pallas_call(
        functools.partial(attend_back_kernel, t, heads),
        grid=(1,),
        in_specs=[pl.BlockSpec(memory_space=pltpu.SMEM)]
        + [whole, whole, left, whole, whole, whole, whole]
        + [pl.BlockSpec(memory_space=pl.ANY)] * 2,
        out_specs=pl.BlockSpec((rows, width), lambda i: (0, 0)),
        out_shape=jax.ShapeDtypeStruct(buffer.shape, BF16),
        scratch_shapes=[
            pltpu.VMEM((rows, heads * HD), F32),
            pltpu.VMEM((heads, rows), F32),
            pltpu.VMEM((heads, key_block(t), HD), F32),
            pltpu.VMEM((heads, key_block(t), HD), F32),
        ],
        input_output_aliases={8: 0},
        compiler_params=params(),
        cost_estimate=pl.CostEstimate(
            flops=5 * rows * rows * HD * heads,
            bytes_accessed=4 * rows * width,
            transcendentals=rows * rows * heads // 2,
        ),
        name="attend_back",
    )(high, qkv, heads_grad, hidden, logs, start, cosine, sine, buffer, after)


def add_rows(into, at, terms, terms_at, count):
    step = 32

    def body(i, unused):
        rows = pl.ds(pl.multiple_of(at + i * step, step), step)
        more = pl.ds(pl.multiple_of(terms_at + i * step, step), step)
        into[rows, :] = (into[rows, :].astype(F32) + terms[more, :].astype(F32)).astype(BF16)
        return unused

    lax.fori_loop(0, count // step, body, 0)


def closing_kernel(n, groups, *refs):
    bits, mp_bits = groups.bit_length() - 1, n.bit_length() - 1
    refs = refs[:6] + refs[7:]
    back_ref, cross_ref, small_ref, in_ref, up_ref, vec_ref, norm_ref, summed_ref, small_out = refs[:9]
    part = refs[9]
    come = {1: refs[10], -1: refs[11]}
    keep, core_in, chunk, in_tiles, up_tiles = refs[12:17]
    stage_in = [refs[17 : 16 + bits], refs[16 + bits : 15 + 2 * bits]]
    small_in, small_sum, send, recv, load, fetch = refs[15 + 2 * bits :]
    z, group = lax.axis_index("mp"), lax.axis_index("dp")
    t, d = norm_ref.shape
    in_width = in_ref.shape[1]
    half = keep.shape[0]
    quarter = half // 2
    ids = pl.DeviceIdType.MESH
    sems = iter(range(send.shape[0]))

    def bit_of(b):
        return lax.rem(group // 2**b, 2)

    def dp_peer(b):
        return {"dp": group + (1 - 2 * bit_of(b)) * 2**b}

    def mp_peer(b):
        return {"mp": z + (1 - 2 * lax.rem(z // 2**b, 2)) * 2**b}

    def remote(source, target, device):
        k = next(sems)
        return pltpu.make_async_remote_copy(source, target, send.at[k], recv.at[k], device, ids)

    barrier = pltpu.get_barrier_semaphore()
    for peer in [dp_peer(b) for b in range(bits)] + [mp_peer(b) for b in range(mp_bits)]:
        pl.semaphore_signal(barrier, inc=1, device_id=peer, device_id_type=ids)
    for way in (1, -1):

        @pl.when((z + way >= 0) & (z + way < n))
        def _():
            pl.semaphore_signal(barrier, inc=1, device_id={"mp": z + way}, device_id_type=ids)

    ends = jnp.where(z == 0, 1, 0) + jnp.where(z == n - 1, 1, 0)
    pl.semaphore_wait(barrier, bits + mp_bits + 2 - ends)

    mine, other = bit_of(0) * half, (1 - bit_of(0)) * half

    def summed_rows(at, count):
        return summed_ref.at[pl.ds(pl.multiple_of(mine + at, 32), count)]

    core = [
        remote(
            cross_ref.at[pl.ds(pl.multiple_of(other + p * quarter, 32), quarter)],
            core_in.at[pl.ds(p * quarter, quarter)],
            dp_peer(0),
        )
        for p in (0, 1)
    ]
    own = pltpu.make_async_copy(cross_ref.at[pl.ds(pl.multiple_of(mine, 32), half)], keep, load.at[0])
    plans = []
    for p, path in enumerate((list(range(1, bits)), list(range(bits - 1, 0, -1)))):
        at, count = p * quarter, quarter
        halvings, regions = [], []
        for s, b in enumerate(path):
            regions.append((at, count))
            count //= 2
            away = keep.at[pl.ds(pl.multiple_of(at + (1 - bit_of(b)) * count, 32), count)]
            at = at + bit_of(b) * count
            halvings.append((remote(away, stage_in[p][s], dp_peer(b)), at, count))
        place = keep.at[pl.ds(pl.multiple_of(at, 32), count)]
        local = pltpu.make_async_copy(place, summed_rows(at, count), load.at[1 + p])
        doublings = [remote(place, summed_rows(at, count), dp_peer(path[-1]))]
        for s in range(bits - 2, -1, -1):
            rows = summed_rows(*regions[s])
            doublings.append(remote(rows, rows, dp_peer(path[s - 1] if s > 0 else 0)))
        plans.append((halvings, local, doublings))

    def first_halving():
        own.wait()
        for p, (halvings, _, _) in enumerate(plans):
            core[p].wait_recv()
            add_rows(keep, p * quarter, core_in, p * quarter, quarter)
            halvings[0][0].start()

    def next_halving(s):
        for p, (halvings, local, doublings) in enumerate(plans):
            copy, at, count = halvings[s - 1]
            copy.wait_recv()
            add_rows(keep, at, stage_in[p][s - 1], 0, count)
            if s < bits - 1:
                halvings[s][0].start()
            else:
                local.start()
                doublings[0].start()

    def doubling(s):
        for _, local, doublings in plans:
            doublings[s - 1].wait_recv()
            if s == 1:
                local.wait()
            doublings[s].start()

    small_peers = [dp_peer(b) for b in range(bits)] + [mp_peer(b) for b in range(mp_bits)]
    small_copies = [remote(small_sum.at[i], small_in.at[i], peer) for i, peer in enumerate(small_peers)]

    def small_step(i):
        if i == 0:
            small_sum[0] = small_ref[...]
        else:
            small_copies[i - 1].wait_recv()
            if i - 1 < bits:
                small_sum[i] = small_sum[i - 1] + small_in[i - 1]
            else:
                small_sum[i, 8:, :] = small_sum[i - 1, 8:, :]
                small_sum[i, :8, :] = small_sum[i - 1, :8, :] + small_in[i - 1, :8, :]
        if i < len(small_peers):
            small_copies[i].start()
        else:
            small_out[...] = small_sum[i]

    def part_rows(position):
        return pl.ds(pl.multiple_of(jnp.clip(position, 0, n - 1) * t, t), t)

    hops = {}
    for k in range(1, n):
        for way in (1, -1):
            here = (z + k < n) if way == 1 else (z >= k)
            first = (z == 0) if way == 1 else (z == n - 1)
            target, device = come[way].at[k - 1], {"mp": z + way}
            at = next(sems)
            bare, passed = (
                pltpu.make_async_remote_copy(source, target, send.at[at], recv.at[at], device, ids)
                for source in (part.at[part_rows(z + way * k)], come[way].at[min(k, n - 2)])
            )
            hops[k, way] = (here & first, here & jnp.logical_not(first), here, bare, passed)

    def line_step(k):
        for way in (1, -1):
            first, later, _, bare, passed = hops[k, way]
            pl.when(first)(bare.start)
            if k < n - 1:

                @pl.when(later)
                def _():
                    hops[k + 1, way][3].wait_recv()
                    begin = pl.multiple_of(jnp.clip(z + way * k, 0, n - 1) * t, t)
                    add_rows(come[way].at[k], 0, part, begin, t)
                    passed.start()

    def line_end():
        for way, first in ((1, z == 0), (-1, z == n - 1)):
            pl.when(jnp.logical_not(first))(hops[1, way][3].wait_recv)
        step = 32

        def body(i, unused):
            rows = pl.ds(pl.multiple_of(i * step, step), step)
            total = part[pl.ds(pl.multiple_of(z * t + i * step, step), step), :].astype(F32)
            for way, first in ((1, z == 0), (-1, z == n - 1)):
                total = total + jnp.where(first, 0.0, come[way][0, rows, :].astype(F32))
            norm_ref[rows, :] = total
            return unused

        lax.fori_loop(0, t // step, body, 0)

    tile = in_tiles.shape[1]
    tiles = d // tile

    def fetches(j, slot):
        rows = pl.ds(pl.multiple_of(j * tile, tile), tile)
        return (
            pltpu.make_async_copy(in_ref.at[rows], in_tiles.at[slot], fetch.at[slot]),
            pltpu.make_async_copy(up_ref.at[rows], up_tiles.at[slot], fetch.at[2 + slot]),
        )

    def product(position):
        rows = part_rows(position)
        copy = pltpu.make_async_copy(back_ref.at[rows], chunk, load.at[3])
        copy.start()
        copy.wait()

        def one_tile(j, unused):
            slot = lax.rem(j, 2)
            for copy in fetches(j, slot):
                copy.wait()
            for copy in fetches(lax.rem(j + 1, tiles), 1 - slot):
                copy.start()
            cols = pl.ds(pl.multiple_of(j * tile, tile), tile)
            total = dot(chunk[:, :in_width], in_tiles[slot], NT) * vec_ref[0:1, cols]
            total = total + dot(chunk[:, in_width:], up_tiles[slot], NT) * vec_ref[2:3, cols]
            part[rows, cols] = total.astype(BF16)
            return unused

        lax.fori_loop(0, tiles, one_tile, 0)

    for copy in core:
        copy.start()
    own.start()
    for copy in fetches(0, 0):
        copy.start()
    small_step(0)

    def one_product(i, unused):
        distance = (n - 1 - i // 2) * (1 - 2 * lax.rem(i, 2))
        position = z + distance

        @pl.when(i == 2)
        def _():
            line_step(n - 1)
            first_halving()

        @pl.when((position >= 0) & (position < n))
        def _():
            product(position)

        return unused

    lax.fori_loop(0, 2 * (n - 1) + 1, one_product, 0)
    for copy in fetches(0, 0):
        copy.wait()
    sums = [functools.partial(next_halving, s) for s in range(1, bits)]
    sums += [functools.partial(doubling, s) for s in range(1, bits)]
    lines = [functools.partial(line_step, k) for k in range(n - 2, 0, -1)] + [line_end]
    smalls = [functools.partial(small_step, i) for i in range(1, bits + mp_bits + 1)]
    lines.pop(0)()
    for at, step in enumerate(sums):
        step()
        if at >= bits - 2 and lines:
            lines.pop(0)()
        if smalls:
            smalls.pop(0)()
    for step in lines + smalls:
        step()
    for _, _, doublings in plans:
        doublings[-1].wait_recv()
    sent = core + small_copies
    for halvings, _, doublings in plans:
        sent = sent + [copy for copy, _, _ in halvings] + doublings
    for copy in sent:
        copy.wait_send()
    for _, _, here, bare, _ in hops.values():
        pl.when(here)(bare.wait_send)


def closing_sums(n, groups, back, cross, small, flat_in, up_weight, vectors, earlier):
    rows, width = back.shape
    d = cross.shape[0]
    t, half, tile = rows // n, d // 2, 256
    bits, mp_bits = groups.bit_length() - 1, n.bit_length() - 1
    stages = [pltpu.VMEM((half // 2 // 2**s, width), BF16) for s in range(1, bits)]
    copies = 2 + 4 * (bits - 1) + 2 + 2 * (n - 1) + bits + mp_bits
    whole, anywhere = pl.BlockSpec(memory_space=pltpu.VMEM), pl.BlockSpec(memory_space=pl.ANY)
    return pl.pallas_call(
        functools.partial(closing_kernel, n, groups),
        in_specs=[anywhere, anywhere, whole, anywhere, anywhere, whole, anywhere],
        out_specs=[whole, anywhere, whole],
        out_shape=[
            jax.ShapeDtypeStruct((t, d), F32),
            jax.ShapeDtypeStruct((d, width), BF16),
            jax.ShapeDtypeStruct(small.shape, F32),
        ],
        scratch_shapes=[pltpu.VMEM((rows, d), BF16)]
        + [pltpu.VMEM((n - 1, t, d), BF16)] * 2
        + [pltpu.VMEM((half, width), BF16)] * 2
        + [pltpu.VMEM((t, width), BF16)]
        + [pltpu.VMEM((2, tile, flat_in.shape[1]), BF16), pltpu.VMEM((2, tile, up_weight.shape[1]), BF16)]
        + stages * 2
        + [pltpu.VMEM((bits + mp_bits,) + small.shape, F32), pltpu.VMEM((bits + mp_bits + 1,) + small.shape, F32)]
        + [pltpu.SemaphoreType.DMA((copies,))] * 2
        + [pltpu.SemaphoreType.DMA((4,))] * 2,
        compiler_params=pltpu.CompilerParams(
            vmem_limit_bytes=60 * 1024 * 1024, collective_id=0, has_side_effects=True
        ),
        name="closing_sums",
    )(back, cross, small, flat_in, up_weight, vectors, earlier)


def finish_kernel(heads, summed_ref, total_ref, vec_ref, out_low, down_low, in_ref, up_ref, out_ref, down_ref):
    in_width = heads * 3 * HD
    for h in range(heads):
        cols = slice(h * 3 * HD, (h + 1) * 3 * HD)
        wide = summed_ref[:, cols].astype(F32)
        in_ref[:, h, :] = wide * vec_ref[:, 0:1] + vec_ref[:, 1:2] * total_ref[0:1, cols]
    wide = summed_ref[:, in_width:].astype(F32)
    up_ref[...] = wide * vec_ref[:, 2:3] + vec_ref[:, 3:4] * total_ref[0:1, in_width:]
    out_ref[...] = out_low[...].astype(F32)
    down_ref[...] = down_low[...].astype(F32)


def finish(heads, summed, totals, vectors, out_down):
    d, width = summed.shape
    in_width, heads_width = heads * 3 * HD, heads * HD
    block = 256
    steps = d // block
    hidden = width - in_width
    out_rows, down_rows = heads_width // steps, hidden // steps
    first = heads_width // down_rows
    return pl.pallas_call(
        functools.partial(finish_kernel, heads),
        grid=(d // block,),
        in_specs=[
            pl.BlockSpec((block, width), lambda i: (i, 0)),
            pl.BlockSpec((8, width), lambda i: (0, 0)),
            pl.BlockSpec((block, 8), lambda i: (i, 0)),
            pl.BlockSpec((out_rows, d), lambda i: (i, 0)),
            pl.BlockSpec((down_rows, d), lambda i: (first + i, 0)),
        ],
        out_specs=[
            pl.BlockSpec((block, heads, 3 * HD), lambda i: (i, 0, 0)),
            pl.BlockSpec((block, hidden), lambda i: (i, 0)),
            pl.BlockSpec((out_rows, d), lambda i: (i, 0)),
            pl.BlockSpec((down_rows, d), lambda i: (i, 0)),
        ],
        out_shape=[
            jax.ShapeDtypeStruct((d, heads, 3 * HD), F32),
            jax.ShapeDtypeStruct((d, hidden), F32),
            jax.ShapeDtypeStruct((heads_width, d), F32),
            jax.ShapeDtypeStruct((hidden, d), F32),
        ],
        compiler_params=params(),
        name="finish",
    )(summed, totals, vectors, out_down, out_down)


def last_hop(to_right, to_left, n):
    right = lax.ppermute(to_right, "mp", [(i, i + 1) for i in range(n - 1)])
    left = lax.ppermute(to_left, "mp", [(i, i - 1) for i in range(1, n)])
    return right, left


def document_starts(row_lengths, length):
    count = row_lengths.shape[0]
    before = np.tri(count, k=-1, dtype=np.int32)
    starts = jnp.sum(before * row_lengths[None, :], axis=1)
    places = jnp.arange(length, dtype=jnp.int32)
    return jnp.max(jnp.where(starts[None, :] <= places[:, None], starts[None, :], 0), axis=1)


def per_device(
    tokens, seq_lengths, attn_gain, attn_shift, mlp_gain, mlp_shift, in_weight, in_bias, out_weight, out_bias,
    up_weight, up_bias, down_weight, down_bias, cotangent,
):
    n, groups = lax.axis_size("mp"), lax.axis_size("dp")
    z, group = lax.axis_index("mp"), lax.axis_index("dp")
    t, d = tokens.shape[1:]
    length = n * t
    local_heads = in_weight.shape[1]
    in_width, heads_width, hidden = local_heads * 3 * HD, local_heads * HD, up_weight.shape[1]

    own_tokens = tokens[0].astype(F32)
    centred = own_tokens - jnp.mean(own_tokens, axis=-1, keepdims=True)
    spread = lax.rsqrt(jnp.mean(centred * centred, axis=-1, keepdims=True) + NORM_EPS)
    normed = centred * spread
    own_grad = cotangent[0]

    flat_in = lax.optimization_barrier(in_weight.reshape(d, in_width))
    share = out_weight.shape[0] // groups
    out_share = lax.dynamic_slice_in_dim(out_weight, group * share, share, axis=0)

    starts = document_starts(seq_lengths[0], length)
    first_of_block = starts[::t]
    low = first_of_block // key_block(t)
    last_key = (jnp.arange(length // key_block(t), dtype=jnp.int32) + 1) * key_block(t) - 1
    high = jnp.sum((first_of_block[None, :] <= last_key[:, None]).astype(jnp.int32), axis=1)
    offsets = jnp.arange(length, dtype=jnp.int32) - starts
    inverse = 10000.0 ** (-jnp.arange(0, ROT, 2).astype(F32) / ROT)
    angles = offsets.astype(F32)[:, None] * inverse[None, :]
    cosine, sine = jnp.cos(angles), jnp.sin(angles)
    cosine = jnp.concatenate([cosine, cosine, jnp.ones((length, 128 - ROT), F32)], axis=1)
    sine = jnp.concatenate([-sine, sine, jnp.zeros((length, 128 - ROT), F32)], axis=1)
    start_row = starts[None, :]

    vectors = jnp.stack([attn_gain, attn_shift, mlp_gain, mlp_shift] * 2)
    x_rows, qkv, joint, slope, down_part = opening(
        n, normed.astype(BF16), flat_in, up_weight, down_weight, vectors, in_bias.reshape(1, in_width),
        up_bias[None, :], cosine, sine,
    )
    out_part = lax.all_gather(after(out_share, slope), "mp", axis=0, tiled=True)
    out_full = lax.all_gather(out_part, "dp", axis=0, tiled=True)
    joint, logs = attend(t, low, qkv, start_row, joint)
    unused, heads_grad, back, out_down_grad, to_right, to_left = middle(
        n, in_width, own_grad, down_part, joint, slope, out_weight, down_weight, out_part
    )

    def rows_for(array):
        def part(position):
            return lax.dynamic_slice_in_dim(array, jnp.clip(position, 0, n - 1) * t, t, axis=0)

        return part

    back = attend_back(
        t, high, qkv, heads_grad, joint, logs, start_row, cosine, sine, back, out_full
    )
    from_left, from_right = last_hop(to_right, to_left, n)
    heads_out = after(joint[:, :heads_width], back, from_left, from_right)
    heads_here = lax.all_to_all(heads_out.reshape(n, t, heads_width), "mp", 0, 0)
    heads_mine = heads_here.reshape(n, t, groups, share).transpose(1, 2, 0, 3).reshape(t, n * heads_width)
    attn_branch = dot(heads_mine, out_full) + out_bias
    mlp_branch = from_left.astype(F32) + from_right.astype(F32) + rows_for(down_part)(z).astype(F32) + down_bias
    block_out = (own_tokens + attn_branch + mlp_branch).astype(BF16)
    squares = jnp.stack([jnp.sum(attn_branch * attn_branch), jnp.sum(mlp_branch * mlp_branch)])

    grad_share = lax.psum_scatter(after(out_down_grad, out_full), "dp", scatter_dimension=0, tiled=True)
    cross, row_sums, total = cross_products(heads_width, x_rows, back, flat_in, up_weight, heads_out)
    grad_share = after(grad_share, row_sums, heads_here)
    out_down_grad = lax.all_gather(grad_share, "dp", axis=0, tiled=True)
    total = total[0]
    attn_sums = row_sums[:, 0:2].T
    mlp_sums = row_sums[:, 2:4].T
    bias_sum = jnp.sum(own_grad.astype(F32), axis=0)
    small = jnp.concatenate(
        [
            attn_sums,
            mlp_sums,
            bias_sum[None],
            jnp.pad(squares, (0, d - 2))[None],
            jnp.zeros((2, d), F32),
            jnp.pad(total[:in_width], (0, d - in_width))[None],
            jnp.pad(total[in_width:], (0, d - hidden))[None],
            jnp.zeros((6, d), F32),
        ]
    )
    norm_grad, cross, small = closing_sums(n, groups, back, cross, small, flat_in, up_weight, vectors, grad_share)
    mean_grad = jnp.mean(norm_grad, axis=-1, keepdims=True)
    mean_normed = jnp.mean(norm_grad * normed, axis=-1, keepdims=True)
    tokens_grad = (own_grad.astype(F32) + spread * (norm_grad - mean_grad - normed * mean_normed)).astype(BF16)
    in_total, up_total = small[8, :in_width], small[9, :hidden]
    totals = jnp.broadcast_to(jnp.concatenate([in_total, up_total])[None], (8, in_width + hidden))
    grad_in_weight, grad_up_weight, grad_out_weight, grad_down_weight = finish(
        local_heads, cross, totals, vectors.T, out_down_grad
    )
    element_count = float(groups * n * t * d)
    return (
        block_out[None],
        tokens_grad[None],
        small[0],
        small[1],
        small[2],
        small[3],
        grad_in_weight,
        in_total.reshape(local_heads, 3 * HD),
        grad_out_weight,
        small[4],
        grad_up_weight,
        up_total,
        grad_down_weight,
        small[4],
        jnp.sqrt(small[5, :2] / element_count),
    )


def solution(mesh):
    rows, weights = P("dp", "mp", None), P(None, "mp", None)
    in_specs = (
        rows, P("dp", None), P(), P(), P(), P(), weights, P("mp", None), P("mp", None), P(),
        P(None, "mp"), P("mp"), P("mp", None), P(), rows,
    )
    out_specs = (
        rows, rows, P(), P(), P(), P(), weights, P("mp", None), P("mp", None), P(),
        P(None, "mp"), P("mp"), P("mp", None), P(), P(),
    )
    return jax.shard_map(per_device, mesh=mesh, in_specs=in_specs, out_specs=out_specs, check_vma=False)
```
